32 devices in a mesh: groups: 2 (over x), tm: 16 (over z, y, core).
Axes of the slice: x: 2, y: 2, z: 4, core: 2. Of those that a mesh axis runs over, the one named last changes fastest.
Arguments:
- latents: float32 [256, 16384], P(None, ('groups', 'tm')), parts along dimension 1, may hold values from -6 to 6
- kernel: float32 [256, 256], replicated, may hold values from -0.375 to 0.375
- loadings: bfloat16 [16384, 256], P(('groups', 'tm')), parts along dimension 0, may hold values from -0.375 to 0.375
- recorded: bfloat16 [2, 8, 128, 16384], P(None, None, None, ('groups', 'tm')), parts along dimension 3, may hold values from -6 to 6
- owner_ids: int32 [32, 2, 8], P(('groups', 'tm')), parts along dimension 0, may hold values from 0 to 15, all different within a row; in each aligned block of 2 rows (0 to 1, 2 to 3, ..., all dimensions but the last counted through in order) at most 2 rows name the same one
- local_ids: int32 [32, 2, 8], P(('groups', 'tm')), parts along dimension 0, may hold values from 0 to 3
- recorded_mask: int32 [2, 8, 128], P(None, None, ('groups', 'tm')), parts along dimension 2, may hold values 0 or 1
Outputs:
- latent_grad: float32 [256, 16384], P(None, ('groups', 'tm')), parts along dimension 1
- loading_grad: float32 [16384, 256], P(('groups', 'tm')), parts along dimension 0
The draws below stay inside these ranges and needn't reach their ends.
There are 2 independent parts, one for each index of `groups`. The reference program is written for one: setup_inputs(seed, part) draws one part's arguments, and reference() takes and returns one part's arrays. A program takes and returns all parts, laid end to end along the dimension named above; an argument that names none is the same for every part. Nothing has to cross between parts.
Inputs may be any that keep to these rules, and one draw needn't show every extreme that they name: `owner_ids`: each probe names 8 different values; within one session the 2 probes together name no value more than 2 times, and some session names some value 2 times.
All inputs are finite; a program needn't handle non-finite values. No bound on the sum of `recorded_mask` on one device may be relied on, other than what follows from the above.
Results may differ from the reference program's by a relative error of at most 0.0027.
Values may be sent and summed in bfloat16 or wider, within the bound.
No kernel may reach another device: no remote copies, remote signals or barrier semaphores. Data moves between devices by JAX's collectives and lax.ppermute only.
A program may use at most 128 MiB of HBM per device.

```python
import math
import jax
import jax.numpy as jnp
import numpy as np
from jax import lax

K = 256
KW = 256
BLK = 128
PROBES = 2
CAP = 2
TBLK_DEV = 4
NBLK_DEV = 4
TOP = 8
SESSIONS = 16
TB = 512
TIME = 8192
TBLKS = 64
NEUR = 8192
N_TM = 16


def touch_ends(array, stream_key, low, top_value):
    spot = [jax.random.randint(jax.random.fold_in(stream_key, axis), (), 0, length) for axis, length in enumerate(array.shape)]
    widest = array.shape.index(max(array.shape))
    neighbour = spot[:widest] + [(spot[widest] + 1) % array.shape[widest]] + spot[widest + 1:]
    return array.at[tuple(spot)].set(low).at[tuple(neighbour)].set(top_value)


def shard_levels(stream_key, dims, split, least, top_value):
    level = 1.0
    for position, parts in split:
        heights = jax.random.uniform(jax.random.fold_in(jax.random.fold_in(stream_key, 6), position), (parts,), jnp.float32, least / len(split), top_value / len(split))
        level = level * jnp.repeat(jnp.exp(heights), dims[position] // parts).reshape((-1,) + (1,) * (len(dims) - 1 - position))
    return level


def deal_out(stream_key, own, number, rows, count, top, most, slope):
    order = jax.random.permutation(stream_key, count)
    crowded, ordinary = portions_of(count, rows * top, most, slope, True), portions_of(count, rows * top, most, slope, False)
    places = jnp.arange(count)

    def named(lengths, turn):
        used = int((lengths > 0).sum())
        fixed = max(1, used // 4)
        moved = fixed + (places - fixed + turn * (used - fixed)) % max(1, count - fixed)
        return jnp.zeros((count,), jnp.int32).at[order[jnp.where(places < fixed, places, moved)]].set(jnp.asarray(lengths, jnp.int32))

    lengths = jnp.where(number % 4 == 0, named(crowded, number // 4), named(ordinary, number - number // 4 - 1))
    mixed = jax.random.permutation(jax.random.fold_in(own, 3), count)
    source_of, taker = mixed[0:count // 2 * 2:2], mixed[1:count // 2 * 2:2]
    room = jnp.minimum(lengths[source_of] - 1, most - lengths[taker]) // 2
    room = jnp.where((source_of == order[0]) | (taker == order[0]) | (lengths[taker] == 0), 0, jnp.maximum(room, 0))
    moved = jax.random.randint(jax.random.fold_in(own, 4), (count // 2,), 0, 1 << 20) % (room + 1)
    lengths = lengths.at[source_of].add(-moved).at[taker].add(moved)
    items = jnp.searchsorted(jnp.cumsum(lengths), jnp.arange(rows * top), side="right").astype(jnp.int32)
    listing = items.reshape(top, rows).T
    listing = listing[jax.random.permutation(jax.random.fold_in(own, 1), rows)]
    turn = jax.random.randint(jax.random.fold_in(own, 2), (rows, 1), 0, top)
    return jnp.take_along_axis(listing, (jnp.arange(top)[None, :] + turn) % top, axis=1)


def portions_of(amount, total, reach, slope, full):
    weights = [(1 << 20) // math.isqrt(rank ** slope) + 1 for rank in range(1, amount + 1)]
    largest = reach if full else min(reach, max(-(-total // amount), total * weights[0] // sum(weights)))
    least = 1 if total - largest >= amount - 1 else 0
    counts, surplus = [largest] + [least] * (amount - 1), total - largest - least * (amount - 1)
    while surplus > 0:
        movable = [i for i in range(1, amount) if counts[i] < largest] or [i for i in range(1, amount) if counts[i] < reach]
        mass, left = sum([weights[i] for i in movable]), surplus
        for i in movable:
            extra = min(reach - counts[i], max(1, left * weights[i] // mass), surplus)
            counts[i] = counts[i] + extra
            surplus = surplus - extra
    return np.array(counts)


def scatter_about(rng, extent, deviation, most, shards=(), dtype=jnp.bfloat16):
    values = deviation * jax.random.normal(rng, extent, jnp.float32)
    if shards:
        values = values * shard_levels(rng, extent, shards, -0.22, 0.18)
    return jnp.clip(values, -most, most).astype(dtype)


def setup_inputs(seed: int = 0, part: int = 0) -> dict:
    streams_of = jax.random.split(jax.random.key(seed), 8)
    part_keys = jax.random.split(jax.random.fold_in(streams_of[7], part), 8)
    latents = scatter_about(part_keys[0], (K, TIME), 1.0, 6.0, ((1, 16),), jnp.float32)
    kernel = scatter_about(streams_of[1], (K, KW), KW ** -0.5, 0.375, (), jnp.float32)
    loadings = scatter_about(part_keys[2], (NEUR, K), K ** -0.5, 0.375, ((0, 16),))
    recorded = scatter_about(part_keys[3], (PROBES, TOP, BLK, TIME), 1.0, 6.0, ((3, 16),))
    owner_ids_keys = jax.random.split(jax.random.fold_in(part_keys[4], 1), SESSIONS * PROBES // PROBES)
    owner_ids_turns = jax.random.permutation(jax.random.fold_in(part_keys[4], 3), SESSIONS * PROBES // PROBES)
    owner_ids = jax.vmap(lambda own, number: deal_out(jax.random.fold_in(part_keys[4], 2), own, number, PROBES, N_TM, TOP, CAP, 2))(owner_ids_keys, owner_ids_turns).reshape((SESSIONS, PROBES, TOP))
    local_ids = touch_ends(jax.random.randint(part_keys[5], (SESSIONS, PROBES, TOP), 0, NBLK_DEV), jax.random.fold_in(part_keys[5], 1), 0, NBLK_DEV - 1).astype(jnp.int32)
    recorded_mask = touch_ends((jax.random.randint(part_keys[6], (PROBES, TOP, TBLKS), 0, 4) < 3).astype(jnp.int32), jax.random.fold_in(part_keys[6], 1), 0, 1)
    return dict(latents=latents, kernel=kernel, loadings=loadings, recorded=recorded, owner_ids=owner_ids, local_ids=local_ids, recorded_mask=recorded_mask)


def smooth(signal, taps):
    lhs = signal[None]
    rhs = taps[:, None, :]
    return lax.conv_general_dilated(lhs, rhs, (1,), "VALID", dimension_numbers=("NCH", "OIH", "NCH"), feature_group_count=signal.shape[0], precision=lax.Precision.HIGHEST)[0]


def reference(latents, kernel, loadings, recorded, owner_ids, local_ids, recorded_mask):
    halfwidth = KW // 2
    padded = jnp.pad(latents, ((0, 0), (halfwidth, halfwidth)))
    smoothed = smooth(padded, kernel)[:, :TIME]
    smoothed_b = smoothed.astype(jnp.bfloat16)
    neuron_blocks = loadings.reshape(NEUR // BLK, BLK, K)
    ident = (owner_ids * NBLK_DEV + local_ids).astype(jnp.int32)
    entry_count = PROBES * TOP

    def one_session(grad_load, session):
        start = (session * TB).astype(jnp.int32)
        latent_slab = lax.dynamic_slice_in_dim(smoothed_b, start, TB, 1)
        session_ids = lax.dynamic_index_in_dim(ident, session, 0, keepdims=False).reshape(-1)
        entry_rows = neuron_blocks[session_ids].reshape(entry_count * BLK, K)
        predicted = jnp.dot(entry_rows, latent_slab, preferred_element_type=jnp.float32)
        observed = lax.dynamic_slice_in_dim(recorded, start, TB, 3).reshape(entry_count * BLK, TB)
        mask_slab = lax.dynamic_slice_in_dim(recorded_mask, (session * TBLK_DEV).astype(jnp.int32), TBLK_DEV, 2)
        mask_bins = jnp.repeat(mask_slab.astype(jnp.float32), BLK, axis=2)
        mask_rows = jnp.broadcast_to(mask_bins[:, :, None, :], (PROBES, TOP, BLK, TB)).reshape(entry_count * BLK, TB)
        residual = (mask_rows * (predicted - observed.astype(jnp.float32))).astype(jnp.bfloat16)
        grad_slab = jnp.dot(entry_rows.T, residual, preferred_element_type=jnp.float32) * (1.0 / BLK)
        grad_part = jnp.dot(residual, latent_slab.T, preferred_element_type=jnp.float32) * (1.0 / BLK)
        term_b = lax.optimization_barrier(grad_part.astype(jnp.bfloat16))
        grad_load = grad_load.at[session_ids].add(term_b.astype(jnp.float32).reshape(entry_count, BLK, K))
        return grad_load, grad_slab

    start_grad = jnp.zeros((NEUR // BLK, BLK, K), jnp.float32)
    grad_load, grad_slabs = lax.scan(one_session, start_grad, jnp.arange(SESSIONS).astype(jnp.int32))
    grad_smoothed = jnp.transpose(grad_slabs, (1, 0, 2)).reshape(K, TIME)
    grad_padded = jnp.pad(grad_smoothed, ((0, 0), (halfwidth, halfwidth)))
    latent_grad = smooth(grad_padded, kernel[:, ::-1])[:, 1:TIME + 1]
    return latent_grad, grad_load.reshape(NEUR, K)
```

```python
import functools

import jax
import jax.numpy as jnp
import numpy as np
from jax import lax
from jax.experimental import pallas as pl
from jax.experimental.pallas import tpu as pltpu
from jax.sharding import PartitionSpec as P

BLK = 128
ROW = 4
F32 = jnp.float32
BF16 = jnp.bfloat16
VMEM = pl.BlockSpec(memory_space=pltpu.VMEM)
ANY = pl.BlockSpec(memory_space=pl.ANY)


def split_const(a):
    high = a.astype(jnp.bfloat16)
    low = (a - high.astype(np.float64)).astype(jnp.bfloat16)
    return high, low


@functools.lru_cache(maxsize=None)
def dft_tables(length, outputs, first):
    half = length // 2
    t = np.arange(length)[:, None]
    f = np.arange(half)[None, :]
    angle = 2 * np.pi * ((t * f) % length) / length
    cos, sin = np.cos(angle), np.sin(angle)
    sin[:, 0] = 1 - 2 * (np.arange(length) % 2)
    forward = np.concatenate([cos, sin], axis=1)
    weight = np.full((half,), 2.0 / length)
    weight[0] = 1.0 / length
    inverse = (forward * np.concatenate([weight, weight])[None, :]).T
    inverse = inverse[:, first : first + outputs]
    return split_const(forward) + split_const(inverse)


def dot3(a, b_high, b_low):
    high = a.astype(BF16)
    low = (a - high.astype(F32)).astype(BF16)
    out = jnp.dot(high, b_high, preferred_element_type=F32)
    out += jnp.dot(low, b_high, preferred_element_type=F32)
    out += jnp.dot(high, b_low, preferred_element_type=F32)
    return out


def product(signal, taps, sign):
    half = signal.shape[1] // 2
    xr, xi = signal[:, :half], signal[:, half:]
    kr, ki = taps[:, :half], taps[:, half:]
    first = lax.broadcasted_iota(jnp.int32, kr.shape, 1) == 0
    kr_i = jnp.where(first, ki, kr)
    ki_x = jnp.where(first, 0.0, ki) * sign
    return jnp.concatenate([xr * kr + xi * ki_x, xi * kr_i - xr * ki_x], axis=1)


def smooth_kernel(low, mid, high, taps, fh, fl, wh, wl, out, spectrum):
    width = low.shape[1]
    bins = mid.shape[1]
    k_spec = dot3(taps[...], fh[: taps.shape[1]], fl[: taps.shape[1]])
    spectrum[...] = k_spec
    x_spec = dot3(mid[...], fh[width : width + bins], fl[width : width + bins])
    x_spec += dot3(low[...], fh[:width], fl[:width])
    x_spec += dot3(high[...], fh[width + bins :], fl[width + bins :])
    out[...] = dot3(product(x_spec, k_spec, 1.0), wh[...], wl[...]).astype(out.dtype)


def unsmooth_kernel(low, mid, high, k_spec, fh, fl, wh, wl, out):
    width = low.shape[1]
    bins = mid.shape[1]
    x_spec = dot3(mid[...], fh[width : width + bins], fl[width : width + bins])
    x_spec += dot3(low[...], fh[:width], fl[:width])
    x_spec += dot3(high[...], fh[width + bins :], fl[width + bins :])
    out[...] = dot3(product(x_spec, k_spec[...], -1.0), wh[...], wl[...])


def session_kernel(
    same, place, mask, mine, theirs, smoothed, recorded, grad, keep, send, rows, resid, sem
):
    entries = rows.shape[0]
    bins = smoothed.shape[1]

    def fetch(e, _):
        source = pl.ds(pl.multiple_of(place[0, e] * BLK, BLK), BLK)

        @pl.when(same[e] == 1)
        def _():
            pltpu.make_async_copy(mine.at[source], rows.at[e], sem.at[e]).start()

        @pl.when(same[e] == 0)
        def _():
            pltpu.make_async_copy(theirs.at[source], rows.at[e], sem.at[e]).start()

        return 0

    lax.fori_loop(0, entries, fetch, 0)
    keep[...] = jnp.zeros_like(keep)
    send[...] = jnp.zeros_like(send)
    grad[...] = jnp.zeros_like(grad)

    def pair(step, _):
        for half in range(2):
            e = step * 2 + half
            pltpu.make_async_copy(mine.at[pl.ds(0, BLK)], rows.at[e], sem.at[e]).wait()
        block = rows[pl.ds(step * 2, 2)].reshape(2 * BLK, rows.shape[2])
        predicted = jnp.dot(block, smoothed[...], preferred_element_type=F32)
        for half in range(2):
            e = step * 2 + half
            for t in range(bins // BLK):
                cut = slice(t * BLK, (t + 1) * BLK)
                weight = mask[e * (bins // BLK) + t].astype(F32)
                part = predicted[half * BLK : (half + 1) * BLK, cut]
                seen = recorded[e, :, cut].astype(F32)
                resid[half * BLK : (half + 1) * BLK, cut] = (weight * (part - seen)).astype(BF16)
        grad[...] += lax.dot_general(
            block, resid[...], (((0,), (0,)), ((), ())), preferred_element_type=F32
        ) * (1.0 / BLK)
        term = lax.dot_general(
            resid[...], smoothed[...], (((1,), (1,)), ((), ())), preferred_element_type=F32
        ) * (1.0 / BLK)
        for half in range(2):
            e = step * 2 + half
            mine_term = term[half * BLK : (half + 1) * BLK].astype(BF16)
            target = pl.ds(pl.multiple_of(place[1, e] * BLK, BLK), BLK)

            @pl.when(same[e] == 1)
            def _():
                keep[target] = (keep[target].astype(F32) + mine_term.astype(F32)).astype(BF16)

            @pl.when(same[e] == 0)
            def _():
                send[target] = (send[target].astype(F32) + mine_term.astype(F32)).astype(BF16)

        return 0

    lax.fori_loop(0, entries // 2, pair, 0)


def local(latents, kernel, loadings, recorded, owner_ids, local_ids, recorded_mask):
    latent_dim, bins = latents.shape
    taps = kernel.shape[1]
    halfwidth = taps // 2
    count = lax.axis_size("tm")
    chain = count // ROW
    local_blocks = loadings.shape[0] // BLK
    chunk = loadings.shape[0]
    me = lax.axis_index("tm")
    my_z, my_y, my_c = me // ROW, (me // 2) % 2, me % 2

    def permute(x, pairs):
        return lax.ppermute(x, "tm", pairs)

    def along(x, zs, step):
        return permute(x, [(z * ROW + w, (z + step) * ROW + w) for z in zs for w in range(ROW)])

    def flip(x, bit):
        return permute(x, [(i, i ^ bit) for i in range(count)])

    order = [sorted(range(chain), key=lambda d: (abs(d - z), -d)) for z in range(chain)]
    near = np.zeros((chain, chain), np.int32)
    for z in range(chain):
        for rank, d in enumerate(order[z]):
            near[z, d] = rank

    def choose(options):
        distinct = []
        for o in options:
            if not any(o is d for d in distinct):
                distinct.append(o)
        value = distinct[0]
        for d in distinct[1:]:
            hit = jnp.asarray([o is d for o in options])[my_z]
            value = jnp.where(hit, d, value)
        return value

    up_one = [(i, i + 1) for i in range(count - 1)]
    down_one = [(i + 1, i) for i in range(count - 1)]

    low = permute(latents[:, bins - halfwidth :], up_one)
    high = permute(latents[:, :halfwidth], down_one)

    from_low, from_high = [loadings], [loadings]
    across = [flip(loadings, 2)]
    for r in range(1, chain):
        from_low.append(along(from_low[-1], range(r - 1, chain - 1), 1))
        from_high.append(along(from_high[-1], range(1, chain - r + 1), -1))
    arrived = [loadings]
    for k in range(1, chain):
        options = []
        for z in range(chain):
            d = order[z][k]
            options.append(from_low[z - d] if d < z else from_high[d - z])
        arrived.append(choose(options))
        across.append(flip(arrived[-1], 2))
    mine = jnp.concatenate(arrived + across)
    theirs = flip(mine, 1)

    length = bins + 2 * halfwidth
    fh, fl, wh, wl = dft_tables(length, bins, 0)
    mxu = latent_dim * length * (length + bins) * 6
    smoothed, spectrum = pl.pallas_call(
        smooth_kernel,
        out_shape=(
            jax.ShapeDtypeStruct((latent_dim, bins), BF16),
            jax.ShapeDtypeStruct((latent_dim, length), F32),
        ),
        in_specs=[VMEM] * 8,
        out_specs=(VMEM, VMEM),
        compiler_params=pltpu.CompilerParams(vmem_limit_bytes=40 * 2**20),
        cost_estimate=pl.CostEstimate(flops=mxu, bytes_accessed=6 * 2**20, transcendentals=0),
        name="smooth",
    )(low, latents, high, kernel, fh, fl, wh, wl)

    owner = owner_ids.reshape(-1)
    slot = local_ids.reshape(-1)
    entries = owner.shape[0]
    owner_z, owner_y, owner_c = owner // ROW, (owner // 2) % 2, owner % 2
    same = (owner_c == my_c).astype(jnp.int32)
    rank = jnp.asarray(near)[my_z][owner_z]
    crossed = (owner_y != my_y).astype(jnp.int32)
    place = jnp.stack(
        [
            (crossed * chain + rank) * local_blocks + slot,
            (crossed * chain + chain - 1 - rank) * local_blocks + slot,
        ]
    )
    table = count // 2 * chunk
    grad, keep, send = pl.pallas_call(
        session_kernel,
        out_shape=(
            jax.ShapeDtypeStruct((latent_dim, bins), F32),
            jax.ShapeDtypeStruct((table, latent_dim), BF16),
            jax.ShapeDtypeStruct((table, latent_dim), BF16),
        ),
        in_specs=[pl.BlockSpec(memory_space=pltpu.SMEM)] * 3 + [ANY, ANY, VMEM, VMEM],
        out_specs=(VMEM, VMEM, VMEM),
        scratch_shapes=[
            pltpu.VMEM((entries, BLK, latent_dim), BF16),
            pltpu.VMEM((2 * BLK, bins), BF16),
            pltpu.SemaphoreType.DMA((entries,)),
        ],
        compiler_params=pltpu.CompilerParams(vmem_limit_bytes=56 * 2**20),
        cost_estimate=pl.CostEstimate(
            flops=6 * entries * BLK * latent_dim * bins, bytes_accessed=8 * 2**20, transcendentals=0
        ),
        name="session",
    )(
        same,
        place,
        recorded_mask.reshape(-1),
        mine,
        theirs,
        smoothed,
        recorded.reshape(entries, BLK, bins),
    )

    grad_low = permute(grad[:, bins - halfwidth :], up_one)
    grad_high = permute(grad[:, :halfwidth], down_one)
    got = flip(send, 1)

    keep = keep.reshape(2, chain, chunk, latent_dim)
    got = got.reshape(2, chain, chunk, latent_dim)
    sums = []
    for k in range(chain):
        out = (keep[1, k].astype(F32) + got[1, k].astype(F32)).astype(BF16)
        back = flip(out, 2)
        sums.append(keep[0, k].astype(F32) + got[0, k].astype(F32) + back.astype(F32))
    rise = fall = None
    for r in range(1, chain):
        far = chain - r
        up_from, down_from = range(0, r), range(far, chain)
        pick_up = choose([sums[chain - 1 - near[z, z + far]] if z in up_from else sums[0] for z in range(chain)])
        pick_down = choose(
            [sums[chain - 1 - near[z, z - far]] if z in down_from else sums[0] for z in range(chain)]
        )
        if rise is not None:
            pick_up += rise.astype(F32)
            pick_down += fall.astype(F32)
        rise = along(pick_up.astype(BF16), up_from, 1)
        fall = along(pick_down.astype(BF16), down_from, -1)
    loading_grad = sums[-1]
    if rise is not None:
        loading_grad = loading_grad + rise.astype(F32) + fall.astype(F32)

    fh, fl, wh, wl = dft_tables(length, bins, 2 * halfwidth)
    latent_grad = pl.pallas_call(
        unsmooth_kernel,
        out_shape=jax.ShapeDtypeStruct((latent_dim, bins), F32),
        in_specs=[VMEM] * 8,
        out_specs=VMEM,
        compiler_params=pltpu.CompilerParams(vmem_limit_bytes=40 * 2**20),
        cost_estimate=pl.CostEstimate(flops=mxu, bytes_accessed=6 * 2**20, transcendentals=0),
        name="unsmooth",
    )(grad_low, grad, grad_high, spectrum, fh, fl, wh, wl)
    return latent_grad, loading_grad


def solution(mesh):
    return jax.shard_map(
        local,
        mesh=mesh,
        in_specs=(
            P(None, ("groups", "tm")),
            P(),
            P(("groups", "tm"), None),
            P(None, None, None, ("groups", "tm")),
            P(("groups", "tm"), None, None),
            P(("groups", "tm"), None, None),
            P(None, None, ("groups", "tm")),
        ),
        out_specs=(P(None, ("groups", "tm")), P(("groups", "tm"), None)),
        check_vma=False,
    )
```

```python
import functools

import jax
import jax.numpy as jnp
import numpy as np
from jax import lax
from jax.experimental import pallas as pl
from jax.experimental.pallas import tpu as pltpu
from jax.sharding import PartitionSpec as P

BLK = 128
ROW = 4
F32 = jnp.float32
BF16 = jnp.bfloat16
VMEM = pl.BlockSpec(memory_space=pltpu.VMEM)
ANY = pl.BlockSpec(memory_space=pl.ANY)


def split_const(a):
    high = a.astype(jnp.bfloat16)
    low = (a - high.astype(np.float64)).astype(jnp.bfloat16)
    return high, low


@functools.lru_cache(maxsize=None)
def dft_tables(length, outputs, first):
    half = length // 2
    t = np.arange(length)[:, None]
    f = np.arange(half)[None, :]
    angle = 2 * np.pi * ((t * f) % length) / length
    cos, sin = np.cos(angle), np.sin(angle)
    sin[:, 0] = 1 - 2 * (np.arange(length) % 2)
    forward = np.concatenate([cos, sin], axis=1)
    weight = np.full((half,), 2.0 / length)
    weight[0] = 1.0 / length
    inverse = (forward * np.concatenate([weight, weight])[None, :]).T
    inverse = inverse[:, first : first + outputs]
    return split_const(forward) + split_const(inverse)


def dot3(a, b_high, b_low):
    high = a.astype(BF16)
    low = (a - high.astype(F32)).astype(BF16)
    out = jnp.dot(high, b_high, preferred_element_type=F32)
    out += jnp.dot(low, b_high, preferred_element_type=F32)
    out += jnp.dot(high, b_low, preferred_element_type=F32)
    return out


def product(signal, taps, sign):
    half = signal.shape[1] // 2
    xr, xi = signal[:, :half], signal[:, half:]
    kr, ki = taps[:, :half], taps[:, half:]
    first = lax.broadcasted_iota(jnp.int32, kr.shape, 1) == 0
    kr_i = jnp.where(first, ki, kr)
    ki_x = jnp.where(first, 0.0, ki) * sign
    return jnp.concatenate([xr * kr + xi * ki_x, xi * kr_i - xr * ki_x], axis=1)


def smooth_kernel(low, mid, high, taps, fh, fl, wh, wl, out, spectrum):
    width = low.shape[1]
    bins = mid.shape[1]
    k_spec = dot3(taps[...], fh[: taps.shape[1]], fl[: taps.shape[1]])
    spectrum[...] = k_spec
    x_spec = dot3(mid[...], fh[width : width + bins], fl[width : width + bins])
    x_spec += dot3(low[...], fh[:width], fl[:width])
    x_spec += dot3(high[...], fh[width + bins :], fl[width + bins :])
    out[...] = dot3(product(x_spec, k_spec, 1.0), wh[...], wl[...]).astype(out.dtype)


def unsmooth_kernel(low, mid, high, k_spec, fh, fl, wh, wl, out):
    width = low.shape[1]
    bins = mid.shape[1]
    x_spec = dot3(mid[...], fh[width : width + bins], fl[width : width + bins])
    x_spec += dot3(low[...], fh[:width], fl[:width])
    x_spec += dot3(high[...], fh[width + bins :], fl[width + bins :])
    out[...] = dot3(product(x_spec, k_spec[...], -1.0), wh[...], wl[...])


def place_of(ids, e, entries, me, forward):
    chain = lax.axis_size("tm") // ROW
    owner, slot = ids[e], ids[entries + e]
    owner_z, owner_y, owner_c = owner // ROW, (owner // 2) % 2, owner % 2
    z, y = me // ROW, (me // 2) % 2
    step = (owner_z - z) if forward else (z - owner_z)
    turn = jnp.where(step < 0, step + chain, step)
    piece = jnp.where(owner_y == y, 0, chain) + turn
    return owner_c, piece, pl.multiple_of(slot * BLK, BLK)


def pack_kernel(entries, ids, asked, *refs):
    pieces, (out, sem) = refs[:-2], refs[-2:]
    me = ids[2 * entries]

    def copy(piece, e, row):
        return pltpu.make_async_copy(
            piece.at[pl.ds(row, BLK)], out.at[pl.ds(pl.multiple_of(e * BLK, BLK), BLK)], sem.at[e]
        )

    def start(e, _):
        core, piece, row = place_of(asked, e, entries, me, False)
        for q, ref in enumerate(pieces):

            @pl.when(jnp.logical_and(core == me % 2, piece == q))
            def _():
                copy(ref, e, row).start()

        return 0

    def wait(e, _):
        core, _, row = place_of(asked, e, entries, me, False)

        @pl.when(core == me % 2)
        def _():
            copy(pieces[0], e, row).wait()

        return 0

    lax.fori_loop(0, entries, start, 0)
    lax.fori_loop(0, entries, wait, 0)


def session_kernel(entries, group, ids, mask, smoothed, recorded, packed, *refs):
    pieces = refs[:-7]
    grad, grad_low, grad_high, terms, rows, resid, sem = refs[-7:]
    bins = smoothed.shape[1]
    me = ids[2 * entries]

    def copy(source, e, row):
        return pltpu.make_async_copy(source.at[pl.ds(row, BLK)], rows.at[e], sem.at[e])

    def fetch(e, _):
        core, piece, row = place_of(ids, e, entries, me, False)
        for q, ref in enumerate(pieces):

            @pl.when(jnp.logical_and(core == me % 2, piece == q))
            def _():
                copy(ref, e, row).start()

        @pl.when(core != me % 2)
        def _():
            copy(packed, e, pl.multiple_of(e * BLK, BLK)).start()

        return 0

    lax.fori_loop(0, entries, fetch, 0)
    grad[...] = jnp.zeros_like(grad)
    depth = group * BLK

    def step(g, _):
        for i in range(group):
            copy(packed, g * group + i, 0).wait()
        block = rows[pl.ds(g * group, group)].reshape(depth, rows.shape[2])
        predicted = jnp.dot(block, smoothed[...], preferred_element_type=F32)
        for i in range(group):
            e = g * group + i
            for t in range(bins // BLK):
                cut = slice(t * BLK, (t + 1) * BLK)
                weight = mask[e * (bins // BLK) + t].astype(F32)
                part = predicted[i * BLK : (i + 1) * BLK, cut]
                seen = recorded[e, :, cut].astype(F32)
                resid[i * BLK : (i + 1) * BLK, cut] = (weight * (part - seen)).astype(BF16)
        term = lax.dot_general(
            resid[...], smoothed[...], (((1,), (1,)), ((), ())), preferred_element_type=F32
        )
        target = pl.ds(pl.multiple_of(g * depth, depth), depth)
        terms[target] = (term * (1.0 / BLK)).astype(BF16)
        grad[...] += lax.dot_general(
            block, resid[...], (((0,), (0,)), ((), ())), preferred_element_type=F32
        ) * (1.0 / BLK)
        return 0

    lax.fori_loop(0, entries // group, step, 0)
    width = grad_low.shape[1]
    grad_low[...] = grad[:, bins - width :]
    grad_high[...] = grad[:, :width]


def merge_kernel(entries, ids, asked, own, got, *refs):
    outs, sums = refs[:-1], refs[-1]
    me = ids[2 * entries]
    chunk = outs[0].shape[0]
    sums[...] = jnp.zeros_like(sums)

    def add(e, _):
        source = pl.ds(pl.multiple_of(e * BLK, BLK), BLK)
        for names, terms in ((ids, own), (asked, got)):
            core, piece, row = place_of(names, e, entries, me, True)

            @pl.when(core == me % 2)
            def _():
                target = pl.ds(pl.multiple_of(piece * chunk + row, BLK), BLK)
                sums[target] += terms[source].astype(F32)

        return 0

    lax.fori_loop(0, entries, add, 0)
    for q, out in enumerate(outs):
        out[...] = sums[q * chunk : (q + 1) * chunk].astype(out.dtype)


def local(latents, kernel, loadings, recorded, owner_ids, local_ids, recorded_mask):
    latent_dim, bins = latents.shape
    halfwidth = kernel.shape[1] // 2
    count = lax.axis_size("tm")
    chain = count // ROW
    chunk = loadings.shape[0]
    entries = owner_ids.size
    smem = pl.BlockSpec(memory_space=pltpu.SMEM)

    def permute(x, pairs):
        return lax.ppermute(x, "tm", pairs)

    def rotate(x, r):
        return permute(x, [(i, (i + r * ROW) % count) for i in range(count)])

    def flip(x, bit):
        return permute(x, [(i, i ^ bit) for i in range(count)])

    up_one = [(i, i + 1) for i in range(count - 1)]
    down_one = [(i + 1, i) for i in range(count - 1)]

    me = jnp.full((1,), lax.axis_index("tm"), jnp.int32)
    ids = jnp.concatenate([owner_ids.reshape(-1), local_ids.reshape(-1), me])
    asked = flip(ids, 1)

    low = permute(latents[:, bins - halfwidth :], up_one)
    high = permute(latents[:, :halfwidth], down_one)

    pieces = [loadings] + [rotate(loadings, r) for r in range(1, chain)]
    pieces += [flip(piece, 2) for piece in pieces]

    length = bins + 2 * halfwidth
    fh, fl, wh, wl = dft_tables(length, bins, 0)
    mxu = latent_dim * length * (length + bins) * 6
    smoothed, spectrum = pl.pallas_call(
        smooth_kernel,
        out_shape=(
            jax.ShapeDtypeStruct((latent_dim, bins), BF16),
            jax.ShapeDtypeStruct((latent_dim, length), F32),
        ),
        in_specs=[VMEM] * 8,
        out_specs=(VMEM, VMEM),
        compiler_params=pltpu.CompilerParams(vmem_limit_bytes=40 * 2**20),
        cost_estimate=pl.CostEstimate(flops=mxu, bytes_accessed=6 * 2**20, transcendentals=0),
        name="smooth",
    )(low, latents, high, kernel, fh, fl, wh, wl)

    slots = jax.ShapeDtypeStruct((entries * BLK, latent_dim), BF16)
    packed = pl.pallas_call(
        functools.partial(pack_kernel, entries),
        out_shape=slots,
        in_specs=[smem] * 2 + [ANY] * len(pieces),
        out_specs=ANY,
        scratch_shapes=[pltpu.SemaphoreType.DMA((entries,))],
        cost_estimate=pl.CostEstimate(flops=0, bytes_accessed=2 * 2**20, transcendentals=0),
        name="pack",
    )(ids, asked, *pieces)
    packed = flip(packed, 1)

    group = 4
    strip = jax.ShapeDtypeStruct((latent_dim, halfwidth), F32)
    grad, grad_low, grad_high, terms = pl.pallas_call(
        functools.partial(session_kernel, entries, group),
        out_shape=(jax.ShapeDtypeStruct((latent_dim, bins), F32), strip, strip, slots),
        in_specs=[smem] * 2 + [VMEM] * 2 + [ANY] * (1 + len(pieces)),
        out_specs=(VMEM,) * 4,
        scratch_shapes=[
            pltpu.VMEM((entries, BLK, latent_dim), BF16),
            pltpu.VMEM((group * BLK, bins), BF16),
            pltpu.SemaphoreType.DMA((entries,)),
        ],
        compiler_params=pltpu.CompilerParams(vmem_limit_bytes=56 * 2**20),
        cost_estimate=pl.CostEstimate(
            flops=6 * entries * BLK * latent_dim * bins, bytes_accessed=8 * 2**20, transcendentals=0
        ),
        name="session",
    )(
        ids,
        recorded_mask.reshape(-1),
        smoothed,
        recorded.reshape(entries, BLK, bins),
        packed,
        *pieces,
    )

    got = flip(terms, 1)
    grad_low = permute(grad_low, up_one)
    grad_high = permute(grad_high, down_one)
    sums = pl.pallas_call(
        functools.partial(merge_kernel, entries),
        out_shape=(jax.ShapeDtypeStruct((chunk, latent_dim), F32),) * chain
        + (jax.ShapeDtypeStruct((chunk, latent_dim), BF16),) * chain,
        in_specs=[smem] * 2 + [VMEM] * 2,
        out_specs=(VMEM,) * (2 * chain),
        scratch_shapes=[pltpu.VMEM((2 * chain * chunk, latent_dim), F32)],
        compiler_params=pltpu.CompilerParams(vmem_limit_bytes=60 * 2**20),
        cost_estimate=pl.CostEstimate(flops=0, bytes_accessed=5 * 2**20, transcendentals=0),
        name="merge",
    )(ids, asked, terms, got)
    turned = []
    far_first = sorted(range(chain), key=lambda r: -min(r, chain - r))
    for r in far_first:
        total = sums[r] + flip(sums[chain + r], 2).astype(F32)
        if r:
            turned.append(rotate(total.astype(BF16), r))
        else:
            loading_grad = total
    for part in turned:
        loading_grad = loading_grad + part.astype(F32)

    fh, fl, wh, wl = dft_tables(length, bins, 2 * halfwidth)
    latent_grad = pl.pallas_call(
        unsmooth_kernel,
        out_shape=jax.ShapeDtypeStruct((latent_dim, bins), F32),
        in_specs=[VMEM] * 8,
        out_specs=VMEM,
        compiler_params=pltpu.CompilerParams(vmem_limit_bytes=40 * 2**20),
        cost_estimate=pl.CostEstimate(flops=mxu, bytes_accessed=6 * 2**20, transcendentals=0),
        name="unsmooth",
    )(grad_low, grad, grad_high, spectrum, fh, fl, wh, wl)
    return latent_grad, loading_grad


def solution(mesh):
    return jax.shard_map(
        local,
        mesh=mesh,
        in_specs=(
            P(None, ("groups", "tm")),
            P(),
            P(("groups", "tm"), None),
            P(None, None, None, ("groups", "tm")),
            P(("groups", "tm"), None, None),
            P(("groups", "tm"), None, None),
            P(None, None, ("groups", "tm")),
        ),
        out_specs=(P(None, ("groups", "tm")), P(("groups", "tm"), None)),
        check_vma=False,
    )
```

```python
import functools

import jax
import jax.numpy as jnp
import numpy as np
from jax import lax
from jax.experimental import pallas as pl
from jax.experimental.pallas import tpu as pltpu
from jax.sharding import PartitionSpec as P

BLK = 128
ROW = 4
F32 = jnp.float32
BF16 = jnp.bfloat16
VMEM = pl.BlockSpec(memory_space=pltpu.VMEM)
ANY = pl.BlockSpec(memory_space=pl.ANY)


def split_const(a):
    high = a.astype(jnp.bfloat16)
    low = (a - high.astype(np.float64)).astype(jnp.bfloat16)
    return high, low


@functools.lru_cache(maxsize=None)
def dft_tables(length, outputs, first):
    half = length // 2
    t = np.arange(length)[:, None]
    f = np.arange(half)[None, :]
    angle = 2 * np.pi * ((t * f) % length) / length
    cos, sin = np.cos(angle), np.sin(angle)
    sin[:, 0] = 1 - 2 * (np.arange(length) % 2)
    forward = np.concatenate([cos, sin], axis=1)
    weight = np.full((half,), 2.0 / length)
    weight[0] = 1.0 / length
    inverse = (forward * np.concatenate([weight, weight])[None, :]).T
    inverse = inverse[:, first : first + outputs]
    return split_const(forward) + split_const(inverse)


def dot3(a, b_high, b_low):
    high = a.astype(BF16)
    low = (a - high.astype(F32)).astype(BF16)
    out = jnp.dot(high, b_high, preferred_element_type=F32)
    out += jnp.dot(low, b_high, preferred_element_type=F32)
    out += jnp.dot(high, b_low, preferred_element_type=F32)
    return out


def product(signal, taps, sign):
    half = signal.shape[1] // 2
    xr, xi = signal[:, :half], signal[:, half:]
    kr, ki = taps[:, :half], taps[:, half:]
    first = lax.broadcasted_iota(jnp.int32, kr.shape, 1) == 0
    kr_i = jnp.where(first, ki, kr)
    ki_x = jnp.where(first, 0.0, ki) * sign
    return jnp.concatenate([xr * kr + xi * ki_x, xi * kr_i - xr * ki_x], axis=1)


def smooth_kernel(low, mid, high, taps, fh, fl, wh, wl, out, spectrum):
    width = low.shape[1]
    bins = mid.shape[1]
    k_spec = dot3(taps[...], fh[: taps.shape[1]], fl[: taps.shape[1]])
    spectrum[...] = k_spec
    x_spec = dot3(mid[...], fh[width : width + bins], fl[width : width + bins])
    x_spec += dot3(low[...], fh[:width], fl[:width])
    x_spec += dot3(high[...], fh[width + bins :], fl[width + bins :])
    out[...] = dot3(product(x_spec, k_spec, 1.0), wh[...], wl[...]).astype(out.dtype)


def unsmooth_kernel(low, mid, high, k_spec, fh, fl, wh, wl, out):
    width = low.shape[1]
    bins = mid.shape[1]
    x_spec = dot3(mid[...], fh[width : width + bins], fl[width : width + bins])
    x_spec += dot3(low[...], fh[:width], fl[:width])
    x_spec += dot3(high[...], fh[width + bins :], fl[width + bins :])
    out[...] = dot3(product(x_spec, k_spec[...], -1.0), wh[...], wl[...])


def place_of(ids, e, entries, me, forward):
    chain = lax.axis_size("tm") // ROW
    owner, slot = ids[e], ids[entries + e]
    owner_z, owner_y, owner_c = owner // ROW, (owner // 2) % 2, owner % 2
    z, y = me // ROW, (me // 2) % 2
    step = (owner_z - z) if forward else (z - owner_z)
    turn = jnp.where(step < 0, step + chain, step)
    piece = jnp.where(owner_y == y, 0, chain) + turn
    return owner_c, piece, pl.multiple_of(slot * BLK, BLK)


def pack_kernel(entries, late, ids, asked, *refs):
    pieces, (out, sem) = refs[:-2], refs[-2:]
    me = ids[2 * entries]

    def copy(piece, e, row):
        return pltpu.make_async_copy(
            piece.at[pl.ds(row, BLK)], out.at[pl.ds(pl.multiple_of(e * BLK, BLK), BLK)], sem.at[e]
        )

    def start(e, _):
        core, piece, row = place_of(asked, e, entries, me, False)
        for q, ref in enumerate(pieces[:late] + (None,) + pieces[late:]):
            if q == late:
                continue

            @pl.when(jnp.logical_and(core == me % 2, piece == q))
            def _():
                copy(ref, e, row).start()

        return 0

    def wait(e, _):
        core, piece, row = place_of(asked, e, entries, me, False)

        @pl.when(jnp.logical_and(core == me % 2, piece != late))
        def _():
            copy(pieces[0], e, row).wait()

        return 0

    lax.fori_loop(0, entries, start, 0)
    lax.fori_loop(0, entries, wait, 0)


def session_kernel(
    entries, group, late, ids, mask, smoothed, recorded, packed, late_theirs, *refs
):
    pieces = refs[:-7]
    grad, grad_low, grad_high, terms, rows, resid, sem = refs[-7:]
    bins = smoothed.shape[1]
    me = ids[2 * entries]

    def copy(source, e, row):
        return pltpu.make_async_copy(source.at[pl.ds(row, BLK)], rows.at[e], sem.at[e])

    def fetch(e, _):
        core, piece, row = place_of(ids, e, entries, me, False)
        for q, ref in enumerate(pieces):

            @pl.when(jnp.logical_and(core == me % 2, piece == q))
            def _():
                copy(ref, e, row).start()

        @pl.when(jnp.logical_and(core != me % 2, piece != late))
        def _():
            copy(packed, e, pl.multiple_of(e * BLK, BLK)).start()

        @pl.when(jnp.logical_and(core != me % 2, piece == late))
        def _():
            copy(late_theirs, e, row).start()

        return 0

    lax.fori_loop(0, entries, fetch, 0)
    grad[...] = jnp.zeros_like(grad)
    depth = group * BLK

    def step(g, _):
        for i in range(group):
            copy(packed, g * group + i, 0).wait()
        block = rows[pl.ds(g * group, group)].reshape(depth, rows.shape[2])
        predicted = jnp.dot(block, smoothed[...], preferred_element_type=F32)
        for i in range(group):
            e = g * group + i
            for t in range(bins // BLK):
                cut = slice(t * BLK, (t + 1) * BLK)
                weight = mask[e * (bins // BLK) + t].astype(F32)
                part = predicted[i * BLK : (i + 1) * BLK, cut]
                seen = recorded[e, :, cut].astype(F32)
                resid[i * BLK : (i + 1) * BLK, cut] = (weight * (part - seen)).astype(BF16)
        term = lax.dot_general(
            resid[...], smoothed[...], (((1,), (1,)), ((), ())), preferred_element_type=F32
        )
        target = pl.ds(pl.multiple_of(g * depth, depth), depth)
        terms[target] = (term * (1.0 / BLK)).astype(BF16)
        grad[...] += lax.dot_general(
            block, resid[...], (((0,), (0,)), ((), ())), preferred_element_type=F32
        ) * (1.0 / BLK)
        return 0

    lax.fori_loop(0, entries // group, step, 0)
    width = grad_low.shape[1]
    grad_low[...] = grad[:, bins - width :]
    grad_high[...] = grad[:, :width]


def merge_kernel(entries, late, only_late, ids, asked, own, got, *refs):
    outs, sums = refs[:-1], refs[-1]
    me = ids[2 * entries]
    chunk = outs[0].shape[0]
    sums[...] = jnp.zeros_like(sums)

    def add(e, _):
        source = pl.ds(pl.multiple_of(e * BLK, BLK), BLK)
        for names, terms in ((ids, own), (asked, got)):
            core, piece, row = place_of(names, e, entries, me, True)

            if only_late:
                wanted, index = piece == late, 0
            else:
                wanted, index = piece != late, jnp.where(piece < late, piece, piece - 1)

            @pl.when(jnp.logical_and(core == me % 2, wanted))
            def _():
                target = pl.ds(pl.multiple_of(index * chunk + row, BLK), BLK)
                sums[target] += terms[source].astype(F32)

        return 0

    lax.fori_loop(0, entries, add, 0)
    for q, out in enumerate(outs):
        out[...] = sums[q * chunk : (q + 1) * chunk].astype(out.dtype)


def local(latents, kernel, loadings, recorded, owner_ids, local_ids, recorded_mask):
    latent_dim, bins = latents.shape
    halfwidth = kernel.shape[1] // 2
    count = lax.axis_size("tm")
    chain = count // ROW
    chunk = loadings.shape[0]
    entries = owner_ids.size
    smem = pl.BlockSpec(memory_space=pltpu.SMEM)

    def permute(x, pairs):
        return lax.ppermute(x, "tm", pairs)

    def rotate(x, r):
        return permute(x, [(i, (i + r * ROW) % count) for i in range(count)])

    def flip(x, bit):
        return permute(x, [(i, i ^ bit) for i in range(count)])

    up_one = [(i, i + 1) for i in range(count - 1)]
    down_one = [(i + 1, i) for i in range(count - 1)]

    me = jnp.full((1,), lax.axis_index("tm"), jnp.int32)
    ids = jnp.concatenate([owner_ids.reshape(-1), local_ids.reshape(-1), me])
    asked = flip(ids, 1)

    low = permute(latents[:, bins - halfwidth :], up_one)
    high = permute(latents[:, :halfwidth], down_one)

    half = chain // 2
    late = chain + half
    straight = [loadings] * chain
    for r in range(1, half):
        straight[r] = rotate(straight[r - 1], 1)
        straight[-r] = rotate(straight[1 - r], -1)
    straight[half] = rotate(straight[half - 1], 1)
    across = [flip(straight[r], 2) if r != half else None for r in range(chain)]

    length = bins + 2 * halfwidth
    fh, fl, wh, wl = dft_tables(length, bins, 0)
    mxu = latent_dim * length * (length + bins) * 6
    smoothed, spectrum = pl.pallas_call(
        smooth_kernel,
        out_shape=(
            jax.ShapeDtypeStruct((latent_dim, bins), BF16),
            jax.ShapeDtypeStruct((latent_dim, length), F32),
        ),
        in_specs=[VMEM] * 8,
        out_specs=(VMEM, VMEM),
        compiler_params=pltpu.CompilerParams(vmem_limit_bytes=40 * 2**20),
        cost_estimate=pl.CostEstimate(flops=mxu, bytes_accessed=6 * 2**20, transcendentals=0),
        name="smooth",
    )(low, latents, high, kernel, fh, fl, wh, wl)

    slots = jax.ShapeDtypeStruct((entries * BLK, latent_dim), BF16)
    ids, asked, smoothed, mask = lax.optimization_barrier(
        (ids, asked, smoothed, recorded_mask.reshape(-1))
    )
    across[half] = flip(straight[half], 2)
    early = straight + across[:half] + across[half + 1 :]
    packed = pl.pallas_call(
        functools.partial(pack_kernel, entries, late),
        out_shape=slots,
        in_specs=[smem] * 2 + [ANY] * len(early),
        out_specs=VMEM,
        scratch_shapes=[pltpu.SemaphoreType.DMA((entries,))],
        cost_estimate=pl.CostEstimate(flops=0, bytes_accessed=2 * 2**20, transcendentals=0),
        name="pack",
    )(ids, asked, *early)
    packed = flip(packed, 1)
    late_theirs = flip(across[half], 1)
    pieces = straight + across

    group = 4
    strip = jax.ShapeDtypeStruct((latent_dim, halfwidth), F32)
    grad, grad_low, grad_high, terms = pl.pallas_call(
        functools.partial(session_kernel, entries, group, late),
        out_shape=(jax.ShapeDtypeStruct((latent_dim, bins), F32), strip, strip, slots),
        in_specs=[smem] * 2 + [VMEM] * 2 + [ANY] * (2 + len(pieces)),
        out_specs=(VMEM,) * 4,
        scratch_shapes=[
            pltpu.VMEM((entries, BLK, latent_dim), BF16),
            pltpu.VMEM((group * BLK, bins), BF16),
            pltpu.SemaphoreType.DMA((entries,)),
        ],
        compiler_params=pltpu.CompilerParams(vmem_limit_bytes=56 * 2**20),
        cost_estimate=pl.CostEstimate(
            flops=6 * entries * BLK * latent_dim * bins, bytes_accessed=8 * 2**20, transcendentals=0
        ),
        name="session",
    )(
        ids,
        mask,
        smoothed,
        recorded.reshape(entries, BLK, bins),
        packed,
        late_theirs,
        *pieces,
    )

    got = flip(terms, 1)
    grad_low = permute(grad_low, up_one)
    grad_high = permute(grad_high, down_one)

    def merge(only_late, out_shape):
        return pl.pallas_call(
            functools.partial(merge_kernel, entries, late, only_late),
            out_shape=out_shape,
            in_specs=[smem] * 2 + [VMEM] * 2,
            out_specs=(VMEM,) * len(out_shape),
            scratch_shapes=[pltpu.VMEM((len(out_shape) * chunk, latent_dim), F32)],
            compiler_params=pltpu.CompilerParams(vmem_limit_bytes=60 * 2**20),
            cost_estimate=pl.CostEstimate(flops=0, bytes_accessed=5 * 2**20, transcendentals=0),
            name="merge",
        )(ids, asked, terms, got)

    wide = jax.ShapeDtypeStruct((chunk, latent_dim), F32)
    narrow = jax.ShapeDtypeStruct((chunk, latent_dim), BF16)
    (sent,) = merge(True, (narrow,))
    back = flip(sent, 2)
    sums = merge(False, (wide,) * chain + (narrow,) * (chain - 1))
    other = {half: back}
    for r in sorted(range(chain), key=lambda r: -min(r, chain - r)):
        if r != half:
            other[r] = flip(sums[chain + r - (r > half)], 2)
    totals = [sums[r] + other[r].astype(F32) for r in range(chain)]
    rise = totals[half]
    for r in range(half - 1, -1, -1):
        rise = totals[r] + rotate(rise.astype(BF16), 1).astype(F32)
    loading_grad = rise
    if half > 1:
        fall = totals[half + 1]
        for r in range(half + 2, chain):
            fall = totals[r] + rotate(fall.astype(BF16), -1).astype(F32)
        loading_grad = loading_grad + rotate(fall.astype(BF16), -1).astype(F32)

    fh, fl, wh, wl = dft_tables(length, bins, 2 * halfwidth)
    latent_grad = pl.pallas_call(
        unsmooth_kernel,
        out_shape=jax.ShapeDtypeStruct((latent_dim, bins), F32),
        in_specs=[VMEM] * 8,
        out_specs=VMEM,
        compiler_params=pltpu.CompilerParams(vmem_limit_bytes=40 * 2**20),
        cost_estimate=pl.CostEstimate(flops=mxu, bytes_accessed=6 * 2**20, transcendentals=0),
        name="unsmooth",
    )(grad_low, grad, grad_high, spectrum, fh, fl, wh, wl)
    return latent_grad, loading_grad


def solution(mesh):
    return jax.shard_map(
        local,
        mesh=mesh,
        in_specs=(
            P(None, ("groups", "tm")),
            P(),
            P(("groups", "tm"), None),
            P(None, None, None, ("groups", "tm")),
            P(("groups", "tm"), None, None),
            P(("groups", "tm"), None, None),
            P(None, None, ("groups", "tm")),
        ),
        out_specs=(P(None, ("groups", "tm")), P(("groups", "tm"), None)),
        check_vma=False,
    )
```

```python
import functools

import jax
import jax.numpy as jnp
import numpy as np
from jax import lax
from jax.experimental import pallas as pl
from jax.experimental.pallas import tpu as pltpu
from jax.sharding import PartitionSpec as P

BLK = 128
ROW = 4
VMEM_LIMIT = 60 * 2**20
F32 = jnp.float32
BF16 = jnp.bfloat16
VMEM = pl.BlockSpec(memory_space=pltpu.VMEM)
HBM = pl.BlockSpec(memory_space=pltpu.HBM)


def split_const(a):
    high = a.astype(jnp.bfloat16)
    low = (a - high.astype(np.float64)).astype(jnp.bfloat16)
    return high, low


@functools.lru_cache(maxsize=None)
def dft_tables(length, outputs, first):
    half = length // 2
    t = np.arange(length)[:, None]
    f = np.arange(half)[None, :]
    angle = 2 * np.pi * ((t * f) % length) / length
    cos, sin = np.cos(angle), np.sin(angle)
    sin[:, 0] = 1 - 2 * (np.arange(length) % 2)
    forward = np.concatenate([cos, sin], axis=1)
    weight = np.full((half,), 2.0 / length)
    weight[0] = 1.0 / length
    inverse = (forward * np.concatenate([weight, weight])[None, :]).T
    inverse = inverse[:, first : first + outputs]
    return split_const(forward) + split_const(inverse)


def parts(a):
    high = a.astype(BF16)
    return high, (a - high.astype(F32)).astype(BF16)


def dot3(a, b_high, b_low):
    high, low = a
    out = jnp.dot(high, b_high, preferred_element_type=F32)
    out += jnp.dot(low, b_high, preferred_element_type=F32)
    out += jnp.dot(high, b_low, preferred_element_type=F32)
    return out


def product(signal, taps, sign):
    half = signal.shape[1] // 2
    xr, xi = signal[:, :half], signal[:, half:]
    kr, ki = taps[:, :half], taps[:, half:]
    first = lax.broadcasted_iota(jnp.int32, kr.shape, 1) == 0
    kr_i = jnp.where(first, ki, kr)
    ki_x = jnp.where(first, 0.0, ki) * sign
    return jnp.concatenate([xr * kr + xi * ki_x, xi * kr_i - xr * ki_x], axis=1)


def with_halo(mid, core_side, far_side, fh, fl):
    width = core_side[0].shape[1]
    bins = mid.shape[1]
    even = lax.rem(lax.axis_index("tm"), 2) == 0
    out = dot3(parts(mid), fh[width : width + bins], fl[width : width + bins])
    for side, later in ((core_side, even), (far_side, jnp.logical_not(even))):
        rows = pl.ds(pl.multiple_of(jnp.where(later, width + bins, 0), BLK), width)
        out += dot3(side, fh[rows], fl[rows])
    return out


def load(sources, targets, sem):
    copies = [
        pltpu.make_async_copy(s, t, sem.at[i]) for i, (s, t) in enumerate(zip(sources, targets))
    ]
    for copy in copies:
        copy.start()
    return copies


def smooth_kernel(mid, core_side, far_side, taps, *refs):
    tables, (out, spectrum), held, sem = refs[:4], refs[4:6], refs[6:10], refs[10]
    copies = load(tables, held, sem)
    fh, fl, wh, wl = held
    copies[0].wait()
    copies[1].wait()
    count = taps.shape[1]
    k_spec = dot3(parts(taps[...]), fh[:count], fl[:count])
    spectrum[...] = k_spec
    x_spec = with_halo(mid[...], parts(core_side[...]), parts(far_side[...]), fh, fl)
    copies[2].wait()
    copies[3].wait()
    out[...] = dot3(parts(product(x_spec, k_spec, 1.0)), wh[...], wl[...]).astype(out.dtype)


def unsmooth_kernel(mid, core_terms, far_side, k_spec, *refs):
    tables, out, held, sem = refs[:4], refs[4], refs[5:10], refs[10]
    first = core_terms.shape[0] - far_side.shape[0]
    copies = load(tables + (core_terms.at[pl.ds(first, far_side.shape[0])],), held, sem)
    fh, fl, wh, wl, core_side = held
    width = far_side.shape[1] // 2
    for i in (0, 1, 4):
        copies[i].wait()
    x_spec = with_halo(
        mid[...],
        (core_side[:, :width], core_side[:, width:]),
        (far_side[:, :width], far_side[:, width:]),
        fh,
        fl,
    )
    copies[2].wait()
    copies[3].wait()
    out[...] = dot3(parts(product(x_spec, k_spec[...], -1.0)), wh[...], wl[...])


def place_of(ids, e, blocks, forward):
    me = lax.axis_index("tm")
    chain = lax.axis_size("tm") // ROW
    top = ids.shape[1]
    code = ids[e // top, e % top]
    owner, slot = code // blocks, code % blocks
    step = owner // ROW - me // ROW
    step = step if forward else -step
    turn = jnp.where(step < 0, step + chain, step)
    piece = jnp.where((owner // 2) % 2 == (me // 2) % 2, 0, chain) + turn
    return owner % 2 == me % 2, piece, pl.multiple_of(slot * BLK, BLK)


def pack_kernel(entries, late, asked, *refs):
    pieces, (out, sem) = refs[:-2], refs[-2:]
    blocks = pieces[0].shape[0] // BLK

    def copy(piece, e, row):
        return pltpu.make_async_copy(
            piece.at[pl.ds(row, BLK)], out.at[pl.ds(pl.multiple_of(e * BLK, BLK), BLK)], sem.at[e]
        )

    def start(e, _):
        core, piece, row = place_of(asked, e, blocks, False)
        for q, ref in enumerate(pieces[:late] + (None,) + pieces[late:]):
            if q == late:
                continue

            @pl.when(jnp.logical_and(core, piece == q))
            def _():
                copy(ref, e, row).start()

        return 0

    def wait(e, _):
        core, piece, row = place_of(asked, e, blocks, False)

        @pl.when(jnp.logical_and(core, piece != late))
        def _():
            copy(pieces[0], e, row).wait()

        return 0

    lax.fori_loop(0, entries, start, 0)
    lax.fori_loop(0, entries, wait, 0)


def session_kernel(
    entries, group, late, ids, mask, smoothed, recorded, packed, late_theirs, *refs
):
    pieces = refs[:-6]
    grad, far_side, terms, rows, resid, sem = refs[-6:]
    blocks = pieces[0].shape[0] // BLK
    bins = smoothed.shape[1]
    top = ids.shape[1]

    def copy(source, e, row):
        return pltpu.make_async_copy(source.at[pl.ds(row, BLK)], rows.at[e], sem.at[e])

    def fetch(e, _):
        core, piece, row = place_of(ids, e, blocks, False)
        for q, ref in enumerate(pieces):

            @pl.when(jnp.logical_and(core, piece == q))
            def _():
                copy(ref, e, row).start()

        @pl.when(jnp.logical_and(jnp.logical_not(core), piece != late))
        def _():
            copy(packed, e, pl.multiple_of(e * BLK, BLK)).start()

        @pl.when(jnp.logical_and(jnp.logical_not(core), piece == late))
        def _():
            copy(late_theirs, e, row).start()

        return 0

    lax.fori_loop(0, entries, fetch, 0)
    grad[...] = jnp.zeros_like(grad)
    depth = group * BLK

    def step(g, _):
        for i in range(group):
            copy(packed, g * group + i, 0).wait()
        block = rows[pl.ds(g * group, group)].reshape(depth, rows.shape[2])
        predicted = jnp.dot(block, smoothed[...], preferred_element_type=F32)
        for i in range(group):
            e = g * group + i
            for t in range(bins // BLK):
                cut = slice(t * BLK, (t + 1) * BLK)
                weight = mask[e // top, t, e % top].astype(F32)
                part = predicted[i * BLK : (i + 1) * BLK, cut]
                seen = recorded[e, :, cut].astype(F32)
                resid[i * BLK : (i + 1) * BLK, cut] = (weight * (part - seen)).astype(BF16)
        term = lax.dot_general(
            resid[...], smoothed[...], (((1,), (1,)), ((), ())), preferred_element_type=F32
        )
        target = pl.ds(pl.multiple_of(g * depth, depth), depth)
        terms[target] = (term * (1.0 / BLK)).astype(BF16)
        grad[...] += lax.dot_general(
            block, resid[...], (((0,), (0,)), ((), ())), preferred_element_type=F32
        ) * (1.0 / BLK)
        return 0

    lax.fori_loop(0, entries // group, step, 0)
    width = far_side.shape[1] // 2
    even = lax.rem(lax.axis_index("tm"), 2) == 0
    later, earlier = grad[:, bins - width :], grad[:, :width]
    core_edge, far_edge = jnp.where(even, later, earlier), jnp.where(even, earlier, later)
    target = pl.ds(entries * BLK, far_side.shape[0])
    terms[target] = jnp.concatenate(parts(core_edge), axis=1)
    far_side[...] = jnp.concatenate(parts(far_edge), axis=1)


def merge_late_kernel(entries, late, ids, asked, own, got, out, slots, sums, sem):
    blocks = out.shape[0] // BLK

    def each(act):
        def body(e, _):
            for i, (names, terms) in enumerate(((ids, own), (asked, got))):
                core, piece, row = place_of(names, e, blocks, True)

                @pl.when(jnp.logical_and(core, piece == late))
                def _():
                    k = e * 2 + i
                    source = pl.ds(pl.multiple_of(e * BLK, BLK), BLK)
                    act(pltpu.make_async_copy(terms.at[source], slots.at[k], sem.at[k]), k, row)

            return 0

        lax.fori_loop(0, entries, body, 0)

    def start(copy, k, row):
        copy.start()

    def add(copy, k, row):
        copy.wait()
        sums[pl.ds(row, BLK)] += slots[k].astype(F32)

    each(start)
    sums[...] = jnp.zeros_like(sums)
    each(add)
    out[...] = sums[...].astype(out.dtype)


def merge_kernel(entries, late, ids, asked, own, got, *refs):
    outs, sums = refs[:-1], refs[-1]
    chunk = outs[0].shape[0]
    sums[...] = jnp.zeros_like(sums)

    def add(e, _):
        source = pl.ds(pl.multiple_of(e * BLK, BLK), BLK)
        for names, terms in ((ids, own), (asked, got)):
            core, piece, row = place_of(names, e, chunk // BLK, True)
            index = jnp.where(piece < late, piece, piece - 1)

            @pl.when(jnp.logical_and(core, piece != late))
            def _():
                target = pl.ds(pl.multiple_of(index * chunk + row, BLK), BLK)
                sums[target] += terms[source].astype(F32)

        return 0

    lax.fori_loop(0, entries, add, 0)
    for q, out in enumerate(outs):
        out[...] = sums[q * chunk : (q + 1) * chunk].astype(out.dtype)


def local(latents, kernel, loadings, recorded, owner_ids, local_ids, recorded_mask):
    latent_dim, bins = latents.shape
    halfwidth = kernel.shape[1] // 2
    count = lax.axis_size("tm")
    chain = count // ROW
    chunk = loadings.shape[0]
    entries = owner_ids.size
    smem = pl.BlockSpec(memory_space=pltpu.SMEM)

    def permute(x, pairs):
        return lax.ppermute(x, "tm", pairs)

    def rotate(x, r):
        return permute(x, [(i, (i + r * ROW) % count) for i in range(count)])

    def flip(x, bit):
        return permute(x, [(i, i ^ bit) for i in range(count)])

    odd_even = [(i, i + 1) for i in range(1, count - 1, 2)]
    odd_even += [(target, source) for source, target in odd_even]

    ids = owner_ids[0] * (chunk // BLK) + local_ids[0]
    asked = flip(ids, 1)
    mask = jnp.transpose(recorded_mask, (0, 2, 1))

    even = lax.axis_index("tm") % 2 == 0
    later, earlier = latents[:, bins - halfwidth :], latents[:, :halfwidth]
    core_side = flip(jnp.where(even, later, earlier), 1)
    far_side = permute(jnp.where(even, earlier, later), odd_even)

    half = chain // 2
    late = chain + half
    straight = [loadings] * chain
    for r in range(1, half):
        straight[r] = rotate(straight[r - 1], 1)
        straight[-r] = rotate(straight[1 - r], -1)
    across = [flip(loadings, 2)] + [None] * (chain - 1)
    if half > 1:
        straight[1], across[0] = lax.optimization_barrier((straight[1], across[0]))
    straight[half] = rotate(straight[half - 1], 1)
    for r in range(1, chain):
        if r != half:
            across[r] = flip(straight[r], 2)

    length = bins + 2 * halfwidth
    tables = dft_tables(length, bins, 0)
    held = [pltpu.VMEM(t.shape, BF16) for t in tables]
    mxu = latent_dim * length * (length + bins) * 6
    smoothed, spectrum = pl.pallas_call(
        smooth_kernel,
        out_shape=(
            jax.ShapeDtypeStruct((latent_dim, bins), BF16),
            jax.ShapeDtypeStruct((latent_dim, length), F32),
        ),
        in_specs=[VMEM] * 4 + [HBM] * 4,
        out_specs=(VMEM, VMEM),
        scratch_shapes=held + [pltpu.SemaphoreType.DMA((4,))],
        compiler_params=pltpu.CompilerParams(vmem_limit_bytes=VMEM_LIMIT),
        cost_estimate=pl.CostEstimate(flops=mxu, bytes_accessed=6 * 2**20, transcendentals=0),
        name="smooth",
    )(latents, core_side, far_side, kernel, *tables)

    slots = jax.ShapeDtypeStruct((entries * BLK, latent_dim), BF16)
    ids, asked, smoothed, mask = lax.optimization_barrier(
        (ids, asked, smoothed, mask)
    )
    across[half] = flip(straight[half], 2)
    early = straight + across[:half] + across[half + 1 :]
    packed = pl.pallas_call(
        functools.partial(pack_kernel, entries, late),
        out_shape=slots,
        in_specs=[smem] + [HBM] * len(early),
        out_specs=VMEM,
        scratch_shapes=[pltpu.SemaphoreType.DMA((entries,))],
        compiler_params=pltpu.CompilerParams(vmem_limit_bytes=VMEM_LIMIT),
        cost_estimate=pl.CostEstimate(flops=0, bytes_accessed=2 * 2**20, transcendentals=0),
        name="pack",
    )(asked, *early)
    packed = flip(packed, 1)
    late_theirs = flip(across[half], 1)
    pieces = straight + across

    group = 4
    extended = jax.ShapeDtypeStruct((entries * BLK + latent_dim, latent_dim), BF16)
    grad, far_side, terms = pl.pallas_call(
        functools.partial(session_kernel, entries, group, late),
        out_shape=(
            jax.ShapeDtypeStruct((latent_dim, bins), F32),
            jax.ShapeDtypeStruct((latent_dim, 2 * halfwidth), BF16),
            extended,
        ),
        in_specs=[smem] * 2 + [VMEM] * 2 + [HBM] * (2 + len(pieces)),
        out_specs=(VMEM,) * 3,
        scratch_shapes=[
            pltpu.VMEM((entries, BLK, latent_dim), BF16),
            pltpu.VMEM((group * BLK, bins), BF16),
            pltpu.SemaphoreType.DMA((entries,)),
        ],
        compiler_params=pltpu.CompilerParams(vmem_limit_bytes=VMEM_LIMIT),
        cost_estimate=pl.CostEstimate(
            flops=6 * entries * BLK * latent_dim * bins, bytes_accessed=8 * 2**20, transcendentals=0
        ),
        name="session",
    )(
        ids,
        mask,
        smoothed,
        recorded.reshape(entries, BLK, bins),
        packed,
        late_theirs,
        *pieces,
    )

    got = flip(terms, 1)
    far_side = permute(far_side, odd_even)
    narrow = jax.ShapeDtypeStruct((chunk, latent_dim), BF16)
    sent = pl.pallas_call(
        functools.partial(merge_late_kernel, entries, late),
        out_shape=narrow,
        in_specs=[smem] * 2 + [HBM] * 2,
        out_specs=VMEM,
        scratch_shapes=[
            pltpu.VMEM((2 * entries, BLK, latent_dim), BF16),
            pltpu.VMEM((chunk, latent_dim), F32),
            pltpu.SemaphoreType.DMA((2 * entries,)),
        ],
        compiler_params=pltpu.CompilerParams(vmem_limit_bytes=VMEM_LIMIT),
        cost_estimate=pl.CostEstimate(flops=0, bytes_accessed=2**20, transcendentals=0),
        name="merge_late",
    )(ids, asked, terms, got)
    back = flip(sent, 2)
    got, far_side = lax.optimization_barrier((got, far_side))
    wide = jax.ShapeDtypeStruct((chunk, latent_dim), F32)
    out_shape = (wide,) * chain + (narrow,) * (chain - 1)
    sums = pl.pallas_call(
        functools.partial(merge_kernel, entries, late),
        out_shape=out_shape,
        in_specs=[smem] * 2 + [VMEM] * 2,
        out_specs=(VMEM,) * len(out_shape),
        scratch_shapes=[pltpu.VMEM((len(out_shape) * chunk, latent_dim), F32)],
        compiler_params=pltpu.CompilerParams(vmem_limit_bytes=VMEM_LIMIT),
        cost_estimate=pl.CostEstimate(flops=0, bytes_accessed=5 * 2**20, transcendentals=0),
        name="merge",
    )(ids, asked, terms, got)
    other = {half: back}
    for r in sorted(range(chain), key=lambda r: -min(r, chain - r)):
        if r != half:
            other[r] = flip(sums[chain + r - (r > half)], 2)
    totals = [sums[r] + other[r].astype(F32) for r in range(chain)]
    rise = totals[half]
    for r in range(half - 1, -1, -1):
        rise = totals[r] + rotate(rise.astype(BF16), 1).astype(F32)
    loading_grad = rise
    if half > 1:
        fall = totals[half + 1]
        for r in range(half + 2, chain):
            fall = totals[r] + rotate(fall.astype(BF16), -1).astype(F32)
        loading_grad = loading_grad + rotate(fall.astype(BF16), -1).astype(F32)

    tables = dft_tables(length, bins, 2 * halfwidth)
    latent_grad = pl.pallas_call(
        unsmooth_kernel,
        out_shape=jax.ShapeDtypeStruct((latent_dim, bins), F32),
        in_specs=[VMEM, HBM, VMEM, VMEM] + [HBM] * 4,
        out_specs=VMEM,
        scratch_shapes=held
        + [pltpu.VMEM((latent_dim, 2 * halfwidth), BF16), pltpu.SemaphoreType.DMA((5,))],
        compiler_params=pltpu.CompilerParams(vmem_limit_bytes=VMEM_LIMIT),
        cost_estimate=pl.CostEstimate(flops=mxu, bytes_accessed=6 * 2**20, transcendentals=0),
        name="unsmooth",
    )(grad, got, far_side, spectrum, *tables)
    return latent_grad, loading_grad


def solution(mesh):
    return jax.shard_map(
        local,
        mesh=mesh,
        in_specs=(
            P(None, ("groups", "tm")),
            P(),
            P(("groups", "tm"), None),
            P(None, None, None, ("groups", "tm")),
            P(("groups", "tm"), None, None),
            P(("groups", "tm"), None, None),
            P(None, None, ("groups", "tm")),
        ),
        out_specs=(P(None, ("groups", "tm")), P(("groups", "tm"), None)),
        check_vma=False,
    )
```

```python
import functools

import jax
import jax.numpy as jnp
import numpy as np
from jax import lax
from jax.experimental import pallas as pl
from jax.experimental.pallas import tpu as pltpu
from jax.sharding import PartitionSpec as P

BLK = 128
ROW = 4
MIB = 2**20
F32 = jnp.float32
BF16 = jnp.bfloat16
VMEM = pl.BlockSpec(memory_space=pltpu.VMEM)
HBM = pl.BlockSpec(memory_space=pltpu.HBM)


def split_const(a):
    high = a.astype(jnp.bfloat16)
    low = (a - high.astype(np.float64)).astype(jnp.bfloat16)
    return high, low


@functools.lru_cache(maxsize=None)
def dft_tables(size):
    t = np.arange(size)[:, None]
    g = np.arange(size)[None, :]
    half = size // 2
    angle = 2 * np.pi * ((t * g[:, :half]) % size) / size
    cos, sin = np.cos(angle), np.sin(angle)
    sin[:, 0] = 1 - 2 * (np.arange(size) % 2)
    real = np.concatenate([cos, sin], axis=1)
    angle = 2 * np.pi * ((t * (3 * g + 1)) % (3 * size)) / (3 * size)
    cos, sin = np.cos(angle), np.sin(angle)
    weight = np.full((size,), 2.0)
    weight[0] = weight[half] = 1.0
    scale = 1.0 / (3 * size)
    tables = [real, cos, sin, (real * weight).T * scale, cos.T * 2 * scale, sin.T * 2 * scale]
    return np.concatenate([part for table in tables for part in split_const(table)])


def parts(a):
    high = a.astype(BF16)
    return high, (a - high.astype(F32)).astype(BF16)


def times(a, tables, index):
    rows, size = a.shape
    high, low = parts(a)
    t_high = tables[2 * index * size : (2 * index + 1) * size]
    t_low = tables[(2 * index + 1) * size : (2 * index + 2) * size]
    out = jnp.dot(jnp.concatenate([high, low]), t_high, preferred_element_type=F32)
    return out[:rows] + out[rows:] + jnp.dot(high, t_low, preferred_element_type=F32)


ROOT = 0.75**0.5


def spectrum_of(thirds, tables):
    first, second, third = thirds
    rows = first.shape[0]
    base = times(first + second + third, tables, 0)
    y = jnp.concatenate([first - 0.5 * (second + third), ROOT * (third - second)])
    cos, sin = times(y, tables, 1), times(y, tables, 2)
    return base, cos[:rows] + sin[rows:], cos[rows:] - sin[:rows]


def filtered(signal, taps, sign, tables, wanted):
    (xb, xr, xi), (kb, kr, ki) = signal, taps
    rows, size = xb.shape
    half = size // 2
    first = lax.broadcasted_iota(jnp.int32, (rows, half), 1) == 0
    kc, ks = kb[:, :half], kb[:, half:]
    kc_s = jnp.where(first, ks, kc)
    ks_x = jnp.where(first, 0.0, ks) * sign
    xc, xs = xb[:, :half], xb[:, half:]
    base = times(jnp.concatenate([xc * kc + xs * ks_x, xs * kc_s - xc * ks_x], axis=1), tables, 3)
    ki = ki * sign
    z = jnp.concatenate([xr * kr + xi * ki, xi * kr - xr * ki])
    cos, sin = times(z, tables, 4), times(z, tables, 5)
    vr, vi = cos[:rows] - sin[rows:], sin[:rows] + cos[rows:]
    each = (base + vr, base - 0.5 * vr - ROOT * vi, base - 0.5 * vr + ROOT * vi)
    return jnp.concatenate([each[m] for m in wanted], axis=1)


def thirds_of(mid, core_side, far_side):
    width = core_side.shape[1]
    size = 2 * width
    even = lax.rem(lax.axis_index("tm"), 2) == 0
    low, high = jnp.where(even, far_side, core_side), jnp.where(even, core_side, far_side)
    last = mid.shape[1] - width
    return (
        jnp.concatenate([low, mid[:, :width]], axis=1),
        mid[:, width : width + size],
        jnp.concatenate([mid[:, last:], high], axis=1),
    )


def smooth_kernel(mid, core_side, far_side, taps, table, out, *refs):
    spectrum, held, sem = refs[:3], refs[3], refs[4]
    copy = pltpu.make_async_copy(table, held, sem)
    copy.start()
    thirds = thirds_of(mid[...], core_side[...], far_side[...])
    copy.wait()
    base = times(taps[...], held, 0)
    kr, ki = times(taps[...], held, 1), -times(taps[...], held, 2)
    for ref, value in zip(spectrum, (base, kr, ki)):
        ref[...] = value
    signal = spectrum_of(thirds, held)
    out[...] = filtered(signal, (base, kr, ki), 1.0, held, (0, 1)).astype(out.dtype)


def unsmooth_kernel(mid, core_side, far_side, base, kr, ki, table, out, held, sem):
    copy = pltpu.make_async_copy(table, held, sem)
    copy.start()
    width = far_side.shape[1] // 2
    first = core_side.shape[0] - far_side.shape[0]
    core = core_side[first:, :width].astype(F32) + core_side[first:, width:].astype(F32)
    far = far_side[:, :width].astype(F32) + far_side[:, width:].astype(F32)
    thirds = thirds_of(mid[...], core, far)
    copy.wait()
    signal = spectrum_of(thirds, held)
    out[...] = filtered(signal, (base[...], kr[...], ki[...]), -1.0, held, (1, 2))


def divide(a, n):
    return a >> (n.bit_length() - 1) if n & (n - 1) == 0 else a // n


def remainder(a, n):
    return a & (n - 1) if n & (n - 1) == 0 else a % n


def place_of(ids, e, me, blocks, forward):
    chain = lax.axis_size("tm") // ROW
    top = ids.shape[1]
    code = ids[divide(e, top), remainder(e, top)]
    owner, slot = divide(code, blocks), remainder(code, blocks)
    step = divide(owner, ROW) - divide(me, ROW)
    step = step if forward else -step
    turn = jnp.where(step < 0, step + chain, step)
    differ = owner ^ me
    piece = jnp.where(differ & 2 == 0, 0, chain) + turn
    return differ & 1 == 0, piece, pl.multiple_of(slot * BLK, BLK)


def pick(refs, index, act):
    if len(refs) == 1:
        act(refs[0])
        return
    half = len(refs) // 2
    lax.cond(
        index < half,
        lambda: pick(refs[:half], index, act),
        lambda: pick(refs[half:], index - half, act),
    )


def pack_kernel(entries, late, asked, *refs):
    pieces, out = refs[:-1], refs[-1]
    blocks = pieces[0].shape[0] // BLK
    me = lax.axis_index("tm")

    def body(e, _):
        core, piece, row = place_of(asked, e, me, blocks, False)
        target = pl.ds(pl.multiple_of(e * BLK, BLK), BLK)

        @pl.when(jnp.logical_and(core, piece != late))
        def _():
            def act(ref):
                out[target] = ref[pl.ds(row, BLK)]

            pick(pieces, jnp.where(piece < late, piece, piece - 1), act)

        return 0

    lax.fori_loop(0, entries, body, 0)


def session_kernel(
    entries, group, late, ids, mask, smoothed, recorded, packed, late_theirs, *refs
):
    pieces = refs[:-5]
    grad, far_side, terms, rows, resid = refs[-5:]
    blocks = pieces[0].shape[0] // BLK
    bins = smoothed.shape[1]
    top = ids.shape[1]
    me = lax.axis_index("tm")
    grad[...] = jnp.zeros_like(grad)
    depth = group * BLK

    def step(g, _):
        for i in range(group):
            e = g * group + i
            core, piece, row = place_of(ids, e, me, blocks, False)

            def own():
                def act(ref):
                    rows[i * BLK : (i + 1) * BLK] = ref[pl.ds(row, BLK)]

                pick(pieces, piece, act)

            def other():
                @pl.when(piece == late)
                def _():
                    rows[i * BLK : (i + 1) * BLK] = late_theirs[pl.ds(row, BLK)]

                @pl.when(piece != late)
                def _():
                    source = pl.ds(pl.multiple_of(e * BLK, BLK), BLK)
                    rows[i * BLK : (i + 1) * BLK] = packed[source]

            lax.cond(core, own, other)
        block = rows[...]
        predicted = jnp.dot(block, smoothed[...], preferred_element_type=F32)
        for i in range(group):
            e = g * group + i
            for t in range(bins // BLK):
                cut = slice(t * BLK, (t + 1) * BLK)
                weight = mask[divide(e, top), t, remainder(e, top)].astype(F32)
                part = predicted[i * BLK : (i + 1) * BLK, cut]
                seen = recorded[e, :, cut].astype(F32)
                resid[i * BLK : (i + 1) * BLK, cut] = (weight * (part - seen)).astype(BF16)
        term = lax.dot_general(
            resid[...], smoothed[...], (((1,), (1,)), ((), ())), preferred_element_type=F32
        )
        target = pl.ds(pl.multiple_of(g * depth, depth), depth)
        terms[target] = (term * (1.0 / BLK)).astype(BF16)
        grad[...] += lax.dot_general(
            block, resid[...], (((0,), (0,)), ((), ())), preferred_element_type=F32
        ) * (1.0 / BLK)
        return 0

    lax.fori_loop(0, entries // group, step, 0)
    width = far_side.shape[1] // 2
    even = me & 1 == 0
    later, earlier = grad[:, bins - width :], grad[:, :width]
    core_edge, far_edge = jnp.where(even, later, earlier), jnp.where(even, earlier, later)
    target = pl.ds(entries * BLK, far_side.shape[0])
    terms[target] = jnp.concatenate(parts(core_edge), axis=1)
    far_side[...] = jnp.concatenate(parts(far_edge), axis=1)


def merge_late_kernel(entries, late, ids, asked, own, got, out, sums):
    blocks = out.shape[0] // BLK
    me = lax.axis_index("tm")
    sums[...] = jnp.zeros_like(sums)

    def add(e, _):
        source = pl.ds(pl.multiple_of(e * BLK, BLK), BLK)
        for names, terms in ((ids, own), (asked, got)):
            core, piece, row = place_of(names, e, me, blocks, True)

            @pl.when(jnp.logical_and(core, piece == late))
            def _():
                sums[pl.ds(row, BLK)] += terms[source].astype(F32)

        return 0

    lax.fori_loop(0, entries, add, 0)
    out[...] = sums[...].astype(out.dtype)


def merge_kernel(entries, late, ids, asked, own, got, *refs):
    chain = len(refs) // 2
    kept, outs, sums = refs[:chain], refs[chain:-1], refs[-1]
    chunk = kept[0].shape[0]
    me = lax.axis_index("tm")
    for ref in kept:
        ref[...] = jnp.zeros_like(ref)
    sums[...] = jnp.zeros_like(sums)

    def add(e, _):
        source = pl.ds(pl.multiple_of(e * BLK, BLK), BLK)
        for names, terms in ((ids, own), (asked, got)):
            core, piece, row = place_of(names, e, me, chunk // BLK, True)
            index = jnp.where(piece < late, piece - chain, piece - 1 - chain)

            @pl.when(jnp.logical_and(core, piece < chain))
            def _():
                def act(ref):
                    ref[pl.ds(row, BLK)] += terms[source].astype(F32)

                pick(kept, piece, act)

            @pl.when(jnp.logical_and(core, jnp.logical_and(piece >= chain, piece != late)))
            def _():
                sums[pl.ds(pl.multiple_of(index * chunk + row, BLK), BLK)] += terms[source].astype(F32)

        return 0

    lax.fori_loop(0, entries, add, 0)
    for q, out in enumerate(outs):
        out[...] = sums[q * chunk : (q + 1) * chunk].astype(out.dtype)


def local(latents, kernel, loadings, recorded, owner_ids, local_ids, recorded_mask):
    latent_dim, bins = latents.shape
    halfwidth = kernel.shape[1] // 2
    count = lax.axis_size("tm")
    chain = count // ROW
    chunk = loadings.shape[0]
    entries = owner_ids.size
    piece_bytes = count * chunk * latent_dim
    smem = pl.BlockSpec(memory_space=pltpu.SMEM)

    def permute(x, pairs):
        return lax.ppermute(x, "tm", pairs)

    def rotate(x, r):
        return permute(x, [(i, (i + r * ROW) % count) for i in range(count)])

    def flip(x, bit):
        return permute(x, [(i, i ^ bit) for i in range(count)])

    odd_even = [(i, i + 1) for i in range(1, count - 1, 2)]
    odd_even += [(target, source) for source, target in odd_even]

    ids = owner_ids[0] * (chunk // BLK) + local_ids[0]
    asked = flip(ids, 1)
    mask = jnp.transpose(recorded_mask, (0, 2, 1))

    even = lax.axis_index("tm") % 2 == 0
    later, earlier = latents[:, bins - halfwidth :], latents[:, :halfwidth]
    core_side = flip(jnp.where(even, later, earlier), 1)
    far_side = permute(jnp.where(even, earlier, later), odd_even)

    half = chain // 2
    late = chain + half
    straight = [loadings] * chain
    for r in range(1, half):
        straight[r] = rotate(straight[r - 1], 1)
        straight[-r] = rotate(straight[1 - r], -1)
    across = [flip(loadings, 2)] + [None] * (chain - 1)
    if half > 1:
        straight[1], across[0] = lax.optimization_barrier((straight[1], across[0]))
    straight[half] = rotate(straight[half - 1], 1)
    for r in range(1, chain):
        if r != half:
            across[r] = flip(straight[r], 2)

    table = dft_tables(2 * halfwidth)
    table_scratch = [pltpu.VMEM(table.shape, BF16), pltpu.SemaphoreType.DMA(())]
    mxu = 40 * 2 * latent_dim * (2 * halfwidth) ** 2
    square = jax.ShapeDtypeStruct((latent_dim, 2 * halfwidth), F32)
    smoothed, *spectrum = pl.pallas_call(
        smooth_kernel,
        out_shape=(jax.ShapeDtypeStruct((latent_dim, bins), BF16),) + (square,) * 3,
        in_specs=[VMEM] * 4 + [HBM],
        out_specs=(VMEM,) * 4,
        scratch_shapes=table_scratch,
        compiler_params=pltpu.CompilerParams(vmem_limit_bytes=16 * MIB),
        cost_estimate=pl.CostEstimate(flops=mxu, bytes_accessed=4 * 2**20, transcendentals=0),
        name="smooth",
    )(latents, core_side, far_side, kernel, table)

    slots = jax.ShapeDtypeStruct((entries * BLK, latent_dim), BF16)
    ids, asked, smoothed, mask = lax.optimization_barrier(
        (ids, asked, smoothed, mask)
    )
    across[half] = flip(straight[half], 2)
    early = straight + across[:half] + across[half + 1 :]
    packed = pl.pallas_call(
        functools.partial(pack_kernel, entries, late),
        out_shape=slots,
        in_specs=[smem] + [VMEM] * len(early),
        out_specs=VMEM,
        compiler_params=pltpu.CompilerParams(vmem_limit_bytes=4 * MIB + 3 * piece_bytes),
        cost_estimate=pl.CostEstimate(flops=0, bytes_accessed=2 * 2**20, transcendentals=0),
        name="pack",
    )(asked, *early)
    packed = flip(packed, 1)
    late_theirs = flip(across[half], 1)
    pieces = straight + across

    group = 4
    extended = jax.ShapeDtypeStruct((entries * BLK + latent_dim, latent_dim), BF16)
    grad, far_side, terms = pl.pallas_call(
        functools.partial(session_kernel, entries, group, late),
        out_shape=(
            jax.ShapeDtypeStruct((latent_dim, bins), F32),
            jax.ShapeDtypeStruct((latent_dim, 2 * halfwidth), BF16),
            extended,
        ),
        in_specs=[smem] * 2 + [VMEM] * (4 + len(pieces)),
        out_specs=(VMEM,) * 3,
        scratch_shapes=[
            pltpu.VMEM((group * BLK, latent_dim), BF16),
            pltpu.VMEM((group * BLK, bins), BF16),
        ],
        compiler_params=pltpu.CompilerParams(vmem_limit_bytes=12 * MIB + 6 * piece_bytes),
        cost_estimate=pl.CostEstimate(
            flops=6 * entries * BLK * latent_dim * bins, bytes_accessed=8 * 2**20, transcendentals=0
        ),
        name="session",
    )(
        ids,
        mask,
        smoothed,
        recorded.reshape(entries, BLK, bins),
        packed,
        late_theirs,
        *pieces,
    )

    got = flip(terms, 1)
    narrow = jax.ShapeDtypeStruct((chunk, latent_dim), BF16)
    sent = pl.pallas_call(
        functools.partial(merge_late_kernel, entries, late),
        out_shape=narrow,
        in_specs=[smem] * 2 + [VMEM] * 2,
        out_specs=VMEM,
        scratch_shapes=[pltpu.VMEM((chunk, latent_dim), F32)],
        compiler_params=pltpu.CompilerParams(vmem_limit_bytes=4 * MIB + 3 * piece_bytes),
        cost_estimate=pl.CostEstimate(flops=0, bytes_accessed=2**20, transcendentals=0),
        name="merge_late",
    )(ids, asked, terms, got)
    back = flip(sent, 2)
    far_side, back = lax.optimization_barrier((far_side, back))
    far_side = permute(far_side, odd_even)
    wide = jax.ShapeDtypeStruct((chunk, latent_dim), F32)
    merged = pl.pallas_call(
        functools.partial(merge_kernel, entries, late),
        out_shape=(wide,) * chain + (narrow,) * (chain - 1),
        in_specs=[smem] * 2 + [VMEM] * 2,
        out_specs=(VMEM,) * (2 * chain - 1),
        scratch_shapes=[pltpu.VMEM(((chain - 1) * chunk, latent_dim), F32)],
        compiler_params=pltpu.CompilerParams(vmem_limit_bytes=4 * MIB + 6 * piece_bytes),
        cost_estimate=pl.CostEstimate(flops=0, bytes_accessed=5 * 2**20, transcendentals=0),
        name="merge",
    )(ids, asked, terms, got)
    other = {half: back}
    for r in sorted(range(chain), key=lambda r: -min(r, chain - r)):
        if r != half:
            other[r] = flip(merged[chain + r - (r > half)], 2)
    totals = [merged[r] + other[r].astype(F32) for r in range(chain)]
    rise = totals[half]
    for r in range(half - 1, -1, -1):
        rise = totals[r] + rotate(rise.astype(BF16), 1).astype(F32)
    loading_grad = rise
    if half > 1:
        fall = totals[half + 1]
        for r in range(half + 2, chain):
            fall = totals[r] + rotate(fall.astype(BF16), -1).astype(F32)
        loading_grad = loading_grad + rotate(fall.astype(BF16), -1).astype(F32)

    latent_grad = pl.pallas_call(
        unsmooth_kernel,
        out_shape=jax.ShapeDtypeStruct((latent_dim, bins), F32),
        in_specs=[VMEM] * 6 + [HBM],
        out_specs=VMEM,
        scratch_shapes=table_scratch,
        compiler_params=pltpu.CompilerParams(vmem_limit_bytes=16 * MIB),
        cost_estimate=pl.CostEstimate(flops=mxu, bytes_accessed=4 * 2**20, transcendentals=0),
        name="unsmooth",
    )(grad, got, far_side, *spectrum, table)
    return latent_grad, loading_grad


def solution(mesh):
    return jax.shard_map(
        local,
        mesh=mesh,
        in_specs=(
            P(None, ("groups", "tm")),
            P(),
            P(("groups", "tm"), None),
            P(None, None, None, ("groups", "tm")),
            P(("groups", "tm"), None, None),
            P(("groups", "tm"), None, None),
            P(None, None, ("groups", "tm")),
        ),
        out_specs=(P(None, ("groups", "tm")), P(("groups", "tm"), None)),
        check_vma=False,
    )
```

```python
import functools

import jax
import jax.numpy as jnp
import numpy as np
from jax import lax
from jax.experimental import pallas as pl
from jax.experimental.pallas import tpu as pltpu
from jax.sharding import PartitionSpec as P

BLK = 128
ROW = 4
MIB = 2**20
F32 = jnp.float32
BF16 = jnp.bfloat16
VMEM = pl.BlockSpec(memory_space=pltpu.VMEM)
HBM = pl.BlockSpec(memory_space=pltpu.HBM)


def split_const(a):
    high = a.astype(jnp.bfloat16)
    low = (a - high.astype(np.float64)).astype(jnp.bfloat16)
    return high, low


@functools.lru_cache(maxsize=None)
def dft_tables(size):
    t = np.arange(size)[:, None]
    g = np.arange(size)[None, :]
    half = size // 2
    angle = 2 * np.pi * ((t * g[:, :half]) % size) / size
    cos, sin = np.cos(angle), np.sin(angle)
    sin[:, 0] = 1 - 2 * (np.arange(size) % 2)
    real = np.concatenate([cos, sin], axis=1)
    angle = 2 * np.pi * ((t * (3 * g + 1)) % (3 * size)) / (3 * size)
    cos, sin = np.cos(angle), np.sin(angle)
    weight = np.full((size,), 2.0)
    weight[0] = weight[half] = 1.0
    scale = 1.0 / (3 * size)
    tables = [real, cos, sin, (real * weight).T * scale, cos.T * 2 * scale, sin.T * 2 * scale]
    return np.concatenate([part for table in tables for part in split_const(table)])


def parts(a):
    high = a.astype(BF16)
    return high, (a - high.astype(F32)).astype(BF16)


def times(a, tables, index):
    rows, size = a.shape
    high, low = parts(a)
    t_high = tables[2 * index * size : (2 * index + 1) * size]
    t_low = tables[(2 * index + 1) * size : (2 * index + 2) * size]
    out = jnp.dot(jnp.concatenate([high, low]), t_high, preferred_element_type=F32)
    return out[:rows] + out[rows:] + jnp.dot(high, t_low, preferred_element_type=F32)


ROOT = 0.75**0.5


def spectrum_of(thirds, tables):
    first, second, third = thirds
    rows = first.shape[0]
    base = times(first + second + third, tables, 0)
    y = jnp.concatenate([first - 0.5 * (second + third), ROOT * (third - second)])
    cos, sin = times(y, tables, 1), times(y, tables, 2)
    return base, cos[:rows] + sin[rows:], cos[rows:] - sin[:rows]


def filtered(signal, taps, sign, tables, wanted):
    (xb, xr, xi), (kb, kr, ki) = signal, taps
    rows, size = xb.shape
    half = size // 2
    first = lax.broadcasted_iota(jnp.int32, (rows, half), 1) == 0
    kc, ks = kb[:, :half], kb[:, half:]
    kc_s = jnp.where(first, ks, kc)
    ks_x = jnp.where(first, 0.0, ks) * sign
    xc, xs = xb[:, :half], xb[:, half:]
    base = times(jnp.concatenate([xc * kc + xs * ks_x, xs * kc_s - xc * ks_x], axis=1), tables, 3)
    ki = ki * sign
    z = jnp.concatenate([xr * kr + xi * ki, xi * kr - xr * ki])
    cos, sin = times(z, tables, 4), times(z, tables, 5)
    vr, vi = cos[:rows] - sin[rows:], sin[:rows] + cos[rows:]
    each = (base + vr, base - 0.5 * vr - ROOT * vi, base - 0.5 * vr + ROOT * vi)
    return jnp.concatenate([each[m] for m in wanted], axis=1)


def thirds_of(mid, core_side, far_side):
    width = core_side.shape[1]
    size = 2 * width
    even = lax.rem(lax.axis_index("tm"), 2) == 0
    low, high = jnp.where(even, far_side, core_side), jnp.where(even, core_side, far_side)
    last = mid.shape[1] - width
    return (
        jnp.concatenate([low, mid[:, :width]], axis=1),
        mid[:, width : width + size],
        jnp.concatenate([mid[:, last:], high], axis=1),
    )


def smooth_kernel(mid, core_side, far_side, taps, table, out, *refs):
    spectrum, held, sem = refs[:3], refs[3], refs[4]
    copy = pltpu.make_async_copy(table, held, sem)
    copy.start()
    thirds = thirds_of(mid[...], core_side[...], far_side[...])
    copy.wait()
    base = times(taps[...], held, 0)
    kr, ki = times(taps[...], held, 1), -times(taps[...], held, 2)
    for ref, value in zip(spectrum, (base, kr, ki)):
        ref[...] = value
    signal = spectrum_of(thirds, held)
    out[...] = filtered(signal, (base, kr, ki), 1.0, held, (0, 1)).astype(out.dtype)


def unsmooth_kernel(mid, core_side, far_side, base, kr, ki, table, out, held, sem):
    copy = pltpu.make_async_copy(table, held, sem)
    copy.start()
    width = far_side.shape[1] // 2
    first = core_side.shape[0] - far_side.shape[0]
    core = core_side[first:, :width].astype(F32) + core_side[first:, width:].astype(F32)
    far = far_side[:, :width].astype(F32) + far_side[:, width:].astype(F32)
    thirds = thirds_of(mid[...], core, far)
    copy.wait()
    signal = spectrum_of(thirds, held)
    out[...] = filtered(signal, (base[...], kr[...], ki[...]), -1.0, held, (1, 2))


def divide(a, n):
    return a >> (n.bit_length() - 1) if n & (n - 1) == 0 else a // n


def remainder(a, n):
    return a & (n - 1) if n & (n - 1) == 0 else a % n


def place_of(ids, e, me, blocks, forward):
    chain = lax.axis_size("tm") // ROW
    top = ids.shape[1]
    code = ids[divide(e, top), remainder(e, top)]
    owner, slot = divide(code, blocks), remainder(code, blocks)
    step = divide(owner, ROW) - divide(me, ROW)
    step = step if forward else -step
    turn = jnp.where(step < 0, step + chain, step)
    differ = owner ^ me
    piece = jnp.where(differ & 2 == 0, 0, chain) + turn
    return differ & 1 == 0, piece, pl.multiple_of(slot * BLK, BLK)


def pick(refs, index, act):
    if len(refs) == 1:
        act(refs[0])
        return
    half = len(refs) // 2
    lax.cond(
        index < half,
        lambda: pick(refs[:half], index, act),
        lambda: pick(refs[half:], index - half, act),
    )


def pack_kernel(first, entries, late, asked, *refs):
    pieces, out = refs[:-1], refs[-1]
    blocks = pieces[0].shape[0] // BLK
    me = lax.axis_index("tm")

    def body(e, _):
        core, piece, row = place_of(asked, first + e, me, blocks, False)
        target = pl.ds(pl.multiple_of(e * BLK, BLK), BLK)

        @pl.when(jnp.logical_and(core, piece != late))
        def _():
            def act(ref):
                out[target] = ref[pl.ds(row, BLK)]

            pick(pieces, jnp.where(piece < late, piece, piece - 1), act)

        return 0

    lax.fori_loop(0, entries, body, 0)


def session_kernel(
    entries, group, late, ids, mask, smoothed, recorded, packed, packed_rest, late_theirs, *refs
):
    pieces = refs[:-5]
    grad, far_side, terms, rows, resid = refs[-5:]
    blocks = pieces[0].shape[0] // BLK
    bins = smoothed.shape[1]
    top = ids.shape[1]
    me = lax.axis_index("tm")
    grad[...] = jnp.zeros_like(grad)
    depth = group * BLK

    def step(g, _):
        for i in range(group):
            e = g * group + i
            core, piece, row = place_of(ids, e, me, blocks, False)

            def own():
                def act(ref):
                    rows[i * BLK : (i + 1) * BLK] = ref[pl.ds(row, BLK)]

                pick(pieces, piece, act)

            def other():
                @pl.when(piece == late)
                def _():
                    rows[i * BLK : (i + 1) * BLK] = late_theirs[pl.ds(row, BLK)]

                @pl.when(piece != late)
                def _():
                    def act(ref):
                        source = pl.ds(pl.multiple_of(remainder(e, entries // 2) * BLK, BLK), BLK)
                        rows[i * BLK : (i + 1) * BLK] = ref[source]

                    pick((packed, packed_rest), divide(e, entries // 2), act)

            lax.cond(core, own, other)
        block = rows[...]
        predicted = jnp.dot(block, smoothed[...], preferred_element_type=F32)
        for i in range(group):
            e = g * group + i
            for t in range(bins // BLK):
                cut = slice(t * BLK, (t + 1) * BLK)
                weight = mask[divide(e, top), t, remainder(e, top)].astype(F32)
                part = predicted[i * BLK : (i + 1) * BLK, cut]
                seen = recorded[e, :, cut].astype(F32)
                resid[i * BLK : (i + 1) * BLK, cut] = (weight * (part - seen)).astype(BF16)
        term = lax.dot_general(
            resid[...], smoothed[...], (((1,), (1,)), ((), ())), preferred_element_type=F32
        )
        target = pl.ds(pl.multiple_of(g * depth, depth), depth)
        terms[target] = (term * (1.0 / BLK)).astype(BF16)
        grad[...] += lax.dot_general(
            block, resid[...], (((0,), (0,)), ((), ())), preferred_element_type=F32
        ) * (1.0 / BLK)
        return 0

    lax.fori_loop(0, entries // group, step, 0)
    width = far_side.shape[1] // 2
    even = me & 1 == 0
    later, earlier = grad[:, bins - width :], grad[:, :width]
    core_edge, far_edge = jnp.where(even, later, earlier), jnp.where(even, earlier, later)
    target = pl.ds(entries * BLK, far_side.shape[0])
    terms[target] = jnp.concatenate(parts(core_edge), axis=1)
    far_side[...] = jnp.concatenate(parts(far_edge), axis=1)


def merge_late_kernel(entries, late, ids, asked, own, got, out, sums):
    blocks = out.shape[0] // BLK
    me = lax.axis_index("tm")
    sums[...] = jnp.zeros_like(sums)

    def add(e, _):
        source = pl.ds(pl.multiple_of(e * BLK, BLK), BLK)
        for names, terms in ((ids, own), (asked, got)):
            core, piece, row = place_of(names, e, me, blocks, True)

            @pl.when(jnp.logical_and(core, piece == late))
            def _():
                sums[pl.ds(row, BLK)] += terms[source].astype(F32)

        return 0

    lax.fori_loop(0, entries, add, 0)
    out[...] = sums[...].astype(out.dtype)


def merge_kernel(entries, late, ids, asked, own, got, *refs):
    chain = len(refs) // 2
    kept, outs, sums = refs[:chain], refs[chain:-1], refs[-1]
    chunk = kept[0].shape[0]
    me = lax.axis_index("tm")
    for ref in kept:
        ref[...] = jnp.zeros_like(ref)
    sums[...] = jnp.zeros_like(sums)

    def add(e, _):
        source = pl.ds(pl.multiple_of(e * BLK, BLK), BLK)
        for names, terms in ((ids, own), (asked, got)):
            core, piece, row = place_of(names, e, me, chunk // BLK, True)
            index = jnp.where(piece < late, piece - chain, piece - 1 - chain)

            @pl.when(jnp.logical_and(core, piece < chain))
            def _():
                def act(ref):
                    ref[pl.ds(row, BLK)] += terms[source].astype(F32)

                pick(kept, piece, act)

            @pl.when(jnp.logical_and(core, jnp.logical_and(piece >= chain, piece != late)))
            def _():
                sums[pl.ds(pl.multiple_of(index * chunk + row, BLK), BLK)] += terms[source].astype(F32)

        return 0

    lax.fori_loop(0, entries, add, 0)
    for q, out in enumerate(outs):
        out[...] = sums[q * chunk : (q + 1) * chunk].astype(out.dtype)


def local(latents, kernel, loadings, recorded, owner_ids, local_ids, recorded_mask):
    latent_dim, bins = latents.shape
    halfwidth = kernel.shape[1] // 2
    count = lax.axis_size("tm")
    chain = count // ROW
    chunk = loadings.shape[0]
    entries = owner_ids.size
    piece_bytes = count * chunk * latent_dim
    smem = pl.BlockSpec(memory_space=pltpu.SMEM)

    def permute(x, pairs):
        return lax.ppermute(x, "tm", pairs)

    def rotate(x, r):
        return permute(x, [(i, (i + r * ROW) % count) for i in range(count)])

    def flip(x, bit):
        return permute(x, [(i, i ^ bit) for i in range(count)])

    odd_even = [(i, i + 1) for i in range(1, count - 1, 2)]
    odd_even += [(target, source) for source, target in odd_even]

    ids = owner_ids[0] * (chunk // BLK) + local_ids[0]
    asked = flip(ids, 1)
    mask = jnp.transpose(recorded_mask, (0, 2, 1))

    even = lax.axis_index("tm") % 2 == 0
    later, earlier = latents[:, bins - halfwidth :], latents[:, :halfwidth]
    core_side = flip(jnp.where(even, later, earlier), 1)
    far_side = permute(jnp.where(even, earlier, later), odd_even)

    half = chain // 2
    late = chain + half
    straight = [loadings] * chain
    for r in range(1, half):
        straight[r] = rotate(straight[r - 1], 1)
        straight[-r] = rotate(straight[1 - r], -1)
    across = [flip(loadings, 2)] + [None] * (chain - 1)
    if half > 1:
        straight[1], across[0] = lax.optimization_barrier((straight[1], across[0]))
    straight[half] = rotate(straight[half - 1], 1)
    for r in range(1, chain):
        if r != half:
            across[r] = flip(straight[r], 2)

    core_side, far_side, straight[half] = lax.optimization_barrier(
        (core_side, far_side, straight[half])
    )
    table = dft_tables(2 * halfwidth)
    table_scratch = [pltpu.VMEM(table.shape, BF16), pltpu.SemaphoreType.DMA(())]
    mxu = 40 * 2 * latent_dim * (2 * halfwidth) ** 2
    square = jax.ShapeDtypeStruct((latent_dim, 2 * halfwidth), F32)
    smoothed, *spectrum = pl.pallas_call(
        smooth_kernel,
        out_shape=(jax.ShapeDtypeStruct((latent_dim, bins), BF16),) + (square,) * 3,
        in_specs=[VMEM] * 4 + [HBM],
        out_specs=(VMEM,) * 4,
        scratch_shapes=table_scratch,
        compiler_params=pltpu.CompilerParams(vmem_limit_bytes=16 * MIB),
        cost_estimate=pl.CostEstimate(flops=mxu, bytes_accessed=4 * 2**20, transcendentals=0),
        name="smooth",
    )(latents, core_side, far_side, kernel, table)

    slots = jax.ShapeDtypeStruct((entries * BLK, latent_dim), BF16)
    across[half] = flip(straight[half], 2)
    early = straight + across[:half] + across[half + 1 :]

    def pack(first, total):
        return pl.pallas_call(
            functools.partial(pack_kernel, first, total, late),
            out_shape=jax.ShapeDtypeStruct((total * BLK, latent_dim), BF16),
            in_specs=[smem] + [VMEM] * len(early),
            out_specs=VMEM,
            compiler_params=pltpu.CompilerParams(vmem_limit_bytes=4 * MIB + 3 * piece_bytes),
            cost_estimate=pl.CostEstimate(flops=0, bytes_accessed=2**20, transcendentals=0),
            name="pack",
        )(asked, *early)

    asked, smoothed, mask = lax.optimization_barrier((asked, smoothed, mask))
    packed = [flip(pack(first, entries // 2), 1) for first in (0, entries // 2)]
    last, smoothed = lax.optimization_barrier((across[half], smoothed))
    late_theirs = flip(last, 1)
    pieces = straight + across

    group = 4
    extended = jax.ShapeDtypeStruct((entries * BLK + latent_dim, latent_dim), BF16)
    grad, far_side, terms = pl.pallas_call(
        functools.partial(session_kernel, entries, group, late),
        out_shape=(
            jax.ShapeDtypeStruct((latent_dim, bins), F32),
            jax.ShapeDtypeStruct((latent_dim, 2 * halfwidth), BF16),
            extended,
        ),
        in_specs=[smem] * 2 + [VMEM] * (5 + len(pieces)),
        out_specs=(VMEM,) * 3,
        scratch_shapes=[
            pltpu.VMEM((group * BLK, latent_dim), BF16),
            pltpu.VMEM((group * BLK, bins), BF16),
        ],
        compiler_params=pltpu.CompilerParams(vmem_limit_bytes=12 * MIB + 6 * piece_bytes),
        cost_estimate=pl.CostEstimate(
            flops=6 * entries * BLK * latent_dim * bins, bytes_accessed=8 * 2**20, transcendentals=0
        ),
        name="session",
    )(
        ids,
        mask,
        smoothed,
        recorded.reshape(entries, BLK, bins),
        *packed,
        late_theirs,
        *pieces,
    )

    got = flip(terms, 1)
    narrow = jax.ShapeDtypeStruct((chunk, latent_dim), BF16)
    sent = pl.pallas_call(
        functools.partial(merge_late_kernel, entries, late),
        out_shape=narrow,
        in_specs=[smem] * 2 + [VMEM] * 2,
        out_specs=VMEM,
        scratch_shapes=[pltpu.VMEM((chunk, latent_dim), F32)],
        compiler_params=pltpu.CompilerParams(vmem_limit_bytes=4 * MIB + 3 * piece_bytes),
        cost_estimate=pl.CostEstimate(flops=0, bytes_accessed=2**20, transcendentals=0),
        name="merge_late",
    )(ids, asked, terms, got)
    back = flip(sent, 2)
    far_side = permute(far_side, odd_even)
    wide = jax.ShapeDtypeStruct((chunk, latent_dim), F32)
    merged = pl.pallas_call(
        functools.partial(merge_kernel, entries, late),
        out_shape=(wide,) * chain + (narrow,) * (chain - 1),
        in_specs=[smem] * 2 + [VMEM] * 2,
        out_specs=(VMEM,) * (2 * chain - 1),
        scratch_shapes=[pltpu.VMEM(((chain - 1) * chunk, latent_dim), F32)],
        compiler_params=pltpu.CompilerParams(vmem_limit_bytes=4 * MIB + 6 * piece_bytes),
        cost_estimate=pl.CostEstimate(flops=0, bytes_accessed=5 * 2**20, transcendentals=0),
        name="merge",
    )(ids, asked, terms, got)
    merged = list(merged)
    far_side, *merged = lax.optimization_barrier((far_side, *merged))
    crossed = {r: merged[chain + r - (r > half)] for r in range(chain) if r != half}
    first = [r for r in range(half + 1, chain)]
    other = {r: flip(crossed[r], 2) for r in first}
    rest = [r for r in crossed if r not in first]
    back, *held = lax.optimization_barrier((back, *(crossed[r] for r in rest)))
    other[half] = back
    for r, part in zip(rest, held):
        other[r] = flip(part, 2)
    totals = [merged[r] + other[r].astype(F32) for r in range(chain)]
    rise = totals[half]
    for r in range(half - 1, -1, -1):
        rise = totals[r] + rotate(rise.astype(BF16), 1).astype(F32)
    loading_grad = rise
    if half > 1:
        fall = totals[half + 1]
        for r in range(half + 2, chain):
            fall = totals[r] + rotate(fall.astype(BF16), -1).astype(F32)
        loading_grad = loading_grad + rotate(fall.astype(BF16), -1).astype(F32)

    latent_grad = pl.pallas_call(
        unsmooth_kernel,
        out_shape=jax.ShapeDtypeStruct((latent_dim, bins), F32),
        in_specs=[VMEM] * 6 + [HBM],
        out_specs=VMEM,
        scratch_shapes=table_scratch,
        compiler_params=pltpu.CompilerParams(vmem_limit_bytes=16 * MIB),
        cost_estimate=pl.CostEstimate(flops=mxu, bytes_accessed=4 * 2**20, transcendentals=0),
        name="unsmooth",
    )(grad, got, far_side, *spectrum, table)
    return latent_grad, loading_grad


def solution(mesh):
    return jax.shard_map(
        local,
        mesh=mesh,
        in_specs=(
            P(None, ("groups", "tm")),
            P(),
            P(("groups", "tm"), None),
            P(None, None, None, ("groups", "tm")),
            P(("groups", "tm"), None, None),
            P(("groups", "tm"), None, None),
            P(None, None, ("groups", "tm")),
        ),
        out_specs=(P(None, ("groups", "tm")), P(("groups", "tm"), None)),
        check_vma=False,
    )
```

```python
import functools

import jax
import jax.numpy as jnp
import numpy as np
from jax import lax
from jax.experimental import pallas as pl
from jax.experimental.pallas import tpu as pltpu
from jax.sharding import PartitionSpec as P

BLK = 128
ROW = 4
MIB = 2**20
F32 = jnp.float32
BF16 = jnp.bfloat16
VMEM = pl.BlockSpec(memory_space=pltpu.VMEM)
HBM = pl.BlockSpec(memory_space=pltpu.HBM)


def split_const(a):
    high = a.astype(jnp.bfloat16)
    low = (a - high.astype(np.float64)).astype(jnp.bfloat16)
    return high, low


@functools.lru_cache(maxsize=None)
def dft_tables(size):
    t = np.arange(size)[:, None]
    g = np.arange(size)[None, :]
    half = size // 2
    angle = 2 * np.pi * ((t * g[:, :half]) % size) / size
    cos, sin = np.cos(angle), np.sin(angle)
    sin[:, 0] = 1 - 2 * (np.arange(size) % 2)
    real = np.concatenate([cos, sin], axis=1)
    angle = 2 * np.pi * ((t * (3 * g + 1)) % (3 * size)) / (3 * size)
    cos, sin = np.cos(angle), np.sin(angle)
    weight = np.full((size,), 2.0)
    weight[0] = weight[half] = 1.0
    scale = 1.0 / (3 * size)
    tables = [real, cos, sin, (real * weight).T * scale, cos.T * 2 * scale, sin.T * 2 * scale]
    return np.concatenate([part for table in tables for part in split_const(table)])


def parts(a):
    high = a.astype(BF16)
    return high, (a - high.astype(F32)).astype(BF16)


def times(a, tables, index):
    rows, size = a.shape
    high, low = parts(a)
    t_high = tables[2 * index * size : (2 * index + 1) * size]
    t_low = tables[(2 * index + 1) * size : (2 * index + 2) * size]
    out = jnp.dot(jnp.concatenate([high, low]), t_high, preferred_element_type=F32)
    return out[:rows] + out[rows:] + jnp.dot(high, t_low, preferred_element_type=F32)


ROOT = 0.75**0.5


def spectrum_of(thirds, tables):
    first, second, third = thirds
    rows = first.shape[0]
    base = times(first + second + third, tables, 0)
    y = jnp.concatenate([first - 0.5 * (second + third), ROOT * (third - second)])
    cos, sin = times(y, tables, 1), times(y, tables, 2)
    return base, cos[:rows] + sin[rows:], cos[rows:] - sin[:rows]


def filtered(signal, taps, sign, tables, wanted):
    (xb, xr, xi), (kb, kr, ki) = signal, taps
    rows, size = xb.shape
    half = size // 2
    first = lax.broadcasted_iota(jnp.int32, (rows, half), 1) == 0
    kc, ks = kb[:, :half], kb[:, half:]
    kc_s = jnp.where(first, ks, kc)
    ks_x = jnp.where(first, 0.0, ks) * sign
    xc, xs = xb[:, :half], xb[:, half:]
    base = times(jnp.concatenate([xc * kc + xs * ks_x, xs * kc_s - xc * ks_x], axis=1), tables, 3)
    ki = ki * sign
    z = jnp.concatenate([xr * kr + xi * ki, xi * kr - xr * ki])
    cos, sin = times(z, tables, 4), times(z, tables, 5)
    vr, vi = cos[:rows] - sin[rows:], sin[:rows] + cos[rows:]
    each = (base + vr, base - 0.5 * vr - ROOT * vi, base - 0.5 * vr + ROOT * vi)
    return jnp.concatenate([each[m] for m in wanted], axis=1)


def thirds_of(mid, core_side, far_side):
    width = core_side.shape[1]
    size = 2 * width
    even = lax.rem(lax.axis_index("tm"), 2) == 0
    low, high = jnp.where(even, far_side, core_side), jnp.where(even, core_side, far_side)
    last = mid.shape[1] - width
    return (
        jnp.concatenate([low, mid[:, :width]], axis=1),
        mid[:, width : width + size],
        jnp.concatenate([mid[:, last:], high], axis=1),
    )


def smooth_kernel(mid, core_side, far_side, taps, table, out, *refs):
    spectrum, held, sem = refs[:3], refs[3], refs[4]
    copy = pltpu.make_async_copy(table, held, sem)
    copy.start()
    thirds = thirds_of(mid[...], core_side[...], far_side[...])
    copy.wait()
    base = times(taps[...], held, 0)
    kr, ki = times(taps[...], held, 1), -times(taps[...], held, 2)
    for ref, value in zip(spectrum, (base, kr, ki)):
        ref[...] = value
    signal = spectrum_of(thirds, held)
    out[...] = filtered(signal, (base, kr, ki), 1.0, held, (0, 1)).astype(out.dtype)


def unsmooth_kernel(mid, got, back, rise, fall, base, kr, ki, table, out, held, sem):
    copy = pltpu.make_async_copy(table, held, sem)
    copy.start()
    rows = mid.shape[0]
    width = got.shape[1] // 2
    me = lax.axis_index("tm")
    count = lax.axis_size("tm")
    first = got.shape[0] - 2 * rows
    core = got[first : first + rows]
    near, below, above = (ref[ref.shape[0] - rows :] for ref in (back, rise, fall))
    equal = (me >> 1) & 1 == me & 1
    far = jnp.where(equal, jnp.where(me & 1 == 0, below, above), near).astype(F32)
    far = jnp.where(jnp.logical_or(me == 0, me == count - 1), 0.0, far)
    core = core.astype(F32)
    thirds = thirds_of(
        mid[...], core[:, :width] + core[:, width:], far[:, :width] + far[:, width:]
    )
    copy.wait()
    signal = spectrum_of(thirds, held)
    out[...] = filtered(signal, (base[...], kr[...], ki[...]), -1.0, held, (1, 2))


def divide(a, n):
    return a >> (n.bit_length() - 1) if n & (n - 1) == 0 else a // n


def remainder(a, n):
    return a & (n - 1) if n & (n - 1) == 0 else a % n


def place_of(ids, e, me, blocks, forward):
    chain = lax.axis_size("tm") // ROW
    top = ids.shape[1]
    code = ids[divide(e, top), remainder(e, top)]
    owner, slot = divide(code, blocks), remainder(code, blocks)
    step = divide(owner, ROW) - divide(me, ROW)
    step = step if forward else -step
    turn = jnp.where(step < 0, step + chain, step)
    differ = owner ^ me
    piece = jnp.where(differ & 2 == 0, 0, chain) + turn
    return differ & 1 == 0, piece, pl.multiple_of(slot * BLK, BLK)


def pick(refs, index, act):
    if len(refs) == 1:
        act(refs[0])
        return
    half = len(refs) // 2
    lax.cond(
        index < half,
        lambda: pick(refs[:half], index, act),
        lambda: pick(refs[half:], index - half, act),
    )


def pack_kernel(first, entries, late, asked, *refs):
    pieces, out = refs[:-1], refs[-1]
    blocks = pieces[0].shape[0] // BLK
    me = lax.axis_index("tm")

    def body(e, _):
        core, piece, row = place_of(asked, first + e, me, blocks, False)
        target = pl.ds(pl.multiple_of(e * BLK, BLK), BLK)

        @pl.when(jnp.logical_and(core, piece != late))
        def _():
            def act(ref):
                out[target] = ref[pl.ds(row, BLK)]

            pick(pieces, jnp.where(piece < late, piece, piece - 1), act)

        return 0

    lax.fori_loop(0, entries, body, 0)


def session_kernel(
    entries, group, late, ids, mask, smoothed, recorded, packed, packed_rest, late_theirs, *refs
):
    pieces = refs[:-4]
    grad, terms, rows, resid = refs[-4:]
    blocks = pieces[0].shape[0] // BLK
    bins = smoothed.shape[1]
    top = ids.shape[1]
    me = lax.axis_index("tm")
    grad[...] = jnp.zeros_like(grad)
    depth = group * BLK

    def step(g, _):
        for i in range(group):
            e = g * group + i
            core, piece, row = place_of(ids, e, me, blocks, False)

            def own():
                def act(ref):
                    rows[i * BLK : (i + 1) * BLK] = ref[pl.ds(row, BLK)]

                pick(pieces, piece, act)

            def other():
                @pl.when(piece == late)
                def _():
                    rows[i * BLK : (i + 1) * BLK] = late_theirs[pl.ds(row, BLK)]

                @pl.when(piece != late)
                def _():
                    def act(ref):
                        source = pl.ds(pl.multiple_of(remainder(e, entries // 2) * BLK, BLK), BLK)
                        rows[i * BLK : (i + 1) * BLK] = ref[source]

                    pick((packed, packed_rest), divide(e, entries // 2), act)

            lax.cond(core, own, other)
        block = rows[...]
        predicted = jnp.dot(block, smoothed[...], preferred_element_type=F32)
        for i in range(group):
            e = g * group + i
            for t in range(bins // BLK):
                cut = slice(t * BLK, (t + 1) * BLK)
                weight = mask[divide(e, top), t, remainder(e, top)].astype(F32)
                part = predicted[i * BLK : (i + 1) * BLK, cut]
                seen = recorded[e, :, cut].astype(F32)
                resid[i * BLK : (i + 1) * BLK, cut] = (weight * (part - seen)).astype(BF16)
        term = lax.dot_general(
            resid[...], smoothed[...], (((1,), (1,)), ((), ())), preferred_element_type=F32
        )
        target = pl.ds(pl.multiple_of(g * depth, depth), depth)
        terms[target] = (term * (1.0 / BLK)).astype(BF16)
        grad[...] += lax.dot_general(
            block, resid[...], (((0,), (0,)), ((), ())), preferred_element_type=F32
        ) * (1.0 / BLK)
        return 0

    lax.fori_loop(0, entries // group, step, 0)
    latent_dim, width = grad.shape[0], rows.shape[1] // 2
    even = me & 1 == 0
    later, earlier = grad[:, bins - width :], grad[:, :width]
    core_edge, far_edge = jnp.where(even, later, earlier), jnp.where(even, earlier, later)
    for k, edge in enumerate((core_edge, far_edge)):
        target = pl.ds(entries * BLK + k * latent_dim, latent_dim)
        terms[target] = jnp.concatenate(parts(edge), axis=1)


def merge_late_kernel(entries, late, ids, asked, own, got, out, sums):
    chunk = sums.shape[0]
    blocks = chunk // BLK
    me = lax.axis_index("tm")
    sums[...] = jnp.zeros_like(sums)

    def add(e, _):
        source = pl.ds(pl.multiple_of(e * BLK, BLK), BLK)
        for names, terms in ((ids, own), (asked, got)):
            core, piece, row = place_of(names, e, me, blocks, True)

            @pl.when(jnp.logical_and(core, piece == late))
            def _():
                sums[pl.ds(row, BLK)] += terms[source].astype(F32)

        return 0

    lax.fori_loop(0, entries, add, 0)
    out[:chunk] = sums[...].astype(out.dtype)
    out[chunk:] = got[got.shape[0] - (out.shape[0] - chunk) :]


def merge_kernel(entries, late, ids, asked, own, got, *refs):
    chain = len(refs) // 2
    kept, outs, sums = refs[:chain], refs[chain:-1], refs[-1]
    chunk = kept[0].shape[0]
    me = lax.axis_index("tm")
    for ref in kept:
        ref[...] = jnp.zeros_like(ref)
    sums[...] = jnp.zeros_like(sums)

    def add(e, _):
        source = pl.ds(pl.multiple_of(e * BLK, BLK), BLK)
        for names, terms in ((ids, own), (asked, got)):
            core, piece, row = place_of(names, e, me, chunk // BLK, True)
            index = jnp.where(piece < late, piece - chain, piece - 1 - chain)

            @pl.when(jnp.logical_and(core, piece < chain))
            def _():
                def act(ref):
                    ref[pl.ds(row, BLK)] += terms[source].astype(F32)

                pick(kept, piece, act)

            @pl.when(jnp.logical_and(core, jnp.logical_and(piece >= chain, piece != late)))
            def _():
                sums[pl.ds(pl.multiple_of(index * chunk + row, BLK), BLK)] += terms[source].astype(F32)

        return 0

    lax.fori_loop(0, entries, add, 0)
    for q, out in enumerate(outs):
        out[...] = sums[q * chunk : (q + 1) * chunk].astype(out.dtype)


def hop_kernel(total, came, back, out):
    chunk = total.shape[0]
    out[:chunk] = (total[...] + came[:chunk].astype(F32)).astype(out.dtype)
    out[chunk:] = back[chunk:]


def local(latents, kernel, loadings, recorded, owner_ids, local_ids, recorded_mask):
    latent_dim, bins = latents.shape
    halfwidth = kernel.shape[1] // 2
    count = lax.axis_size("tm")
    chain = count // ROW
    chunk = loadings.shape[0]
    entries = owner_ids.size
    piece_bytes = count * chunk * latent_dim
    smem = pl.BlockSpec(memory_space=pltpu.SMEM)

    def permute(x, pairs):
        return lax.ppermute(x, "tm", pairs)

    def rotate(x, r):
        return permute(x, [(i, (i + r * ROW) % count) for i in range(count)])

    def flip(x, bit):
        return permute(x, [(i, i ^ bit) for i in range(count)])

    odd_even = [(i, i + 1) for i in range(1, count - 1, 2)]
    odd_even += [(target, source) for source, target in odd_even]

    ids = owner_ids[0] * (chunk // BLK) + local_ids[0]
    asked = flip(ids, 1)
    mask = jnp.transpose(recorded_mask, (0, 2, 1))

    even = lax.axis_index("tm") % 2 == 0
    later, earlier = latents[:, bins - halfwidth :], latents[:, :halfwidth]
    core_side = flip(jnp.where(even, later, earlier), 1)
    far_side = permute(jnp.where(even, earlier, later), odd_even)

    half = chain // 2
    late = chain + half
    straight = [loadings] * chain
    for r in range(1, half):
        straight[r] = rotate(straight[r - 1], 1)
        straight[-r] = rotate(straight[1 - r], -1)
    across = [flip(loadings, 2)] + [None] * (chain - 1)
    if half > 1:
        straight[1], across[0] = lax.optimization_barrier((straight[1], across[0]))
    straight[half] = rotate(straight[half - 1], 1)
    for r in range(1, chain):
        if r != half:
            across[r] = flip(straight[r], 2)

    table = dft_tables(2 * halfwidth)
    table_scratch = [pltpu.VMEM(table.shape, BF16), pltpu.SemaphoreType.DMA(())]
    mxu = 40 * 2 * latent_dim * (2 * halfwidth) ** 2
    square = jax.ShapeDtypeStruct((latent_dim, 2 * halfwidth), F32)
    smoothed, *spectrum = pl.pallas_call(
        smooth_kernel,
        out_shape=(jax.ShapeDtypeStruct((latent_dim, bins), BF16),) + (square,) * 3,
        in_specs=[VMEM] * 4 + [HBM],
        out_specs=(VMEM,) * 4,
        scratch_shapes=table_scratch,
        compiler_params=pltpu.CompilerParams(vmem_limit_bytes=16 * MIB),
        cost_estimate=pl.CostEstimate(flops=mxu, bytes_accessed=4 * 2**20, transcendentals=0),
        name="smooth",
    )(latents, core_side, far_side, kernel, table)

    slots = jax.ShapeDtypeStruct((entries * BLK, latent_dim), BF16)
    across[half] = flip(straight[half], 2)
    early = straight + across[:half] + across[half + 1 :]

    def pack(first, total):
        return pl.pallas_call(
            functools.partial(pack_kernel, first, total, late),
            out_shape=jax.ShapeDtypeStruct((total * BLK, latent_dim), BF16),
            in_specs=[smem] + [VMEM] * len(early),
            out_specs=VMEM,
            compiler_params=pltpu.CompilerParams(vmem_limit_bytes=4 * MIB + 3 * piece_bytes),
            cost_estimate=pl.CostEstimate(flops=0, bytes_accessed=2**20, transcendentals=0),
            name="pack",
        )(asked, *early)

    asked, smoothed, mask = lax.optimization_barrier((asked, smoothed, mask))
    packed = [flip(pack(first, entries // 2), 1) for first in (0, entries // 2)]
    last, smoothed = lax.optimization_barrier((across[half], smoothed))
    late_theirs = flip(last, 1)
    pieces = straight + across

    group = 4
    extended = jax.ShapeDtypeStruct((entries * BLK + 2 * latent_dim, latent_dim), BF16)
    grad, terms = pl.pallas_call(
        functools.partial(session_kernel, entries, group, late),
        out_shape=(
            jax.ShapeDtypeStruct((latent_dim, bins), F32),
            extended,
        ),
        in_specs=[smem] * 2 + [VMEM] * (5 + len(pieces)),
        out_specs=(VMEM,) * 2,
        scratch_shapes=[
            pltpu.VMEM((group * BLK, latent_dim), BF16),
            pltpu.VMEM((group * BLK, bins), BF16),
        ],
        compiler_params=pltpu.CompilerParams(vmem_limit_bytes=12 * MIB + 6 * piece_bytes),
        cost_estimate=pl.CostEstimate(
            flops=6 * entries * BLK * latent_dim * bins, bytes_accessed=8 * 2**20, transcendentals=0
        ),
        name="session",
    )(
        ids,
        mask,
        smoothed,
        recorded.reshape(entries, BLK, bins),
        *packed,
        late_theirs,
        *pieces,
    )

    got = flip(terms, 1)
    narrow = jax.ShapeDtypeStruct((chunk, latent_dim), BF16)
    sent = pl.pallas_call(
        functools.partial(merge_late_kernel, entries, late),
        out_shape=jax.ShapeDtypeStruct((chunk + latent_dim, latent_dim), BF16),
        in_specs=[smem] * 2 + [VMEM] * 2,
        out_specs=VMEM,
        scratch_shapes=[pltpu.VMEM((chunk, latent_dim), F32)],
        compiler_params=pltpu.CompilerParams(vmem_limit_bytes=4 * MIB + 3 * piece_bytes),
        cost_estimate=pl.CostEstimate(flops=0, bytes_accessed=2**20, transcendentals=0),
        name="merge_late",
    )(ids, asked, terms, got)
    wide = jax.ShapeDtypeStruct((chunk, latent_dim), F32)
    sent, ids = lax.optimization_barrier((sent, ids))
    back = flip(sent, 2)
    merged = pl.pallas_call(
        functools.partial(merge_kernel, entries, late),
        out_shape=(wide,) * chain + (narrow,) * (chain - 1),
        in_specs=[smem] * 2 + [VMEM] * 2,
        out_specs=(VMEM,) * (2 * chain - 1),
        scratch_shapes=[pltpu.VMEM(((chain - 1) * chunk, latent_dim), F32)],
        compiler_params=pltpu.CompilerParams(vmem_limit_bytes=4 * MIB + 6 * piece_bytes),
        cost_estimate=pl.CostEstimate(flops=0, bytes_accessed=5 * 2**20, transcendentals=0),
        name="merge",
    )(ids, asked, terms, got)
    crossed = {r: merged[chain + r - (r > half)] for r in range(chain) if r != half}
    other = {r: flip(part, 2) for r, part in crossed.items()}

    def hop(total, came):
        return pl.pallas_call(
            hop_kernel,
            out_shape=jax.ShapeDtypeStruct(back.shape, BF16),
            in_specs=[VMEM] * 3,
            out_specs=VMEM,
            compiler_params=pltpu.CompilerParams(vmem_limit_bytes=8 * MIB),
            cost_estimate=pl.CostEstimate(flops=2 * 10**9, bytes_accessed=MIB, transcendentals=0),
            name="hop",
        )(total, came, back)

    rise = hop(merged[half], back)
    totals = {r: merged[r] + other[r].astype(F32) for r in other}
    rise_side = rise = rotate(rise, 1)
    for r in range(half - 1, 0, -1):
        rise = rotate((totals[r] + rise[:chunk].astype(F32)).astype(BF16), 1)
    fall_side = fall = rotate(hop(merged[half + 1], other[half + 1]), -1)
    for r in range(half + 2, chain):
        fall = rotate((totals[r] + fall[:chunk].astype(F32)).astype(BF16), -1)
    loading_grad = totals[0] + rise[:chunk].astype(F32) + fall[:chunk].astype(F32)

    latent_grad = pl.pallas_call(
        unsmooth_kernel,
        out_shape=jax.ShapeDtypeStruct((latent_dim, bins), F32),
        in_specs=[VMEM] * 8 + [HBM],
        out_specs=VMEM,
        scratch_shapes=table_scratch,
        compiler_params=pltpu.CompilerParams(vmem_limit_bytes=16 * MIB),
        cost_estimate=pl.CostEstimate(flops=mxu, bytes_accessed=4 * 2**20, transcendentals=0),
        name="unsmooth",
    )(grad, got, back, rise_side, fall_side, *spectrum, table)
    return latent_grad, loading_grad


def solution(mesh):
    return jax.shard_map(
        local,
        mesh=mesh,
        in_specs=(
            P(None, ("groups", "tm")),
            P(),
            P(("groups", "tm"), None),
            P(None, None, None, ("groups", "tm")),
            P(("groups", "tm"), None, None),
            P(("groups", "tm"), None, None),
            P(None, None, ("groups", "tm")),
        ),
        out_specs=(P(None, ("groups", "tm")), P(("groups", "tm"), None)),
        check_vma=False,
    )
```

```python
import functools

import jax
import jax.numpy as jnp
import numpy as np
from jax import lax
from jax.experimental import pallas as pl
from jax.experimental.pallas import tpu as pltpu
from jax.sharding import PartitionSpec as P

BLK = 128
ROW = 4
MIB = 2**20
F32 = jnp.float32
BF16 = jnp.bfloat16
VMEM = pl.BlockSpec(memory_space=pltpu.VMEM)
HBM = pl.BlockSpec(memory_space=pltpu.HBM)


def split_const(a):
    high = a.astype(jnp.bfloat16)
    low = (a - high.astype(np.float64)).astype(jnp.bfloat16)
    return high, low


@functools.lru_cache(maxsize=None)
def dft_tables(size):
    t = np.arange(size)[:, None]
    g = np.arange(size)[None, :]
    half = size // 2
    angle = 2 * np.pi * ((t * g[:, :half]) % size) / size
    cos, sin = np.cos(angle), np.sin(angle)
    sin[:, 0] = 1 - 2 * (np.arange(size) % 2)
    real = np.concatenate([cos, sin], axis=1)
    angle = 2 * np.pi * ((t * (3 * g + 1)) % (3 * size)) / (3 * size)
    cos, sin = np.cos(angle), np.sin(angle)
    weight = np.full((size,), 2.0)
    weight[0] = weight[half] = 1.0
    scale = 1.0 / (3 * size)
    tables = [real, cos, sin, (real * weight).T * scale, cos.T * 2 * scale, sin.T * 2 * scale]
    return np.concatenate([part for table in tables for part in split_const(table)])


def parts(a):
    high = a.astype(BF16)
    return high, (a - high.astype(F32)).astype(BF16)


def times(a, tables, index):
    rows, size = a.shape
    high, low = parts(a)
    t_high = tables[2 * index * size : (2 * index + 1) * size]
    t_low = tables[(2 * index + 1) * size : (2 * index + 2) * size]
    out = jnp.dot(jnp.concatenate([high, low]), t_high, preferred_element_type=F32)
    return out[:rows] + out[rows:] + jnp.dot(high, t_low, preferred_element_type=F32)


ROOT = 0.75**0.5


def spectrum_of(thirds, tables):
    first, second, third = thirds
    rows = first.shape[0]
    base = times(first + second + third, tables, 0)
    y = jnp.concatenate([first - 0.5 * (second + third), ROOT * (third - second)])
    cos, sin = times(y, tables, 1), times(y, tables, 2)
    return base, cos[:rows] + sin[rows:], cos[rows:] - sin[:rows]


def filtered(signal, taps, sign, tables, wanted):
    (xb, xr, xi), (kb, kr, ki) = signal, taps
    rows, size = xb.shape
    half = size // 2
    first = lax.broadcasted_iota(jnp.int32, (rows, half), 1) == 0
    kc, ks = kb[:, :half], kb[:, half:]
    kc_s = jnp.where(first, ks, kc)
    ks_x = jnp.where(first, 0.0, ks) * sign
    xc, xs = xb[:, :half], xb[:, half:]
    base = times(jnp.concatenate([xc * kc + xs * ks_x, xs * kc_s - xc * ks_x], axis=1), tables, 3)
    ki = ki * sign
    z = jnp.concatenate([xr * kr + xi * ki, xi * kr - xr * ki])
    cos, sin = times(z, tables, 4), times(z, tables, 5)
    vr, vi = cos[:rows] - sin[rows:], sin[:rows] + cos[rows:]
    each = (base + vr, base - 0.5 * vr - ROOT * vi, base - 0.5 * vr + ROOT * vi)
    return jnp.concatenate([each[m] for m in wanted], axis=1)


def thirds_of(mid, core_side, far_side):
    width = core_side.shape[1]
    size = 2 * width
    even = lax.rem(lax.axis_index("tm"), 2) == 0
    low, high = jnp.where(even, far_side, core_side), jnp.where(even, core_side, far_side)
    last = mid.shape[1] - width
    return (
        jnp.concatenate([low, mid[:, :width]], axis=1),
        mid[:, width : width + size],
        jnp.concatenate([mid[:, last:], high], axis=1),
    )


def smooth_kernel(mid, core_side, far_side, taps, table, out, *refs):
    spectrum, held, sem = refs[:3], refs[3], refs[4]
    copy = pltpu.make_async_copy(table, held, sem)
    copy.start()
    thirds = thirds_of(mid[...], core_side[...], far_side[...])
    copy.wait()
    base = times(taps[...], held, 0)
    kr, ki = times(taps[...], held, 1), -times(taps[...], held, 2)
    for ref, value in zip(spectrum, (base, kr, ki)):
        ref[...] = value
    signal = spectrum_of(thirds, held)
    out[...] = filtered(signal, (base, kr, ki), 1.0, held, (0, 1)).astype(out.dtype)


def unsmooth_kernel(mid, got, far_side, base, kr, ki, table, out, held, sem):
    copy = pltpu.make_async_copy(table, held, sem)
    copy.start()
    width = far_side.shape[1] // 2
    core = got[got.shape[0] - far_side.shape[0] :].astype(F32)
    far = far_side[...].astype(F32)
    thirds = thirds_of(
        mid[...], core[:, :width] + core[:, width:], far[:, :width] + far[:, width:]
    )
    copy.wait()
    signal = spectrum_of(thirds, held)
    out[...] = filtered(signal, (base[...], kr[...], ki[...]), -1.0, held, (1, 2))


def divide(a, n):
    return a >> (n.bit_length() - 1) if n & (n - 1) == 0 else a // n


def remainder(a, n):
    return a & (n - 1) if n & (n - 1) == 0 else a % n


def place_of(ids, e, me, blocks, forward):
    chain = lax.axis_size("tm") // ROW
    top = ids.shape[1]
    code = ids[divide(e, top), remainder(e, top)]
    owner, slot = divide(code, blocks), remainder(code, blocks)
    step = divide(owner, ROW) - divide(me, ROW)
    step = step if forward else -step
    turn = jnp.where(step < 0, step + chain, step)
    differ = owner ^ me
    piece = jnp.where(differ & 2 == 0, 0, chain) + turn
    return differ & 1 == 0, piece, pl.multiple_of(slot * BLK, BLK)


def pick(refs, index, act):
    if len(refs) == 1:
        act(refs[0])
        return
    half = len(refs) // 2
    lax.cond(
        index < half,
        lambda: pick(refs[:half], index, act),
        lambda: pick(refs[half:], index - half, act),
    )


def pack_kernel(first, entries, late, asked, *refs):
    pieces, out = refs[:-1], refs[-1]
    blocks = pieces[0].shape[0] // BLK
    me = lax.axis_index("tm")

    def body(e, _):
        core, piece, row = place_of(asked, first + e, me, blocks, False)
        target = pl.ds(pl.multiple_of(e * BLK, BLK), BLK)

        @pl.when(jnp.logical_and(core, piece != late))
        def _():
            def act(ref):
                out[target] = ref[pl.ds(row, BLK)]

            pick(pieces, jnp.where(piece < late, piece, piece - 1), act)

        return 0

    lax.fori_loop(0, entries, body, 0)


def session_kernel(
    entries, group, late, ids, mask, smoothed, recorded, packed, packed_rest, late_theirs, *refs
):
    pieces = refs[:-5]
    grad, far_side, terms, rows, resid = refs[-5:]
    blocks = pieces[0].shape[0] // BLK
    bins = smoothed.shape[1]
    top = ids.shape[1]
    me = lax.axis_index("tm")
    grad[...] = jnp.zeros_like(grad)
    depth = group * BLK

    def step(g, _):
        for i in range(group):
            e = g * group + i
            core, piece, row = place_of(ids, e, me, blocks, False)

            def own():
                def act(ref):
                    rows[i * BLK : (i + 1) * BLK] = ref[pl.ds(row, BLK)]

                pick(pieces, piece, act)

            def other():
                @pl.when(piece == late)
                def _():
                    rows[i * BLK : (i + 1) * BLK] = late_theirs[pl.ds(row, BLK)]

                @pl.when(piece != late)
                def _():
                    def act(ref):
                        source = pl.ds(pl.multiple_of(remainder(e, entries // 2) * BLK, BLK), BLK)
                        rows[i * BLK : (i + 1) * BLK] = ref[source]

                    pick((packed, packed_rest), divide(e, entries // 2), act)

            lax.cond(core, own, other)
        block = rows[...]
        predicted = jnp.dot(block, smoothed[...], preferred_element_type=F32)
        for i in range(group):
            e = g * group + i
            for t in range(bins // BLK):
                cut = slice(t * BLK, (t + 1) * BLK)
                weight = mask[divide(e, top), t, remainder(e, top)].astype(F32)
                part = predicted[i * BLK : (i + 1) * BLK, cut]
                seen = recorded[e, :, cut].astype(F32)
                resid[i * BLK : (i + 1) * BLK, cut] = (weight * (part - seen)).astype(BF16)
        term = lax.dot_general(
            resid[...], smoothed[...], (((1,), (1,)), ((), ())), preferred_element_type=F32
        )
        target = pl.ds(pl.multiple_of(g * depth, depth), depth)
        terms[target] = (term * (1.0 / BLK)).astype(BF16)
        grad[...] += lax.dot_general(
            block, resid[...], (((0,), (0,)), ((), ())), preferred_element_type=F32
        ) * (1.0 / BLK)
        return 0

    lax.fori_loop(0, entries // group, step, 0)
    latent_dim, width = grad.shape[0], rows.shape[1] // 2
    even = me & 1 == 0
    later, earlier = grad[:, bins - width :], grad[:, :width]
    core_edge, far_edge = jnp.where(even, later, earlier), jnp.where(even, earlier, later)
    terms[pl.ds(entries * BLK, latent_dim)] = jnp.concatenate(parts(core_edge), axis=1)
    far_side[...] = jnp.concatenate(parts(far_edge), axis=1)


def merge_late_kernel(entries, late, ids, asked, own, got, out, sums):
    blocks = out.shape[0] // BLK
    me = lax.axis_index("tm")
    sums[...] = jnp.zeros_like(sums)

    def add(e, _):
        source = pl.ds(pl.multiple_of(e * BLK, BLK), BLK)
        for names, terms in ((ids, own), (asked, got)):
            core, piece, row = place_of(names, e, me, blocks, True)

            @pl.when(jnp.logical_and(core, piece == late))
            def _():
                sums[pl.ds(row, BLK)] += terms[source].astype(F32)

        return 0

    lax.fori_loop(0, entries, add, 0)
    out[...] = sums[...].astype(out.dtype)


def merge_kernel(entries, late, ids, asked, own, got, *refs):
    chain = len(refs) // 2
    kept, outs, sums = refs[:chain], refs[chain:-1], refs[-1]
    chunk = kept[0].shape[0]
    me = lax.axis_index("tm")
    for ref in kept:
        ref[...] = jnp.zeros_like(ref)
    sums[...] = jnp.zeros_like(sums)

    def add(e, _):
        source = pl.ds(pl.multiple_of(e * BLK, BLK), BLK)
        for names, terms in ((ids, own), (asked, got)):
            core, piece, row = place_of(names, e, me, chunk // BLK, True)
            index = jnp.where(piece < late, piece - chain, piece - 1 - chain)

            @pl.when(jnp.logical_and(core, piece < chain))
            def _():
                def act(ref):
                    ref[pl.ds(row, BLK)] += terms[source].astype(F32)

                pick(kept, piece, act)

            @pl.when(jnp.logical_and(core, jnp.logical_and(piece >= chain, piece != late)))
            def _():
                sums[pl.ds(pl.multiple_of(index * chunk + row, BLK), BLK)] += terms[source].astype(F32)

        return 0

    lax.fori_loop(0, entries, add, 0)
    for q, out in enumerate(outs):
        out[...] = sums[q * chunk : (q + 1) * chunk].astype(out.dtype)


def hop_kernel(total, *refs):
    out = refs[-1]
    value = total[...]
    for came in refs[:-1]:
        value += came[...].astype(F32)
    out[...] = value.astype(out.dtype)


def local(latents, kernel, loadings, recorded, owner_ids, local_ids, recorded_mask):
    latent_dim, bins = latents.shape
    halfwidth = kernel.shape[1] // 2
    count = lax.axis_size("tm")
    chain = count // ROW
    chunk = loadings.shape[0]
    entries = owner_ids.size
    piece_bytes = count * chunk * latent_dim
    smem = pl.BlockSpec(memory_space=pltpu.SMEM)

    def permute(x, pairs):
        return lax.ppermute(x, "tm", pairs)

    def rotate(x, r):
        return permute(x, [(i, (i + r * ROW) % count) for i in range(count)])

    def flip(x, bit):
        return permute(x, [(i, i ^ bit) for i in range(count)])

    odd_even = [(i, i + 1) for i in range(1, count - 1, 2)]
    odd_even += [(target, source) for source, target in odd_even]

    ids = owner_ids[0] * (chunk // BLK) + local_ids[0]
    asked = flip(ids, 1)
    mask = jnp.transpose(recorded_mask, (0, 2, 1))

    even = lax.axis_index("tm") % 2 == 0
    later, earlier = latents[:, bins - halfwidth :], latents[:, :halfwidth]
    core_side = flip(jnp.where(even, later, earlier), 1)
    far_side = permute(jnp.where(even, earlier, later), odd_even)

    half = chain // 2
    late = chain + half
    straight = [loadings] * chain
    for r in range(1, half):
        straight[r] = rotate(straight[r - 1], 1)
        straight[-r] = rotate(straight[1 - r], -1)
    across = [flip(loadings, 2)] + [None] * (chain - 1)
    if half > 1:
        straight[1], across[0] = lax.optimization_barrier((straight[1], across[0]))
    straight[half] = rotate(straight[half - 1], 1)
    for r in range(1, chain):
        if r != half:
            across[r] = flip(straight[r], 2)

    table = dft_tables(2 * halfwidth)
    table_scratch = [pltpu.VMEM(table.shape, BF16), pltpu.SemaphoreType.DMA(())]
    mxu = 40 * 2 * latent_dim * (2 * halfwidth) ** 2
    square = jax.ShapeDtypeStruct((latent_dim, 2 * halfwidth), F32)
    smoothed, *spectrum = pl.pallas_call(
        smooth_kernel,
        out_shape=(jax.ShapeDtypeStruct((latent_dim, bins), BF16),) + (square,) * 3,
        in_specs=[VMEM] * 4 + [HBM],
        out_specs=(VMEM,) * 4,
        scratch_shapes=table_scratch,
        compiler_params=pltpu.CompilerParams(vmem_limit_bytes=52 * MIB),
        cost_estimate=pl.CostEstimate(flops=mxu, bytes_accessed=4 * 2**20, transcendentals=0),
        name="smooth",
    )(latents, core_side, far_side, kernel, table)

    slots = jax.ShapeDtypeStruct((entries * BLK, latent_dim), BF16)
    across[half] = flip(straight[half], 2)
    early = straight + across[:half] + across[half + 1 :]

    def pack(first, total):
        return pl.pallas_call(
            functools.partial(pack_kernel, first, total, late),
            out_shape=jax.ShapeDtypeStruct((total * BLK, latent_dim), BF16),
            in_specs=[smem] + [VMEM] * len(early),
            out_specs=VMEM,
            compiler_params=pltpu.CompilerParams(vmem_limit_bytes=4 * MIB + 3 * piece_bytes),
            cost_estimate=pl.CostEstimate(flops=0, bytes_accessed=2**20, transcendentals=0),
            name="pack",
        )(asked, *early)

    asked, smoothed, mask = lax.optimization_barrier((asked, smoothed, mask))
    packed = [flip(pack(first, entries // 2), 1) for first in (0, entries // 2)]
    last, smoothed = lax.optimization_barrier((across[half], smoothed))
    late_theirs = flip(last, 1)
    pieces = straight + across

    group = 4
    extended = jax.ShapeDtypeStruct((entries * BLK + latent_dim, latent_dim), BF16)
    grad, far_side, terms = pl.pallas_call(
        functools.partial(session_kernel, entries, group, late),
        out_shape=(
            jax.ShapeDtypeStruct((latent_dim, bins), F32),
            jax.ShapeDtypeStruct((latent_dim, 2 * halfwidth), BF16),
            extended,
        ),
        in_specs=[smem] * 2 + [VMEM] * (5 + len(pieces)),
        out_specs=(VMEM,) * 3,
        scratch_shapes=[
            pltpu.VMEM((group * BLK, latent_dim), BF16),
            pltpu.VMEM((group * BLK, bins), BF16),
        ],
        compiler_params=pltpu.CompilerParams(vmem_limit_bytes=12 * MIB + 6 * piece_bytes),
        cost_estimate=pl.CostEstimate(
            flops=6 * entries * BLK * latent_dim * bins, bytes_accessed=8 * 2**20, transcendentals=0
        ),
        name="session",
    )(
        ids,
        mask,
        smoothed,
        recorded.reshape(entries, BLK, bins),
        *packed,
        late_theirs,
        *pieces,
    )

    got = flip(terms, 1)
    narrow = jax.ShapeDtypeStruct((chunk, latent_dim), BF16)
    sent = pl.pallas_call(
        functools.partial(merge_late_kernel, entries, late),
        out_shape=narrow,
        in_specs=[smem] * 2 + [VMEM] * 2,
        out_specs=VMEM,
        scratch_shapes=[pltpu.VMEM((chunk, latent_dim), F32)],
        compiler_params=pltpu.CompilerParams(vmem_limit_bytes=4 * MIB + 3 * piece_bytes),
        cost_estimate=pl.CostEstimate(flops=0, bytes_accessed=2**20, transcendentals=0),
        name="merge_late",
    )(ids, asked, terms, got)
    wide = jax.ShapeDtypeStruct((chunk, latent_dim), F32)
    sent, ids = lax.optimization_barrier((sent, ids))
    back = flip(sent, 2)
    merged = pl.pallas_call(
        functools.partial(merge_kernel, entries, late),
        out_shape=(wide,) * chain + (narrow,) * (chain - 1),
        in_specs=[smem] * 2 + [VMEM] * 2,
        out_specs=(VMEM,) * (2 * chain - 1),
        scratch_shapes=[pltpu.VMEM(((chain - 1) * chunk, latent_dim), F32)],
        compiler_params=pltpu.CompilerParams(vmem_limit_bytes=4 * MIB + 6 * piece_bytes),
        cost_estimate=pl.CostEstimate(flops=0, bytes_accessed=5 * 2**20, transcendentals=0),
        name="merge",
    )(ids, asked, terms, got)
    crossed = {r: merged[chain + r - (r > half)] for r in range(chain) if r != half}
    other = {r: flip(part, 2) for r, part in crossed.items()}

    def hop(total, *came):
        return pl.pallas_call(
            hop_kernel,
            out_shape=narrow,
            in_specs=[VMEM] * (1 + len(came)),
            out_specs=VMEM,
            compiler_params=pltpu.CompilerParams(vmem_limit_bytes=8 * MIB),
            cost_estimate=pl.CostEstimate(flops=10**9, bytes_accessed=MIB, transcendentals=0),
            name="hop",
        )(total, *came)

    rise = hop(merged[half], back)
    rise, far_side = lax.optimization_barrier((rise, far_side))
    far_side = permute(far_side, odd_even)
    other[half + 1], far_side = lax.optimization_barrier((other[half + 1], far_side))
    rise = rotate(rise, 1)
    for r in range(half - 1, 0, -1):
        rise = rotate(hop(merged[r], other[r], rise), 1)
    fall = rotate(hop(merged[half + 1], other[half + 1]), -1)
    for r in range(half + 2, chain):
        fall = rotate(hop(merged[r], other[r], fall), -1)
    loading_grad = merged[0] + other[0].astype(F32) + rise.astype(F32) + fall.astype(F32)

    latent_grad = pl.pallas_call(
        unsmooth_kernel,
        out_shape=jax.ShapeDtypeStruct((latent_dim, bins), F32),
        in_specs=[VMEM] * 6 + [HBM],
        out_specs=VMEM,
        scratch_shapes=table_scratch,
        compiler_params=pltpu.CompilerParams(vmem_limit_bytes=16 * MIB),
        cost_estimate=pl.CostEstimate(flops=mxu, bytes_accessed=4 * 2**20, transcendentals=0),
        name="unsmooth",
    )(grad, got, far_side, *spectrum, table)
    return latent_grad, loading_grad


def solution(mesh):
    return jax.shard_map(
        local,
        mesh=mesh,
        in_specs=(
            P(None, ("groups", "tm")),
            P(),
            P(("groups", "tm"), None),
            P(None, None, None, ("groups", "tm")),
            P(("groups", "tm"), None, None),
            P(("groups", "tm"), None, None),
            P(None, None, ("groups", "tm")),
        ),
        out_specs=(P(None, ("groups", "tm")), P(("groups", "tm"), None)),
        check_vma=False,
    )
```

```python
import functools

import jax
import jax.numpy as jnp
import numpy as np
from jax import lax
from jax.experimental import pallas as pl
from jax.experimental.pallas import tpu as pltpu
from jax.sharding import PartitionSpec as P

BLK = 128
ROW = 4
MIB = 2**20
F32 = jnp.float32
BF16 = jnp.bfloat16
VMEM = pl.BlockSpec(memory_space=pltpu.VMEM)
HBM = pl.BlockSpec(memory_space=pltpu.HBM)


def split_const(a):
    high = a.astype(jnp.bfloat16)
    low = (a - high.astype(np.float64)).astype(jnp.bfloat16)
    return high, low


@functools.lru_cache(maxsize=None)
def dft_tables(size):
    t = np.arange(size)[:, None]
    g = np.arange(size)[None, :]
    half = size // 2
    angle = 2 * np.pi * ((t * g[:, :half]) % size) / size
    cos, sin = np.cos(angle), np.sin(angle)
    sin[:, 0] = 1 - 2 * (np.arange(size) % 2)
    real = np.concatenate([cos, sin], axis=1)
    angle = 2 * np.pi * ((t * (3 * g + 1)) % (3 * size)) / (3 * size)
    cos, sin = np.cos(angle), np.sin(angle)
    weight = np.full((size,), 2.0)
    weight[0] = weight[half] = 1.0
    scale = 1.0 / (3 * size)
    tables = [real, cos, sin, (real * weight).T * scale, cos.T * 2 * scale, sin.T * 2 * scale]
    return np.concatenate([part for table in tables for part in split_const(table)])


def parts(a):
    high = a.astype(BF16)
    return high, (a - high.astype(F32)).astype(BF16)


class Tables:
    def __init__(self, source, held, sem):
        count = sem.shape[0]
        rows = held.shape[0] // count
        self.held = held
        self.copies = [
            pltpu.make_async_copy(source.at[cut], held.at[cut], sem.at[i])
            for i, cut in enumerate(pl.ds(i * rows, rows) for i in range(count))
        ]
        for copy in self.copies:
            copy.start()
        self.here = set()

    def __getitem__(self, index):
        if index not in self.here:
            self.here.add(index)
            self.copies[index].wait()
        size = self.held.shape[1]
        first = 2 * index * size
        return self.held[first : first + size], self.held[first + size : first + 2 * size]


def times(a, tables, index):
    rows, size = a.shape
    high, low = parts(a)
    t_high, t_low = tables[index]
    out = jnp.dot(jnp.concatenate([high, low]), t_high, preferred_element_type=F32)
    return out[:rows] + out[rows:] + jnp.dot(high, t_low, preferred_element_type=F32)


ROOT = 0.75**0.5


def spectrum_of(thirds, tables):
    first, second, third = thirds
    rows = first.shape[0]
    base = times(first + second + third, tables, 0)
    y = jnp.concatenate([first - 0.5 * (second + third), ROOT * (third - second)])
    cos, sin = times(y, tables, 1), times(y, tables, 2)
    return base, cos[:rows] + sin[rows:], cos[rows:] - sin[:rows]


def filtered(signal, taps, sign, tables, wanted):
    (xb, xr, xi), (kb, kr, ki) = signal, taps
    rows, size = xb.shape
    half = size // 2
    first = lax.broadcasted_iota(jnp.int32, (rows, half), 1) == 0
    kc, ks = kb[:, :half], kb[:, half:]
    kc_s = jnp.where(first, ks, kc)
    ks_x = jnp.where(first, 0.0, ks) * sign
    xc, xs = xb[:, :half], xb[:, half:]
    base = times(jnp.concatenate([xc * kc + xs * ks_x, xs * kc_s - xc * ks_x], axis=1), tables, 3)
    ki = ki * sign
    z = jnp.concatenate([xr * kr + xi * ki, xi * kr - xr * ki])
    cos, sin = times(z, tables, 4), times(z, tables, 5)
    vr, vi = cos[:rows] - sin[rows:], sin[:rows] + cos[rows:]
    each = (base + vr, base - 0.5 * vr - ROOT * vi, base - 0.5 * vr + ROOT * vi)
    return jnp.concatenate([each[m] for m in wanted], axis=1)


def thirds_of(mid, core_side, far_side):
    width = core_side.shape[1]
    size = 2 * width
    even = lax.rem(lax.axis_index("tm"), 2) == 0
    low, high = jnp.where(even, far_side, core_side), jnp.where(even, core_side, far_side)
    last = mid.shape[1] - width
    return (
        jnp.concatenate([low, mid[:, :width]], axis=1),
        mid[:, width : width + size],
        jnp.concatenate([mid[:, last:], high], axis=1),
    )


def smooth_kernel(mid, core_side, far_side, taps, table, out, *refs):
    spectrum, held, sem = refs[:3], refs[3], refs[4]
    tables = Tables(table, held, sem)
    thirds = thirds_of(mid[...], core_side[...], far_side[...])
    base = times(taps[...], tables, 0)
    kr, ki = times(taps[...], tables, 1), -times(taps[...], tables, 2)
    for ref, value in zip(spectrum, (base, kr, ki)):
        ref[...] = value
    signal = spectrum_of(thirds, tables)
    out[...] = filtered(signal, (base, kr, ki), 1.0, tables, (0, 1)).astype(out.dtype)


def unsmooth_kernel(mid, got, far_side, base, kr, ki, table, out, held, sem):
    tables = Tables(table, held, sem)
    width = far_side.shape[1] // 2
    core = got[got.shape[0] - far_side.shape[0] :].astype(F32)
    far = far_side[...].astype(F32)
    thirds = thirds_of(
        mid[...], core[:, :width] + core[:, width:], far[:, :width] + far[:, width:]
    )
    signal = spectrum_of(thirds, tables)
    out[...] = filtered(signal, (base[...], kr[...], ki[...]), -1.0, tables, (1, 2))


def divide(a, n):
    return a >> (n.bit_length() - 1) if n & (n - 1) == 0 else a // n


def remainder(a, n):
    return a & (n - 1) if n & (n - 1) == 0 else a % n


def place_of(ids, e, me, blocks, forward):
    chain = lax.axis_size("tm") // ROW
    top = ids.shape[1]
    code = ids[divide(e, top), remainder(e, top)]
    owner, slot = divide(code, blocks), remainder(code, blocks)
    step = divide(owner, ROW) - divide(me, ROW)
    step = step if forward else -step
    turn = jnp.where(step < 0, step + chain, step)
    differ = owner ^ me
    piece = jnp.where(differ & 2 == 0, 0, chain) + turn
    return differ & 1 == 0, piece, pl.multiple_of(slot * BLK, BLK)


def pick(refs, index, act):
    if len(refs) == 1:
        act(refs[0])
        return
    half = len(refs) // 2
    lax.cond(
        index < half,
        lambda: pick(refs[:half], index, act),
        lambda: pick(refs[half:], index - half, act),
    )


def pack_kernel(first, entries, late, asked, *refs):
    pieces, out = refs[:-1], refs[-1]
    blocks = pieces[0].shape[0] // BLK
    me = lax.axis_index("tm")

    def body(e, _):
        core, piece, row = place_of(asked, first + e, me, blocks, False)
        target = pl.ds(pl.multiple_of(e * BLK, BLK), BLK)

        @pl.when(jnp.logical_and(core, piece != late))
        def _():
            def act(ref):
                out[target] = ref[pl.ds(row, BLK)]

            pick(pieces, jnp.where(piece < late, piece, piece - 1), act)

        return 0

    lax.fori_loop(0, entries, body, 0)


def session_kernel(
    entries, group, late, ids, mask, smoothed, recorded, packed, packed_rest, late_theirs, *refs
):
    pieces = refs[:-5]
    grad, far_side, terms, rows, resid = refs[-5:]
    blocks = pieces[0].shape[0] // BLK
    bins = smoothed.shape[1]
    top = ids.shape[1]
    me = lax.axis_index("tm")
    grad[...] = jnp.zeros_like(grad)
    depth = group * BLK

    def step(g, _):
        for i in range(group):
            e = g * group + i
            core, piece, row = place_of(ids, e, me, blocks, False)

            def own():
                def act(ref):
                    rows[i * BLK : (i + 1) * BLK] = ref[pl.ds(row, BLK)]

                pick(pieces, piece, act)

            def other():
                @pl.when(piece == late)
                def _():
                    rows[i * BLK : (i + 1) * BLK] = late_theirs[pl.ds(row, BLK)]

                @pl.when(piece != late)
                def _():
                    def act(ref):
                        source = pl.ds(pl.multiple_of(remainder(e, entries // 2) * BLK, BLK), BLK)
                        rows[i * BLK : (i + 1) * BLK] = ref[source]

                    pick((packed, packed_rest), divide(e, entries // 2), act)

            lax.cond(core, own, other)
        block = rows[...]
        predicted = jnp.dot(block, smoothed[...], preferred_element_type=F32)
        for i in range(group):
            e = g * group + i
            for t in range(bins // BLK):
                cut = slice(t * BLK, (t + 1) * BLK)
                weight = mask[divide(e, top), t, remainder(e, top)].astype(F32)
                part = predicted[i * BLK : (i + 1) * BLK, cut]
                seen = recorded[e, :, cut].astype(F32)
                resid[i * BLK : (i + 1) * BLK, cut] = (weight * (part - seen)).astype(BF16)
        term = lax.dot_general(
            resid[...], smoothed[...], (((1,), (1,)), ((), ())), preferred_element_type=F32
        )
        target = pl.ds(pl.multiple_of(g * depth, depth), depth)
        terms[target] = (term * (1.0 / BLK)).astype(BF16)
        grad[...] += lax.dot_general(
            block, resid[...], (((0,), (0,)), ((), ())), preferred_element_type=F32
        ) * (1.0 / BLK)
        return 0

    lax.fori_loop(0, entries // group, step, 0)
    latent_dim, width = grad.shape[0], rows.shape[1] // 2
    even = me & 1 == 0
    later, earlier = grad[:, bins - width :], grad[:, :width]
    core_edge, far_edge = jnp.where(even, later, earlier), jnp.where(even, earlier, later)
    terms[pl.ds(entries * BLK, latent_dim)] = jnp.concatenate(parts(core_edge), axis=1)
    far_side[...] = jnp.concatenate(parts(far_edge), axis=1)


def merge_late_kernel(entries, late, ids, asked, own, got, out, sums):
    blocks = out.shape[0] // BLK
    me = lax.axis_index("tm")
    sums[...] = jnp.zeros_like(sums)

    def add(e, _):
        source = pl.ds(pl.multiple_of(e * BLK, BLK), BLK)
        for names, terms in ((ids, own), (asked, got)):
            core, piece, row = place_of(names, e, me, blocks, True)

            @pl.when(jnp.logical_and(core, piece == late))
            def _():
                sums[pl.ds(row, BLK)] += terms[source].astype(F32)

        return 0

    lax.fori_loop(0, entries, add, 0)
    out[...] = sums[...].astype(out.dtype)


def merge_kernel(entries, late, ids, asked, own, got, *refs):
    chain = len(refs) // 2
    kept, outs, sums = refs[:chain], refs[chain:-1], refs[-1]
    chunk = kept[0].shape[0]
    me = lax.axis_index("tm")
    for ref in kept:
        ref[...] = jnp.zeros_like(ref)
    sums[...] = jnp.zeros_like(sums)

    def add(e, _):
        source = pl.ds(pl.multiple_of(e * BLK, BLK), BLK)
        for names, terms in ((ids, own), (asked, got)):
            core, piece, row = place_of(names, e, me, chunk // BLK, True)
            index = jnp.where(piece < late, piece - chain, piece - 1 - chain)

            @pl.when(jnp.logical_and(core, piece < chain))
            def _():
                def act(ref):
                    ref[pl.ds(row, BLK)] += terms[source].astype(F32)

                pick(kept, piece, act)

            @pl.when(jnp.logical_and(core, jnp.logical_and(piece >= chain, piece != late)))
            def _():
                sums[pl.ds(pl.multiple_of(index * chunk + row, BLK), BLK)] += terms[source].astype(F32)

        return 0

    lax.fori_loop(0, entries, add, 0)
    for q, out in enumerate(outs):
        out[...] = sums[q * chunk : (q + 1) * chunk].astype(out.dtype)


def hop_kernel(total, *refs):
    out = refs[-1]
    value = total[...]
    for came in refs[:-1]:
        value += came[...].astype(F32)
    out[...] = value.astype(out.dtype)


def local(latents, kernel, loadings, recorded, owner_ids, local_ids, recorded_mask):
    latent_dim, bins = latents.shape
    halfwidth = kernel.shape[1] // 2
    count = lax.axis_size("tm")
    chain = count // ROW
    chunk = loadings.shape[0]
    entries = owner_ids.size
    piece_bytes = count * chunk * latent_dim
    smem = pl.BlockSpec(memory_space=pltpu.SMEM)

    def permute(x, pairs):
        return lax.ppermute(x, "tm", pairs)

    def rotate(x, r):
        return permute(x, [(i, (i + r * ROW) % count) for i in range(count)])

    def flip(x, bit):
        return permute(x, [(i, i ^ bit) for i in range(count)])

    odd_even = [(i, i + 1) for i in range(1, count - 1, 2)]
    odd_even += [(target, source) for source, target in odd_even]

    ids = owner_ids[0] * (chunk // BLK) + local_ids[0]
    asked = flip(ids, 1)
    mask = jnp.transpose(recorded_mask, (0, 2, 1))

    even = lax.axis_index("tm") % 2 == 0
    later, earlier = latents[:, bins - halfwidth :], latents[:, :halfwidth]
    core_side = flip(jnp.where(even, later, earlier), 1)
    far_side = permute(jnp.where(even, earlier, later), odd_even)

    half = chain // 2
    late = chain + half
    straight = [loadings] * chain
    for r in range(1, half):
        straight[r] = rotate(straight[r - 1], 1)
        straight[-r] = rotate(straight[1 - r], -1)
    across = [flip(loadings, 2)] + [None] * (chain - 1)
    if half > 1:
        straight[1], across[0] = lax.optimization_barrier((straight[1], across[0]))
    straight[half] = rotate(straight[half - 1], 1)
    for r in range(1, chain):
        if r != half:
            across[r] = flip(straight[r], 2)

    table = dft_tables(2 * halfwidth)
    table_scratch = [pltpu.VMEM(table.shape, BF16), pltpu.SemaphoreType.DMA((6,))]
    mxu = 40 * 2 * latent_dim * (2 * halfwidth) ** 2
    square = jax.ShapeDtypeStruct((latent_dim, 2 * halfwidth), F32)
    smoothed, *spectrum = pl.pallas_call(
        smooth_kernel,
        out_shape=(jax.ShapeDtypeStruct((latent_dim, bins), BF16),) + (square,) * 3,
        in_specs=[VMEM] * 4 + [HBM],
        out_specs=(VMEM,) * 4,
        scratch_shapes=table_scratch,
        compiler_params=pltpu.CompilerParams(vmem_limit_bytes=53 * MIB),
        cost_estimate=pl.CostEstimate(flops=mxu, bytes_accessed=4 * 2**20, transcendentals=0),
        name="smooth",
    )(latents, core_side, far_side, kernel, table)

    slots = jax.ShapeDtypeStruct((entries * BLK, latent_dim), BF16)
    across[half] = flip(straight[half], 2)
    early = straight + across[:half] + across[half + 1 :]

    def pack(first, total):
        return pl.pallas_call(
            functools.partial(pack_kernel, first, total, late),
            out_shape=jax.ShapeDtypeStruct((total * BLK, latent_dim), BF16),
            in_specs=[smem] + [VMEM] * len(early),
            out_specs=VMEM,
            compiler_params=pltpu.CompilerParams(vmem_limit_bytes=4 * MIB + 3 * piece_bytes),
            cost_estimate=pl.CostEstimate(flops=0, bytes_accessed=2**20, transcendentals=0),
            name="pack",
        )(asked, *early)

    asked, smoothed, mask = lax.optimization_barrier((asked, smoothed, mask))
    packed = [flip(pack(first, entries // 2), 1) for first in (0, entries // 2)]
    last, smoothed = lax.optimization_barrier((across[half], smoothed))
    late_theirs = flip(last, 1)
    pieces = straight + across

    group = 4
    extended = jax.ShapeDtypeStruct((entries * BLK + latent_dim, latent_dim), BF16)
    grad, far_side, terms = pl.pallas_call(
        functools.partial(session_kernel, entries, group, late),
        out_shape=(
            jax.ShapeDtypeStruct((latent_dim, bins), F32),
            jax.ShapeDtypeStruct((latent_dim, 2 * halfwidth), BF16),
            extended,
        ),
        in_specs=[smem] * 2 + [VMEM] * (5 + len(pieces)),
        out_specs=(VMEM,) * 3,
        scratch_shapes=[
            pltpu.VMEM((group * BLK, latent_dim), BF16),
            pltpu.VMEM((group * BLK, bins), BF16),
        ],
        compiler_params=pltpu.CompilerParams(vmem_limit_bytes=12 * MIB + 6 * piece_bytes),
        cost_estimate=pl.CostEstimate(
            flops=6 * entries * BLK * latent_dim * bins, bytes_accessed=8 * 2**20, transcendentals=0
        ),
        name="session",
    )(
        ids,
        mask,
        smoothed,
        recorded.reshape(entries, BLK, bins),
        *packed,
        late_theirs,
        *pieces,
    )

    got = flip(terms, 1)
    narrow = jax.ShapeDtypeStruct((chunk, latent_dim), BF16)
    sent = pl.pallas_call(
        functools.partial(merge_late_kernel, entries, late),
        out_shape=narrow,
        in_specs=[smem] * 2 + [VMEM] * 2,
        out_specs=VMEM,
        scratch_shapes=[pltpu.VMEM((chunk, latent_dim), F32)],
        compiler_params=pltpu.CompilerParams(vmem_limit_bytes=4 * MIB + 3 * piece_bytes),
        cost_estimate=pl.CostEstimate(flops=0, bytes_accessed=2**20, transcendentals=0),
        name="merge_late",
    )(ids, asked, terms, got)
    wide = jax.ShapeDtypeStruct((chunk, latent_dim), F32)
    sent, ids = lax.optimization_barrier((sent, ids))
    back = flip(sent, 2)
    merged = pl.pallas_call(
        functools.partial(merge_kernel, entries, late),
        out_shape=(wide,) * chain + (narrow,) * (chain - 1),
        in_specs=[smem] * 2 + [VMEM] * 2,
        out_specs=(VMEM,) * (2 * chain - 1),
        scratch_shapes=[pltpu.VMEM(((chain - 1) * chunk, latent_dim), F32)],
        compiler_params=pltpu.CompilerParams(vmem_limit_bytes=4 * MIB + 6 * piece_bytes),
        cost_estimate=pl.CostEstimate(flops=0, bytes_accessed=5 * 2**20, transcendentals=0),
        name="merge",
    )(ids, asked, terms, got)
    crossed = {r: merged[chain + r - (r > half)] for r in range(chain) if r != half}
    other = {r: flip(part, 2) for r, part in crossed.items() if r}

    def hop(total, *came):
        return pl.pallas_call(
            hop_kernel,
            out_shape=narrow,
            in_specs=[VMEM] * (1 + len(came)),
            out_specs=VMEM,
            compiler_params=pltpu.CompilerParams(vmem_limit_bytes=8 * MIB),
            cost_estimate=pl.CostEstimate(flops=0, bytes_accessed=MIB, transcendentals=0),
            name="hop",
        )(total, *came)

    rise = hop(merged[half], back)
    rise, far_side = lax.optimization_barrier((rise, far_side))
    far_side = permute(far_side, odd_even)
    far_side, own = lax.optimization_barrier((far_side, crossed[0]))
    other[0] = flip(own, 2)
    rise = rotate(rise, 1)
    for r in range(half - 1, 0, -1):
        rise = rotate(hop(merged[r], other[r], rise), 1)
    fall = rotate(hop(merged[half + 1], other[half + 1]), -1)
    for r in range(half + 2, chain):
        fall = rotate(hop(merged[r], other[r], fall), -1)
    loading_grad = merged[0] + other[0].astype(F32) + rise.astype(F32) + fall.astype(F32)

    latent_grad = pl.pallas_call(
        unsmooth_kernel,
        out_shape=jax.ShapeDtypeStruct((latent_dim, bins), F32),
        in_specs=[VMEM] * 6 + [HBM],
        out_specs=VMEM,
        scratch_shapes=table_scratch,
        compiler_params=pltpu.CompilerParams(vmem_limit_bytes=16 * MIB),
        cost_estimate=pl.CostEstimate(flops=mxu, bytes_accessed=4 * 2**20, transcendentals=0),
        name="unsmooth",
    )(grad, got, far_side, *spectrum, table)
    return latent_grad, loading_grad


def solution(mesh):
    return jax.shard_map(
        local,
        mesh=mesh,
        in_specs=(
            P(None, ("groups", "tm")),
            P(),
            P(("groups", "tm"), None),
            P(None, None, None, ("groups", "tm")),
            P(("groups", "tm"), None, None),
            P(("groups", "tm"), None, None),
            P(None, None, ("groups", "tm")),
        ),
        out_specs=(P(None, ("groups", "tm")), P(("groups", "tm"), None)),
        check_vma=False,
    )
```

```python
import functools

import jax
import jax.numpy as jnp
import numpy as np
from jax import lax
from jax.experimental import pallas as pl
from jax.experimental.pallas import tpu as pltpu
from jax.sharding import PartitionSpec as P

BLK = 128
ROW = 4
MIB = 2**20
F32 = jnp.float32
BF16 = jnp.bfloat16
VMEM = pl.BlockSpec(memory_space=pltpu.VMEM)
HBM = pl.BlockSpec(memory_space=pltpu.HBM)


def split_const(a):
    high = a.astype(jnp.bfloat16)
    low = (a - high.astype(np.float64)).astype(jnp.bfloat16)
    return high, low


@functools.lru_cache(maxsize=None)
def dft_tables(size):
    t = np.arange(size)[:, None]
    g = np.arange(size)[None, :]
    half = size // 2
    angle = 2 * np.pi * ((t * g[:, :half]) % size) / size
    cos, sin = np.cos(angle), np.sin(angle)
    sin[:, 0] = 1 - 2 * (np.arange(size) % 2)
    real = np.concatenate([cos, sin], axis=1)
    angle = 2 * np.pi * ((t * (3 * g + 1)) % (3 * size)) / (3 * size)
    cos, sin = np.cos(angle), np.sin(angle)
    weight = np.full((size,), 2.0)
    weight[0] = weight[half] = 1.0
    scale = 1.0 / (3 * size)
    tables = [real, cos, sin, (real * weight).T * scale, cos.T * 2 * scale, sin.T * 2 * scale]
    return np.concatenate([part for table in tables for part in split_const(table)])


def parts(a):
    high = a.astype(BF16)
    return high, (a - high.astype(F32)).astype(BF16)


def times(a, tables, index):
    rows, size = a.shape
    high, low = parts(a)
    first = 2 * index * size
    t_high, t_low = tables[first : first + size], tables[first + size : first + 2 * size]
    out = jnp.dot(jnp.concatenate([high, low]), t_high, preferred_element_type=F32)
    return out[:rows] + out[rows:] + jnp.dot(high, t_low, preferred_element_type=F32)


ROOT = 0.75**0.5


def spectrum_of(thirds, tables):
    first, second, third = thirds
    rows = first.shape[0]
    base = times(first + second + third, tables, 0)
    y = jnp.concatenate([first - 0.5 * (second + third), ROOT * (third - second)])
    cos, sin = times(y, tables, 1), times(y, tables, 2)
    return base, cos[:rows] + sin[rows:], cos[rows:] - sin[:rows]


def filtered(signal, taps, sign, tables, wanted):
    (xb, xr, xi), (kb, kr, ki) = signal, taps
    rows, size = xb.shape
    half = size // 2
    first = lax.broadcasted_iota(jnp.int32, (rows, half), 1) == 0
    kc, ks = kb[:, :half], kb[:, half:]
    kc_s = jnp.where(first, ks, kc)
    ks_x = jnp.where(first, 0.0, ks) * sign
    xc, xs = xb[:, :half], xb[:, half:]
    base = times(jnp.concatenate([xc * kc + xs * ks_x, xs * kc_s - xc * ks_x], axis=1), tables, 3)
    ki = ki * sign
    z = jnp.concatenate([xr * kr + xi * ki, xi * kr - xr * ki])
    cos, sin = times(z, tables, 4), times(z, tables, 5)
    vr, vi = cos[:rows] - sin[rows:], sin[:rows] + cos[rows:]
    each = (base + vr, base - 0.5 * vr - ROOT * vi, base - 0.5 * vr + ROOT * vi)
    return jnp.concatenate([each[m] for m in wanted], axis=1)


def thirds_of(mid, core_side, far_side):
    width = core_side.shape[1]
    size = 2 * width
    even = lax.rem(lax.axis_index("tm"), 2) == 0
    low, high = jnp.where(even, far_side, core_side), jnp.where(even, core_side, far_side)
    last = mid.shape[1] - width
    return (
        jnp.concatenate([low, mid[:, :width]], axis=1),
        mid[:, width : width + size],
        jnp.concatenate([mid[:, last:], high], axis=1),
    )


def prepare_kernel(table, taps, mid, tables, bins, base, kr, ki, held, sem):
    rows = table.shape[0] // 6
    cuts = [pl.ds(i * rows, rows) for i in range(6)]
    copies = [pltpu.make_async_copy(taps, held, sem.at[0])]
    copies += [
        pltpu.make_async_copy(table.at[cut], tables.at[cut], sem.at[1 + i])
        for i, cut in enumerate(cuts)
    ]
    copies += [pltpu.make_async_copy(mid, bins, sem.at[7])]
    for copy in copies:
        copy.start()
    copies[0].wait()
    for i, (ref, sign) in enumerate(((base, 1.0), (kr, 1.0), (ki, -1.0))):
        copies[1 + i].wait()
        ref[...] = times(held[...], tables, i) * sign
    for copy in copies[4:]:
        copy.wait()


def smooth_kernel(mid, core_side, far_side, tables, base, kr, ki, out):
    thirds = thirds_of(mid[...], core_side[...], far_side[...])
    signal = spectrum_of(thirds, tables)
    taps = (base[...], kr[...], ki[...])
    out[...] = filtered(signal, taps, 1.0, tables, (0, 1)).astype(out.dtype)


def unsmooth_kernel(mid, got, far_side, tables, base, kr, ki, out):
    width = far_side.shape[1] // 2
    core = got[got.shape[0] - far_side.shape[0] :].astype(F32)
    far = far_side[...].astype(F32)
    thirds = thirds_of(
        mid[...], core[:, :width] + core[:, width:], far[:, :width] + far[:, width:]
    )
    signal = spectrum_of(thirds, tables)
    taps = (base[...], kr[...], ki[...])
    out[...] = filtered(signal, taps, -1.0, tables, (1, 2))


def divide(a, n):
    return a >> (n.bit_length() - 1) if n & (n - 1) == 0 else a // n


def remainder(a, n):
    return a & (n - 1) if n & (n - 1) == 0 else a % n


def place_of(ids, e, me, blocks, forward):
    chain = lax.axis_size("tm") // ROW
    top = ids.shape[1]
    code = ids[divide(e, top), remainder(e, top)]
    owner, slot = divide(code, blocks), remainder(code, blocks)
    step = divide(owner, ROW) - divide(me, ROW)
    step = step if forward else -step
    turn = jnp.where(step < 0, step + chain, step)
    differ = owner ^ me
    piece = jnp.where(differ & 2 == 0, 0, chain) + turn
    return differ & 1 == 0, piece, pl.multiple_of(slot * BLK, BLK)


def pick(refs, index, act):
    if len(refs) == 1:
        act(refs[0])
        return
    half = len(refs) // 2
    lax.cond(
        index < half,
        lambda: pick(refs[:half], index, act),
        lambda: pick(refs[half:], index - half, act),
    )


def pack_kernel(first, entries, late, asked, *refs):
    pieces, out = refs[:-1], refs[-1]
    blocks = pieces[0].shape[0] // BLK
    me = lax.axis_index("tm")

    def body(e, _):
        core, piece, row = place_of(asked, first + e, me, blocks, False)
        target = pl.ds(pl.multiple_of(e * BLK, BLK), BLK)

        @pl.when(jnp.logical_and(core, piece != late))
        def _():
            def act(ref):
                out[target] = ref[pl.ds(row, BLK)]

            pick(pieces, jnp.where(piece < late, piece, piece - 1), act)

        return 0

    lax.fori_loop(0, entries, body, 0)


def session_kernel(
    entries, group, late, ids, mask, smoothed, recorded, packed, packed_rest, late_theirs, *refs
):
    pieces = refs[:-5]
    grad, far_side, terms, rows, resid = refs[-5:]
    blocks = pieces[0].shape[0] // BLK
    bins = smoothed.shape[1]
    top = ids.shape[1]
    me = lax.axis_index("tm")
    grad[...] = jnp.zeros_like(grad)
    depth = group * BLK

    def step(g, _):
        for i in range(group):
            e = g * group + i
            core, piece, row = place_of(ids, e, me, blocks, False)

            def own():
                def act(ref):
                    rows[i * BLK : (i + 1) * BLK] = ref[pl.ds(row, BLK)]

                pick(pieces, piece, act)

            def other():
                @pl.when(piece == late)
                def _():
                    rows[i * BLK : (i + 1) * BLK] = late_theirs[pl.ds(row, BLK)]

                @pl.when(piece != late)
                def _():
                    def act(ref):
                        source = pl.ds(pl.multiple_of(remainder(e, entries // 2) * BLK, BLK), BLK)
                        rows[i * BLK : (i + 1) * BLK] = ref[source]

                    pick((packed, packed_rest), divide(e, entries // 2), act)

            lax.cond(core, own, other)
        block = rows[...]
        predicted = jnp.dot(block, smoothed[...], preferred_element_type=F32)
        for i in range(group):
            e = g * group + i
            for t in range(bins // BLK):
                cut = slice(t * BLK, (t + 1) * BLK)
                weight = mask[divide(e, top), t, remainder(e, top)].astype(F32)
                part = predicted[i * BLK : (i + 1) * BLK, cut]
                seen = recorded[e, :, cut].astype(F32)
                resid[i * BLK : (i + 1) * BLK, cut] = (weight * (part - seen)).astype(BF16)
        term = lax.dot_general(
            resid[...], smoothed[...], (((1,), (1,)), ((), ())), preferred_element_type=F32
        )
        target = pl.ds(pl.multiple_of(g * depth, depth), depth)
        terms[target] = (term * (1.0 / BLK)).astype(BF16)
        grad[...] += lax.dot_general(
            block, resid[...], (((0,), (0,)), ((), ())), preferred_element_type=F32
        ) * (1.0 / BLK)
        return 0

    lax.fori_loop(0, entries // group, step, 0)
    latent_dim, width = grad.shape[0], rows.shape[1] // 2
    even = me & 1 == 0
    later, earlier = grad[:, bins - width :], grad[:, :width]
    core_edge, far_edge = jnp.where(even, later, earlier), jnp.where(even, earlier, later)
    terms[pl.ds(entries * BLK, latent_dim)] = jnp.concatenate(parts(core_edge), axis=1)
    far_side[...] = jnp.concatenate(parts(far_edge), axis=1)


def merge_late_kernel(entries, late, ids, asked, own, got, out, sums):
    blocks = out.shape[0] // BLK
    me = lax.axis_index("tm")
    sums[...] = jnp.zeros_like(sums)

    def add(e, _):
        source = pl.ds(pl.multiple_of(e * BLK, BLK), BLK)
        for names, terms in ((ids, own), (asked, got)):
            core, piece, row = place_of(names, e, me, blocks, True)

            @pl.when(jnp.logical_and(core, piece == late))
            def _():
                sums[pl.ds(row, BLK)] += terms[source].astype(F32)

        return 0

    lax.fori_loop(0, entries, add, 0)
    out[...] = sums[...].astype(out.dtype)


def merge_kernel(entries, late, ids, asked, own, got, *refs):
    chain = len(refs) // 2
    kept, outs, sums = refs[:chain], refs[chain:-1], refs[-1]
    chunk = kept[0].shape[0]
    me = lax.axis_index("tm")
    for ref in kept:
        ref[...] = jnp.zeros_like(ref)
    sums[...] = jnp.zeros_like(sums)

    def add(e, _):
        source = pl.ds(pl.multiple_of(e * BLK, BLK), BLK)
        for names, terms in ((ids, own), (asked, got)):
            core, piece, row = place_of(names, e, me, chunk // BLK, True)
            index = jnp.where(piece < late, piece - chain, piece - 1 - chain)

            @pl.when(jnp.logical_and(core, piece < chain))
            def _():
                def act(ref):
                    ref[pl.ds(row, BLK)] += terms[source].astype(F32)

                pick(kept, piece, act)

            @pl.when(jnp.logical_and(core, jnp.logical_and(piece >= chain, piece != late)))
            def _():
                sums[pl.ds(pl.multiple_of(index * chunk + row, BLK), BLK)] += terms[source].astype(F32)

        return 0

    lax.fori_loop(0, entries, add, 0)
    for q, out in enumerate(outs):
        out[...] = sums[q * chunk : (q + 1) * chunk].astype(out.dtype)


def hop_kernel(total, *refs):
    out = refs[-1]
    value = total[...]
    for came in refs[:-1]:
        value += came[...].astype(F32)
    out[...] = value.astype(out.dtype)


def local(latents, kernel, loadings, recorded, owner_ids, local_ids, recorded_mask):
    latent_dim, bins = latents.shape
    halfwidth = kernel.shape[1] // 2
    count = lax.axis_size("tm")
    chain = count // ROW
    chunk = loadings.shape[0]
    entries = owner_ids.size
    piece_bytes = count * chunk * latent_dim
    smem = pl.BlockSpec(memory_space=pltpu.SMEM)

    def permute(x, pairs):
        return lax.ppermute(x, "tm", pairs)

    def rotate(x, r):
        return permute(x, [(i, (i + r * ROW) % count) for i in range(count)])

    def flip(x, bit):
        return permute(x, [(i, i ^ bit) for i in range(count)])

    odd_even = [(i, i + 1) for i in range(1, count - 1, 2)]
    odd_even += [(target, source) for source, target in odd_even]

    ids = owner_ids[0] * (chunk // BLK) + local_ids[0]
    asked = flip(ids, 1)
    mask = jnp.transpose(recorded_mask, (0, 2, 1))

    even = lax.axis_index("tm") % 2 == 0
    later, earlier = latents[:, bins - halfwidth :], latents[:, :halfwidth]
    core_side = flip(jnp.where(even, later, earlier), 1)
    far_side = permute(jnp.where(even, earlier, later), odd_even)

    half = chain // 2
    late = chain + half
    straight = [loadings] * chain
    for r in range(1, half):
        straight[r] = rotate(straight[r - 1], 1)
        straight[-r] = rotate(straight[1 - r], -1)
    across = [flip(loadings, 2)] + [None] * (chain - 1)
    if half > 1:
        straight[1], across[0] = lax.optimization_barrier((straight[1], across[0]))
    straight[half] = rotate(straight[half - 1], 1)
    table = dft_tables(2 * halfwidth)
    mxu = 30 * 2 * latent_dim * (2 * halfwidth) ** 2
    square = jax.ShapeDtypeStruct((latent_dim, 2 * halfwidth), F32)
    prepared = pl.pallas_call(
        prepare_kernel,
        out_shape=(
            jax.ShapeDtypeStruct(table.shape, BF16),
            jax.ShapeDtypeStruct(latents.shape, F32),
        )
        + (square,) * 3,
        in_specs=[HBM] * 3,
        out_specs=(VMEM,) * 5,
        scratch_shapes=[pltpu.VMEM(kernel.shape, F32), pltpu.SemaphoreType.DMA((8,))],
        compiler_params=pltpu.CompilerParams(vmem_limit_bytes=50 * MIB),
        cost_estimate=pl.CostEstimate(flops=mxu // 3, bytes_accessed=4 * MIB, transcendentals=0),
        name="prepare",
    )(table, kernel, latents)
    straight[-1], *prepared = lax.optimization_barrier((straight[-1], *prepared))
    spectrum, held_bins = [prepared[0], *prepared[2:]], prepared[1]
    for r in range(1, chain):
        if r != half:
            across[r] = flip(straight[r], 2)

    smoothed = pl.pallas_call(
        smooth_kernel,
        out_shape=jax.ShapeDtypeStruct((latent_dim, bins), BF16),
        in_specs=[VMEM] * 7,
        out_specs=VMEM,
        compiler_params=pltpu.CompilerParams(vmem_limit_bytes=16 * MIB),
        cost_estimate=pl.CostEstimate(flops=mxu, bytes_accessed=4 * MIB, transcendentals=0),
        name="smooth",
    )(held_bins, core_side, far_side, *spectrum)

    slots = jax.ShapeDtypeStruct((entries * BLK, latent_dim), BF16)
    across[half] = flip(straight[half], 2)
    early = straight + across[:half] + across[half + 1 :]

    def pack(first, total):
        return pl.pallas_call(
            functools.partial(pack_kernel, first, total, late),
            out_shape=jax.ShapeDtypeStruct((total * BLK, latent_dim), BF16),
            in_specs=[smem] + [VMEM] * len(early),
            out_specs=VMEM,
            compiler_params=pltpu.CompilerParams(vmem_limit_bytes=4 * MIB + 3 * piece_bytes),
            cost_estimate=pl.CostEstimate(flops=0, bytes_accessed=2**20, transcendentals=0),
            name="pack",
        )(asked, *early)

    asked, smoothed, mask = lax.optimization_barrier((asked, smoothed, mask))
    packed = [flip(pack(first, entries // 2), 1) for first in (0, entries // 2)]
    last, smoothed = lax.optimization_barrier((across[half], smoothed))
    late_theirs = flip(last, 1)
    pieces = straight + across

    group = 4
    extended = jax.ShapeDtypeStruct((entries * BLK + latent_dim, latent_dim), BF16)
    grad, far_side, terms = pl.pallas_call(
        functools.partial(session_kernel, entries, group, late),
        out_shape=(
            jax.ShapeDtypeStruct((latent_dim, bins), F32),
            jax.ShapeDtypeStruct((latent_dim, 2 * halfwidth), BF16),
            extended,
        ),
        in_specs=[smem] * 2 + [VMEM] * (5 + len(pieces)),
        out_specs=(VMEM,) * 3,
        scratch_shapes=[
            pltpu.VMEM((group * BLK, latent_dim), BF16),
            pltpu.VMEM((group * BLK, bins), BF16),
        ],
        compiler_params=pltpu.CompilerParams(vmem_limit_bytes=12 * MIB + 6 * piece_bytes),
        cost_estimate=pl.CostEstimate(
            flops=6 * entries * BLK * latent_dim * bins, bytes_accessed=8 * 2**20, transcendentals=0
        ),
        name="session",
    )(
        ids,
        mask,
        smoothed,
        recorded.reshape(entries, BLK, bins),
        *packed,
        late_theirs,
        *pieces,
    )

    got = flip(terms, 1)
    narrow = jax.ShapeDtypeStruct((chunk, latent_dim), BF16)
    sent = pl.pallas_call(
        functools.partial(merge_late_kernel, entries, late),
        out_shape=narrow,
        in_specs=[smem] * 2 + [VMEM] * 2,
        out_specs=VMEM,
        scratch_shapes=[pltpu.VMEM((chunk, latent_dim), F32)],
        compiler_params=pltpu.CompilerParams(vmem_limit_bytes=4 * MIB + 3 * piece_bytes),
        cost_estimate=pl.CostEstimate(flops=0, bytes_accessed=2**20, transcendentals=0),
        name="merge_late",
    )(ids, asked, terms, got)
    wide = jax.ShapeDtypeStruct((chunk, latent_dim), F32)
    sent, ids = lax.optimization_barrier((sent, ids))
    back = flip(sent, 2)
    merged = pl.pallas_call(
        functools.partial(merge_kernel, entries, late),
        out_shape=(wide,) * chain + (narrow,) * (chain - 1),
        in_specs=[smem] * 2 + [VMEM] * 2,
        out_specs=(VMEM,) * (2 * chain - 1),
        scratch_shapes=[pltpu.VMEM(((chain - 1) * chunk, latent_dim), F32)],
        compiler_params=pltpu.CompilerParams(vmem_limit_bytes=4 * MIB + 6 * piece_bytes),
        cost_estimate=pl.CostEstimate(flops=0, bytes_accessed=5 * 2**20, transcendentals=0),
        name="merge",
    )(ids, asked, terms, got)
    crossed = {r: merged[chain + r - (r > half)] for r in range(chain) if r != half}
    other = {r: flip(part, 2) for r, part in crossed.items() if r}

    def hop(total, *came):
        return pl.pallas_call(
            hop_kernel,
            out_shape=narrow,
            in_specs=[VMEM] * (1 + len(came)),
            out_specs=VMEM,
            compiler_params=pltpu.CompilerParams(vmem_limit_bytes=8 * MIB),
            cost_estimate=pl.CostEstimate(flops=0, bytes_accessed=MIB, transcendentals=0),
            name="hop",
        )(total, *came)

    rise = hop(merged[half], back)
    rise, far_side = lax.optimization_barrier((rise, far_side))
    far_side = permute(far_side, odd_even)
    rise = rotate(rise, 1)
    for r in range(half - 1, 0, -1):
        rise = hop(merged[r], other[r], rise)
        if r == 1:
            _, far_side, own = lax.optimization_barrier((rise, far_side, crossed[0]))
            other[0] = flip(own, 2)
        rise = rotate(rise, 1)
    fall = rotate(hop(merged[half + 1], other[half + 1]), -1)
    for r in range(half + 2, chain):
        fall = rotate(hop(merged[r], other[r], fall), -1)
    loading_grad = merged[0] + other[0].astype(F32) + rise.astype(F32) + fall.astype(F32)

    latent_grad = pl.pallas_call(
        unsmooth_kernel,
        out_shape=jax.ShapeDtypeStruct((latent_dim, bins), F32),
        in_specs=[VMEM] * 7,
        out_specs=VMEM,
        compiler_params=pltpu.CompilerParams(vmem_limit_bytes=16 * MIB),
        cost_estimate=pl.CostEstimate(flops=mxu, bytes_accessed=4 * MIB, transcendentals=0),
        name="unsmooth",
    )(grad, got, far_side, *spectrum)
    return latent_grad, loading_grad


def solution(mesh):
    return jax.shard_map(
        local,
        mesh=mesh,
        in_specs=(
            P(None, ("groups", "tm")),
            P(),
            P(("groups", "tm"), None),
            P(None, None, None, ("groups", "tm")),
            P(("groups", "tm"), None, None),
            P(("groups", "tm"), None, None),
            P(None, None, ("groups", "tm")),
        ),
        out_specs=(P(None, ("groups", "tm")), P(("groups", "tm"), None)),
        check_vma=False,
    )
```

```python
import functools

import jax
import jax.numpy as jnp
import numpy as np
from jax import lax
from jax.experimental import pallas as pl
from jax.experimental.pallas import tpu as pltpu
from jax.sharding import PartitionSpec as P

BLK = 128
ROW = 4
MIB = 2**20
F32 = jnp.float32
BF16 = jnp.bfloat16
VMEM = pl.BlockSpec(memory_space=pltpu.VMEM)
HBM = pl.BlockSpec(memory_space=pltpu.HBM)


def split_const(a):
    high = a.astype(jnp.bfloat16)
    low = (a - high.astype(np.float64)).astype(jnp.bfloat16)
    return high, low


@functools.lru_cache(maxsize=None)
def dft_tables(size):
    t = np.arange(size)[:, None]
    g = np.arange(size)[None, :]
    half = size // 2
    angle = 2 * np.pi * ((t * g[:, :half]) % size) / size
    cos, sin = np.cos(angle), np.sin(angle)
    sin[:, 0] = 1 - 2 * (np.arange(size) % 2)
    real = np.concatenate([cos, sin], axis=1)
    angle = 2 * np.pi * ((t * (3 * g + 1)) % (3 * size)) / (3 * size)
    cos, sin = np.cos(angle), np.sin(angle)
    weight = np.full((size,), 2.0)
    weight[0] = weight[half] = 1.0
    scale = 1.0 / (3 * size)
    tables = [real, cos, sin, (real * weight).T * scale, cos.T * 2 * scale, sin.T * 2 * scale]
    return np.concatenate([part for table in tables for part in split_const(table)])


def parts(a):
    high = a.astype(BF16)
    return high, (a - high.astype(F32)).astype(BF16)


def times(a, tables, index):
    rows, size = a.shape
    high, low = parts(a)
    first = 2 * index * size
    t_high, t_low = tables[first : first + size], tables[first + size : first + 2 * size]
    out = jnp.dot(jnp.concatenate([high, low]), t_high, preferred_element_type=F32)
    return out[:rows] + out[rows:] + jnp.dot(high, t_low, preferred_element_type=F32)


ROOT = 0.75**0.5


def spectrum_of(thirds, tables):
    first, second, third = thirds
    rows = first.shape[0]
    base = times(first + second + third, tables, 0)
    y = jnp.concatenate([first - 0.5 * (second + third), ROOT * (third - second)])
    cos, sin = times(y, tables, 1), times(y, tables, 2)
    return base, cos[:rows] + sin[rows:], cos[rows:] - sin[:rows]


def filtered(signal, taps, sign, tables, wanted):
    (xb, xr, xi), (kb, kr, ki) = signal, taps
    rows, size = xb.shape
    half = size // 2
    first = lax.broadcasted_iota(jnp.int32, (rows, half), 1) == 0
    kc, ks = kb[:, :half], kb[:, half:]
    kc_s = jnp.where(first, ks, kc)
    ks_x = jnp.where(first, 0.0, ks) * sign
    xc, xs = xb[:, :half], xb[:, half:]
    base = times(jnp.concatenate([xc * kc + xs * ks_x, xs * kc_s - xc * ks_x], axis=1), tables, 3)
    ki = ki * sign
    z = jnp.concatenate([xr * kr + xi * ki, xi * kr - xr * ki])
    cos, sin = times(z, tables, 4), times(z, tables, 5)
    vr, vi = cos[:rows] - sin[rows:], sin[:rows] + cos[rows:]
    each = (base + vr, base - 0.5 * vr - ROOT * vi, base - 0.5 * vr + ROOT * vi)
    return jnp.concatenate([each[m] for m in wanted], axis=1)


def thirds_of(mid, core_side, far_side):
    width = core_side.shape[1]
    size = 2 * width
    even = lax.rem(lax.axis_index("tm"), 2) == 0
    low, high = jnp.where(even, far_side, core_side), jnp.where(even, core_side, far_side)
    last = mid.shape[1] - width
    return (
        jnp.concatenate([low, mid[:, :width]], axis=1),
        mid[:, width : width + size],
        jnp.concatenate([mid[:, last:], high], axis=1),
    )


def prepare_kernel(table, taps, mid, tables, bins, base, kr, ki, held, sem):
    rows = table.shape[0] // 6
    cuts = [pl.ds(i * rows, rows) for i in range(6)]
    copies = [pltpu.make_async_copy(taps, held, sem.at[0])]
    copies += [
        pltpu.make_async_copy(table.at[cut], tables.at[cut], sem.at[1 + i])
        for i, cut in enumerate(cuts)
    ]
    copies += [pltpu.make_async_copy(mid, bins, sem.at[7])]
    for copy in copies:
        copy.start()
    copies[0].wait()
    for i, (ref, sign) in enumerate(((base, 1.0), (kr, 1.0), (ki, -1.0))):
        copies[1 + i].wait()
        ref[...] = times(held[...], tables, i) * sign
    for copy in copies[4:]:
        copy.wait()


def smooth_kernel(mid, core_side, far_side, tables, base, kr, ki, out):
    thirds = thirds_of(mid[...], core_side[...], far_side[...])
    signal = spectrum_of(thirds, tables)
    taps = (base[...], kr[...], ki[...])
    out[...] = filtered(signal, taps, 1.0, tables, (0, 1)).astype(out.dtype)


def unsmooth_kernel(mid, got, far_side, tables, base, kr, ki, out):
    width = far_side.shape[1] // 2
    core = got[got.shape[0] - far_side.shape[0] :].astype(F32)
    far = far_side[...].astype(F32)
    thirds = thirds_of(
        mid[...], core[:, :width] + core[:, width:], far[:, :width] + far[:, width:]
    )
    signal = spectrum_of(thirds, tables)
    taps = (base[...], kr[...], ki[...])
    out[...] = filtered(signal, taps, -1.0, tables, (1, 2))


def divide(a, n):
    return a >> (n.bit_length() - 1) if n & (n - 1) == 0 else a // n


def remainder(a, n):
    return a & (n - 1) if n & (n - 1) == 0 else a % n


def place_of(ids, e, me, blocks, forward):
    chain = lax.axis_size("tm") // ROW
    top = ids.shape[1]
    code = ids[divide(e, top), remainder(e, top)]
    owner, slot = divide(code, blocks), remainder(code, blocks)
    step = divide(owner, ROW) - divide(me, ROW)
    step = step if forward else -step
    turn = jnp.where(step < 0, step + chain, step)
    differ = owner ^ me
    piece = jnp.where(differ & 2 == 0, 0, chain) + turn
    return differ & 1 == 0, piece, pl.multiple_of(slot * BLK, BLK)


def pick(refs, index, act):
    if len(refs) == 1:
        act(refs[0])
        return
    half = len(refs) // 2
    lax.cond(
        index < half,
        lambda: pick(refs[:half], index, act),
        lambda: pick(refs[half:], index - half, act),
    )


def pack_kernel(first, entries, late, asked, *refs):
    pieces, out = refs[:-1], refs[-1]
    blocks = pieces[0].shape[0] // BLK
    me = lax.axis_index("tm")

    def body(e, _):
        core, piece, row = place_of(asked, first + e, me, blocks, False)
        target = pl.ds(pl.multiple_of(e * BLK, BLK), BLK)

        @pl.when(jnp.logical_and(core, piece != late))
        def _():
            def act(ref):
                out[target] = ref[pl.ds(row, BLK)]

            pick(pieces, jnp.where(piece < late, piece, piece - 1), act)

        return 0

    lax.fori_loop(0, entries, body, 0)


def session_kernel(
    entries, group, late, ids, mask, smoothed, recorded, packed, packed_rest, late_theirs, *refs
):
    pieces = refs[:-5]
    grad, far_side, terms, rows, resid = refs[-5:]
    blocks = pieces[0].shape[0] // BLK
    bins = smoothed.shape[1]
    top = ids.shape[1]
    me = lax.axis_index("tm")
    grad[...] = jnp.zeros_like(grad)
    depth = group * BLK

    def step(g, _):
        for i in range(group):
            e = g * group + i
            core, piece, row = place_of(ids, e, me, blocks, False)

            def own():
                def act(ref):
                    rows[i * BLK : (i + 1) * BLK] = ref[pl.ds(row, BLK)]

                pick(pieces, piece, act)

            def other():
                @pl.when(piece == late)
                def _():
                    rows[i * BLK : (i + 1) * BLK] = late_theirs[pl.ds(row, BLK)]

                @pl.when(piece != late)
                def _():
                    def act(ref):
                        source = pl.ds(pl.multiple_of(remainder(e, entries // 2) * BLK, BLK), BLK)
                        rows[i * BLK : (i + 1) * BLK] = ref[source]

                    pick((packed, packed_rest), divide(e, entries // 2), act)

            lax.cond(core, own, other)
        block = rows[...]
        predicted = jnp.dot(block, smoothed[...], preferred_element_type=F32)
        for i in range(group):
            e = g * group + i
            for t in range(bins // BLK):
                cut = slice(t * BLK, (t + 1) * BLK)
                weight = mask[divide(e, top), t, remainder(e, top)].astype(F32)
                part = predicted[i * BLK : (i + 1) * BLK, cut]
                seen = recorded[e, :, cut].astype(F32)
                resid[i * BLK : (i + 1) * BLK, cut] = (weight * (part - seen)).astype(BF16)
        term = lax.dot_general(
            resid[...], smoothed[...], (((1,), (1,)), ((), ())), preferred_element_type=F32
        )
        target = pl.ds(pl.multiple_of(g * depth, depth), depth)
        terms[target] = (term * (1.0 / BLK)).astype(BF16)
        grad[...] += lax.dot_general(
            block, resid[...], (((0,), (0,)), ((), ())), preferred_element_type=F32
        ) * (1.0 / BLK)
        return 0

    lax.fori_loop(0, entries // group, step, 0)
    latent_dim, width = grad.shape[0], rows.shape[1] // 2
    even = me & 1 == 0
    later, earlier = grad[:, bins - width :], grad[:, :width]
    core_edge, far_edge = jnp.where(even, later, earlier), jnp.where(even, earlier, later)
    terms[pl.ds(entries * BLK, latent_dim)] = jnp.concatenate(parts(core_edge), axis=1)
    far_side[...] = jnp.concatenate(parts(far_edge), axis=1)


def merge_late_kernel(entries, late, ids, asked, own, got, out, sums):
    blocks = out.shape[0] // BLK
    me = lax.axis_index("tm")
    sums[...] = jnp.zeros_like(sums)

    def add(e, _):
        source = pl.ds(pl.multiple_of(e * BLK, BLK), BLK)
        for names, terms in ((ids, own), (asked, got)):
            core, piece, row = place_of(names, e, me, blocks, True)

            @pl.when(jnp.logical_and(core, piece == late))
            def _():
                sums[pl.ds(row, BLK)] += terms[source].astype(F32)

        return 0

    lax.fori_loop(0, entries, add, 0)
    out[...] = sums[...].astype(out.dtype)


def merge_kernel(entries, late, ids, asked, own, got, *refs):
    chain = len(refs) // 2
    kept, outs, sums = refs[:chain], refs[chain:-1], refs[-1]
    chunk = kept[0].shape[0]
    me = lax.axis_index("tm")
    for ref in kept:
        ref[...] = jnp.zeros_like(ref)
    sums[...] = jnp.zeros_like(sums)

    def add(e, _):
        source = pl.ds(pl.multiple_of(e * BLK, BLK), BLK)
        for names, terms in ((ids, own), (asked, got)):
            core, piece, row = place_of(names, e, me, chunk // BLK, True)
            index = jnp.where(piece < late, piece - chain, piece - 1 - chain)

            @pl.when(jnp.logical_and(core, piece < chain))
            def _():
                def act(ref):
                    ref[pl.ds(row, BLK)] += terms[source].astype(F32)

                pick(kept, piece, act)

            @pl.when(jnp.logical_and(core, jnp.logical_and(piece >= chain, piece != late)))
            def _():
                sums[pl.ds(pl.multiple_of(index * chunk + row, BLK), BLK)] += terms[source].astype(F32)

        return 0

    lax.fori_loop(0, entries, add, 0)
    for q, out in enumerate(outs):
        out[...] = sums[q * chunk : (q + 1) * chunk].astype(out.dtype)


def hop_kernel(total, *refs):
    out = refs[-1]
    value = total[...]
    for came in refs[:-1]:
        value += came[...].astype(F32)
    out[...] = value.astype(out.dtype)


def local(latents, kernel, loadings, recorded, owner_ids, local_ids, recorded_mask):
    latent_dim, bins = latents.shape
    halfwidth = kernel.shape[1] // 2
    count = lax.axis_size("tm")
    chain = count // ROW
    chunk = loadings.shape[0]
    entries = owner_ids.size
    piece_bytes = count * chunk * latent_dim
    smem = pl.BlockSpec(memory_space=pltpu.SMEM)

    def permute(x, pairs):
        return lax.ppermute(x, "tm", pairs)

    def rotate(x, r):
        return permute(x, [(i, (i + r * ROW) % count) for i in range(count)])

    def flip(x, bit):
        return permute(x, [(i, i ^ bit) for i in range(count)])

    odd_even = [(i, i + 1) for i in range(1, count - 1, 2)]
    odd_even += [(target, source) for source, target in odd_even]

    ids = owner_ids[0] * (chunk // BLK) + local_ids[0]
    asked = flip(ids, 1)
    mask = jnp.transpose(recorded_mask, (0, 2, 1))

    even = lax.axis_index("tm") % 2 == 0
    later, earlier = latents[:, bins - halfwidth :], latents[:, :halfwidth]
    core_side = flip(jnp.where(even, later, earlier), 1)
    far_side = permute(jnp.where(even, earlier, later), odd_even)

    half = chain // 2
    late = chain + half
    straight = [loadings] * chain
    for r in range(1, half):
        straight[r] = rotate(straight[r - 1], 1)
        straight[-r] = rotate(straight[1 - r], -1)
    across = [flip(loadings, 2)] + [None] * (chain - 1)
    if half > 1:
        straight[1], across[0] = lax.optimization_barrier((straight[1], across[0]))
    straight[half] = rotate(straight[half - 1], 1)
    straight[1], kernel = lax.optimization_barrier((straight[1], kernel))
    table = dft_tables(2 * halfwidth)
    mxu = 30 * 2 * latent_dim * (2 * halfwidth) ** 2
    square = jax.ShapeDtypeStruct((latent_dim, 2 * halfwidth), F32)
    prepared = pl.pallas_call(
        prepare_kernel,
        out_shape=(
            jax.ShapeDtypeStruct(table.shape, BF16),
            jax.ShapeDtypeStruct(latents.shape, F32),
        )
        + (square,) * 3,
        in_specs=[HBM] * 3,
        out_specs=(VMEM,) * 5,
        scratch_shapes=[pltpu.VMEM(kernel.shape, F32), pltpu.SemaphoreType.DMA((8,))],
        compiler_params=pltpu.CompilerParams(vmem_limit_bytes=50 * MIB),
        cost_estimate=pl.CostEstimate(flops=mxu // 3, bytes_accessed=4 * MIB, transcendentals=0),
        name="prepare",
    )(table, kernel, latents)
    straight[-1], *prepared = lax.optimization_barrier((straight[-1], *prepared))
    spectrum, held_bins = [prepared[0], *prepared[2:]], prepared[1]
    for r in range(1, chain):
        if r != half:
            across[r] = flip(straight[r], 2)

    smoothed = pl.pallas_call(
        smooth_kernel,
        out_shape=jax.ShapeDtypeStruct((latent_dim, bins), BF16),
        in_specs=[VMEM] * 7,
        out_specs=VMEM,
        compiler_params=pltpu.CompilerParams(vmem_limit_bytes=16 * MIB),
        cost_estimate=pl.CostEstimate(flops=mxu, bytes_accessed=4 * MIB, transcendentals=0),
        name="smooth",
    )(held_bins, core_side, far_side, *spectrum)

    slots = jax.ShapeDtypeStruct((entries * BLK, latent_dim), BF16)
    across[half] = flip(straight[half], 2)
    early = straight + across[:half] + across[half + 1 :]

    def pack(first, total):
        return pl.pallas_call(
            functools.partial(pack_kernel, first, total, late),
            out_shape=jax.ShapeDtypeStruct((total * BLK, latent_dim), BF16),
            in_specs=[smem] + [VMEM] * len(early),
            out_specs=VMEM,
            compiler_params=pltpu.CompilerParams(vmem_limit_bytes=4 * MIB + 3 * piece_bytes),
            cost_estimate=pl.CostEstimate(flops=0, bytes_accessed=2**20, transcendentals=0),
            name="pack",
        )(asked, *early)

    asked, smoothed, mask = lax.optimization_barrier((asked, smoothed, mask))
    packed = [flip(pack(first, entries // 2), 1) for first in (0, entries // 2)]
    last, smoothed = lax.optimization_barrier((across[half], smoothed))
    late_theirs = flip(last, 1)
    pieces = straight + across

    group = 4
    extended = jax.ShapeDtypeStruct((entries * BLK + latent_dim, latent_dim), BF16)
    grad, far_side, terms = pl.pallas_call(
        functools.partial(session_kernel, entries, group, late),
        out_shape=(
            jax.ShapeDtypeStruct((latent_dim, bins), F32),
            jax.ShapeDtypeStruct((latent_dim, 2 * halfwidth), BF16),
            extended,
        ),
        in_specs=[smem] * 2 + [VMEM] * (5 + len(pieces)),
        out_specs=(VMEM,) * 3,
        scratch_shapes=[
            pltpu.VMEM((group * BLK, latent_dim), BF16),
            pltpu.VMEM((group * BLK, bins), BF16),
        ],
        compiler_params=pltpu.CompilerParams(vmem_limit_bytes=12 * MIB + 6 * piece_bytes),
        cost_estimate=pl.CostEstimate(
            flops=6 * entries * BLK * latent_dim * bins, bytes_accessed=8 * 2**20, transcendentals=0
        ),
        name="session",
    )(
        ids,
        mask,
        smoothed,
        recorded.reshape(entries, BLK, bins),
        *packed,
        late_theirs,
        *pieces,
    )

    got = flip(terms, 1)
    narrow = jax.ShapeDtypeStruct((chunk, latent_dim), BF16)
    sent = pl.pallas_call(
        functools.partial(merge_late_kernel, entries, late),
        out_shape=narrow,
        in_specs=[smem] * 2 + [VMEM] * 2,
        out_specs=VMEM,
        scratch_shapes=[pltpu.VMEM((chunk, latent_dim), F32)],
        compiler_params=pltpu.CompilerParams(vmem_limit_bytes=4 * MIB + 3 * piece_bytes),
        cost_estimate=pl.CostEstimate(flops=0, bytes_accessed=2**20, transcendentals=0),
        name="merge_late",
    )(ids, asked, terms, got)
    wide = jax.ShapeDtypeStruct((chunk, latent_dim), F32)
    sent, ids = lax.optimization_barrier((sent, ids))
    back = flip(sent, 2)
    merged = pl.pallas_call(
        functools.partial(merge_kernel, entries, late),
        out_shape=(wide,) * chain + (narrow,) * (chain - 1),
        in_specs=[smem] * 2 + [VMEM] * 2,
        out_specs=(VMEM,) * (2 * chain - 1),
        scratch_shapes=[pltpu.VMEM(((chain - 1) * chunk, latent_dim), F32)],
        compiler_params=pltpu.CompilerParams(vmem_limit_bytes=4 * MIB + 6 * piece_bytes),
        cost_estimate=pl.CostEstimate(flops=0, bytes_accessed=5 * 2**20, transcendentals=0),
        name="merge",
    )(ids, asked, terms, got)
    crossed = {r: merged[chain + r - (r > half)] for r in range(chain) if r != half}
    other = {r: flip(part, 2) for r, part in crossed.items() if r}

    def hop(total, *came):
        return pl.pallas_call(
            hop_kernel,
            out_shape=narrow,
            in_specs=[VMEM] * (1 + len(came)),
            out_specs=VMEM,
            compiler_params=pltpu.CompilerParams(vmem_limit_bytes=8 * MIB),
            cost_estimate=pl.CostEstimate(flops=0, bytes_accessed=MIB, transcendentals=0),
            name="hop",
        )(total, *came)

    rise = hop(merged[half], back)
    rise, far_side = lax.optimization_barrier((rise, far_side))
    far_side = permute(far_side, odd_even)
    far_side, own = lax.optimization_barrier((far_side, crossed[0]))
    other[0] = flip(own, 2)
    rise = rotate(rise, 1)
    for r in range(half - 1, 0, -1):
        rise = rotate(hop(merged[r], other[r], rise), 1)
    fall = rotate(hop(merged[half + 1], other[half + 1]), -1)
    for r in range(half + 2, chain):
        fall = rotate(hop(merged[r], other[r], fall), -1)
    loading_grad = merged[0] + other[0].astype(F32) + rise.astype(F32) + fall.astype(F32)

    latent_grad = pl.pallas_call(
        unsmooth_kernel,
        out_shape=jax.ShapeDtypeStruct((latent_dim, bins), F32),
        in_specs=[VMEM] * 7,
        out_specs=VMEM,
        compiler_params=pltpu.CompilerParams(vmem_limit_bytes=16 * MIB),
        cost_estimate=pl.CostEstimate(flops=mxu, bytes_accessed=4 * MIB, transcendentals=0),
        name="unsmooth",
    )(grad, got, far_side, *spectrum)
    return latent_grad, loading_grad


def solution(mesh):
    return jax.shard_map(
        local,
        mesh=mesh,
        in_specs=(
            P(None, ("groups", "tm")),
            P(),
            P(("groups", "tm"), None),
            P(None, None, None, ("groups", "tm")),
            P(("groups", "tm"), None, None),
            P(("groups", "tm"), None, None),
            P(None, None, ("groups", "tm")),
        ),
        out_specs=(P(None, ("groups", "tm")), P(("groups", "tm"), None)),
        check_vma=False,
    )
```

```python
import functools

import jax
import jax.numpy as jnp
import numpy as np
from jax import lax
from jax.experimental import pallas as pl
from jax.experimental.pallas import tpu as pltpu
from jax.sharding import PartitionSpec as P

BLK = 128
ROW = 4
MIB = 2**20
F32 = jnp.float32
BF16 = jnp.bfloat16
VMEM = pl.BlockSpec(memory_space=pltpu.VMEM)
HBM = pl.BlockSpec(memory_space=pltpu.HBM)


def split_const(a):
    high = a.astype(jnp.bfloat16)
    low = (a - high.astype(np.float64)).astype(jnp.bfloat16)
    return high, low


@functools.lru_cache(maxsize=None)
def dft_tables(size):
    t = np.arange(size)[:, None]
    g = np.arange(size)[None, :]
    half = size // 2
    angle = 2 * np.pi * ((t * g[:, :half]) % size) / size
    cos, sin = np.cos(angle), np.sin(angle)
    sin[:, 0] = 1 - 2 * (np.arange(size) % 2)
    real = np.concatenate([cos, sin], axis=1)
    angle = 2 * np.pi * ((t * (3 * g + 1)) % (3 * size)) / (3 * size)
    cos, sin = np.cos(angle), np.sin(angle)
    weight = np.full((size,), 2.0)
    weight[0] = weight[half] = 1.0
    scale = 1.0 / (3 * size)
    tables = [real, cos, sin, (real * weight).T * scale, cos.T * 2 * scale, sin.T * 2 * scale]
    return np.concatenate([part for table in tables for part in split_const(table)])


def parts(a):
    high = a.astype(BF16)
    return high, (a - high.astype(F32)).astype(BF16)


def times(a, tables, index):
    rows, size = a.shape
    high, low = parts(a)
    first = 2 * index * size
    t_high, t_low = tables[first : first + size], tables[first + size : first + 2 * size]
    out = jnp.dot(jnp.concatenate([high, low]), t_high, preferred_element_type=F32)
    return out[:rows] + out[rows:] + jnp.dot(high, t_low, preferred_element_type=F32)


ROOT = 0.75**0.5


def spectrum_of(thirds, tables):
    first, second, third = thirds
    rows = first.shape[0]
    base = times(first + second + third, tables, 0)
    y = jnp.concatenate([first - 0.5 * (second + third), ROOT * (third - second)])
    cos, sin = times(y, tables, 1), times(y, tables, 2)
    return base, cos[:rows] + sin[rows:], cos[rows:] - sin[:rows]


def filtered(signal, taps, sign, tables, wanted):
    (xb, xr, xi), (kb, kr, ki) = signal, taps
    rows, size = xb.shape
    half = size // 2
    first = lax.broadcasted_iota(jnp.int32, (rows, half), 1) == 0
    kc, ks = kb[:, :half], kb[:, half:]
    kc_s = jnp.where(first, ks, kc)
    ks_x = jnp.where(first, 0.0, ks) * sign
    xc, xs = xb[:, :half], xb[:, half:]
    base = times(jnp.concatenate([xc * kc + xs * ks_x, xs * kc_s - xc * ks_x], axis=1), tables, 3)
    ki = ki * sign
    z = jnp.concatenate([xr * kr + xi * ki, xi * kr - xr * ki])
    cos, sin = times(z, tables, 4), times(z, tables, 5)
    vr, vi = cos[:rows] - sin[rows:], sin[:rows] + cos[rows:]
    each = (base + vr, base - 0.5 * vr - ROOT * vi, base - 0.5 * vr + ROOT * vi)
    return jnp.concatenate([each[m] for m in wanted], axis=1)


def thirds_of(mid, core_side, far_side):
    width = core_side.shape[1]
    size = 2 * width
    even = lax.rem(lax.axis_index("tm"), 2) == 0
    low, high = jnp.where(even, far_side, core_side), jnp.where(even, core_side, far_side)
    last = mid.shape[1] - width
    return (
        jnp.concatenate([low, mid[:, :width]], axis=1),
        mid[:, width : width + size],
        jnp.concatenate([mid[:, last:], high], axis=1),
    )


def prepare_kernel(table, taps, mid, tables, bins, base, kr, ki, held, sem):
    rows = table.shape[0] // 6
    cuts = [pl.ds(i * rows, rows) for i in range(6)]
    copies = [pltpu.make_async_copy(taps, held, sem.at[0])]
    copies += [
        pltpu.make_async_copy(table.at[cut], tables.at[cut], sem.at[1 + i])
        for i, cut in enumerate(cuts)
    ]
    copies += [pltpu.make_async_copy(mid, bins, sem.at[7])]
    for copy in copies:
        copy.start()
    copies[0].wait()
    for i, (ref, sign) in enumerate(((base, 1.0), (kr, 1.0), (ki, -1.0))):
        copies[1 + i].wait()
        ref[...] = times(held[...], tables, i) * sign
    for copy in copies[4:]:
        copy.wait()


def smooth_kernel(mid, core_side, far_side, tables, base, kr, ki, out):
    thirds = thirds_of(mid[...], core_side[...], far_side[...])
    signal = spectrum_of(thirds, tables)
    taps = (base[...], kr[...], ki[...])
    out[...] = filtered(signal, taps, 1.0, tables, (0, 1)).astype(out.dtype)


def unsmooth_kernel(mid, got, far_side, tables, base, kr, ki, out):
    width = far_side.shape[1] // 2
    core = got[got.shape[0] - far_side.shape[0] :].astype(F32)
    far = far_side[...].astype(F32)
    thirds = thirds_of(
        mid[...], core[:, :width] + core[:, width:], far[:, :width] + far[:, width:]
    )
    signal = spectrum_of(thirds, tables)
    taps = (base[...], kr[...], ki[...])
    out[...] = filtered(signal, taps, -1.0, tables, (1, 2))


def divide(a, n):
    return a >> (n.bit_length() - 1) if n & (n - 1) == 0 else a // n


def remainder(a, n):
    return a & (n - 1) if n & (n - 1) == 0 else a % n


def place_of(ids, e, me, blocks, forward):
    chain = lax.axis_size("tm") // ROW
    top = ids.shape[1]
    code = ids[divide(e, top), remainder(e, top)]
    owner, slot = divide(code, blocks), remainder(code, blocks)
    step = divide(owner, ROW) - divide(me, ROW)
    step = step if forward else -step
    turn = jnp.where(step < 0, step + chain, step)
    differ = owner ^ me
    piece = jnp.where(differ & 2 == 0, 0, chain) + turn
    return differ & 1 == 0, piece, pl.multiple_of(slot * BLK, BLK)


def pick(refs, index, act):
    if len(refs) == 1:
        act(refs[0])
        return
    half = len(refs) // 2
    lax.cond(
        index < half,
        lambda: pick(refs[:half], index, act),
        lambda: pick(refs[half:], index - half, act),
    )


def pack_kernel(first, entries, late, asked, *refs):
    pieces, out = refs[:-1], refs[-1]
    blocks = pieces[0].shape[0] // BLK
    me = lax.axis_index("tm")

    def body(e, _):
        core, piece, row = place_of(asked, first + e, me, blocks, False)
        target = pl.ds(pl.multiple_of(e * BLK, BLK), BLK)

        @pl.when(jnp.logical_and(core, piece != late))
        def _():
            def act(ref):
                out[target] = ref[pl.ds(row, BLK)]

            pick(pieces, jnp.where(piece < late, piece, piece - 1), act)

        return 0

    lax.fori_loop(0, entries, body, 0)


def session_kernel(
    entries, group, late, ids, mask, smoothed, recorded, packed, packed_rest, late_theirs, *refs
):
    pieces = refs[:-5]
    grad, far_side, terms, rows, resid = refs[-5:]
    blocks = pieces[0].shape[0] // BLK
    bins = smoothed.shape[1]
    top = ids.shape[1]
    me = lax.axis_index("tm")
    grad[...] = jnp.zeros_like(grad)
    depth = group * BLK

    def step(g, _):
        for i in range(group):
            e = g * group + i
            core, piece, row = place_of(ids, e, me, blocks, False)

            def own():
                def act(ref):
                    rows[i * BLK : (i + 1) * BLK] = ref[pl.ds(row, BLK)]

                pick(pieces, piece, act)

            def other():
                @pl.when(piece == late)
                def _():
                    rows[i * BLK : (i + 1) * BLK] = late_theirs[pl.ds(row, BLK)]

                @pl.when(piece != late)
                def _():
                    def act(ref):
                        source = pl.ds(pl.multiple_of(remainder(e, entries // 2) * BLK, BLK), BLK)
                        rows[i * BLK : (i + 1) * BLK] = ref[source]

                    pick((packed, packed_rest), divide(e, entries // 2), act)

            lax.cond(core, own, other)
        block = rows[...]
        predicted = jnp.dot(block, smoothed[...], preferred_element_type=F32)
        for i in range(group):
            e = g * group + i
            for t in range(bins // BLK):
                cut = slice(t * BLK, (t + 1) * BLK)
                weight = mask[divide(e, top), t, remainder(e, top)].astype(F32)
                part = predicted[i * BLK : (i + 1) * BLK, cut]
                seen = recorded[e, :, cut].astype(F32)
                resid[i * BLK : (i + 1) * BLK, cut] = (weight * (part - seen)).astype(BF16)
        term = lax.dot_general(
            resid[...], smoothed[...], (((1,), (1,)), ((), ())), preferred_element_type=F32
        )
        target = pl.ds(pl.multiple_of(g * depth, depth), depth)
        terms[target] = (term * (1.0 / BLK)).astype(BF16)
        grad[...] += lax.dot_general(
            block, resid[...], (((0,), (0,)), ((), ())), preferred_element_type=F32
        ) * (1.0 / BLK)
        return 0

    lax.fori_loop(0, entries // group, step, 0)
    latent_dim, width = grad.shape[0], rows.shape[1] // 2
    even = me & 1 == 0
    later, earlier = grad[:, bins - width :], grad[:, :width]
    core_edge, far_edge = jnp.where(even, later, earlier), jnp.where(even, earlier, later)
    terms[pl.ds(entries * BLK, latent_dim)] = jnp.concatenate(parts(core_edge), axis=1)
    far_side[...] = jnp.concatenate(parts(far_edge), axis=1)


def merge_late_kernel(entries, late, ids, asked, own, got, out, sums):
    blocks = out.shape[0] // BLK
    me = lax.axis_index("tm")
    sums[...] = jnp.zeros_like(sums)

    def add(e, _):
        source = pl.ds(pl.multiple_of(e * BLK, BLK), BLK)
        for names, terms in ((ids, own), (asked, got)):
            core, piece, row = place_of(names, e, me, blocks, True)

            @pl.when(jnp.logical_and(core, piece == late))
            def _():
                sums[pl.ds(row, BLK)] += terms[source].astype(F32)

        return 0

    lax.fori_loop(0, entries, add, 0)
    out[...] = sums[...].astype(out.dtype)


def merge_kernel(entries, late, ids, asked, own, got, *refs):
    chain = len(refs) // 2
    kept, outs, sums = refs[:chain], refs[chain:-1], refs[-1]
    chunk = kept[0].shape[0]
    me = lax.axis_index("tm")
    for ref in kept:
        ref[...] = jnp.zeros_like(ref)
    sums[...] = jnp.zeros_like(sums)

    def add(e, _):
        source = pl.ds(pl.multiple_of(e * BLK, BLK), BLK)
        for names, terms in ((ids, own), (asked, got)):
            core, piece, row = place_of(names, e, me, chunk // BLK, True)
            index = jnp.where(piece < late, piece - chain, piece - 1 - chain)

            @pl.when(jnp.logical_and(core, piece < chain))
            def _():
                def act(ref):
                    ref[pl.ds(row, BLK)] += terms[source].astype(F32)

                pick(kept, piece, act)

            @pl.when(jnp.logical_and(core, jnp.logical_and(piece >= chain, piece != late)))
            def _():
                sums[pl.ds(pl.multiple_of(index * chunk + row, BLK), BLK)] += terms[source].astype(F32)

        return 0

    lax.fori_loop(0, entries, add, 0)
    for q, out in enumerate(outs):
        out[...] = sums[q * chunk : (q + 1) * chunk].astype(out.dtype)


def hop_kernel(total, *refs):
    out = refs[-1]
    value = total[...]
    for came in refs[:-1]:
        value += came[...].astype(F32)
    out[...] = value.astype(out.dtype)


def local(latents, kernel, loadings, recorded, owner_ids, local_ids, recorded_mask):
    latent_dim, bins = latents.shape
    halfwidth = kernel.shape[1] // 2
    count = lax.axis_size("tm")
    chain = count // ROW
    chunk = loadings.shape[0]
    entries = owner_ids.size
    piece_bytes = count * chunk * latent_dim
    smem = pl.BlockSpec(memory_space=pltpu.SMEM)

    def permute(x, pairs):
        return lax.ppermute(x, "tm", pairs)

    def rotate(x, r):
        return permute(x, [(i, (i + r * ROW) % count) for i in range(count)])

    def flip(x, bit):
        return permute(x, [(i, i ^ bit) for i in range(count)])

    odd_even = [(i, i + 1) for i in range(1, count - 1, 2)]
    odd_even += [(target, source) for source, target in odd_even]

    ids = owner_ids[0] * (chunk // BLK) + local_ids[0]
    asked = flip(ids, 1)
    mask = jnp.transpose(recorded_mask, (0, 2, 1))

    even = lax.axis_index("tm") % 2 == 0
    later, earlier = latents[:, bins - halfwidth :], latents[:, :halfwidth]
    core_side = flip(jnp.where(even, later, earlier), 1)
    far_side = permute(jnp.where(even, earlier, later), odd_even)

    half = chain // 2
    late, late_sum = 2 * chain - 1, chain + half
    straight = [loadings] * chain
    straight[1] = rotate(loadings, 1)
    across = [flip(loadings, 2)] + [None] * (chain - 1)
    straight[1], across[0], core_side, far_side = lax.optimization_barrier(
        (straight[1], across[0], core_side, far_side)
    )
    for r in range(2, half + 1):
        straight[r] = rotate(straight[r - 1], 1)
    straight[1], kernel = lax.optimization_barrier((straight[1], kernel))
    table = dft_tables(2 * halfwidth)
    mxu = 30 * 2 * latent_dim * (2 * halfwidth) ** 2
    square = jax.ShapeDtypeStruct((latent_dim, 2 * halfwidth), F32)
    prepared = pl.pallas_call(
        prepare_kernel,
        out_shape=(
            jax.ShapeDtypeStruct(table.shape, BF16),
            jax.ShapeDtypeStruct(latents.shape, F32),
        )
        + (square,) * 3,
        in_specs=[HBM] * 3,
        out_specs=(VMEM,) * 5,
        scratch_shapes=[pltpu.VMEM(kernel.shape, F32), pltpu.SemaphoreType.DMA((8,))],
        compiler_params=pltpu.CompilerParams(vmem_limit_bytes=50 * MIB),
        cost_estimate=pl.CostEstimate(flops=mxu // 3, bytes_accessed=4 * MIB, transcendentals=0),
        name="prepare",
    )(table, kernel, latents)
    other_way, *prepared = lax.optimization_barrier((loadings, *prepared))
    spectrum, held_bins = [prepared[0], *prepared[2:]], prepared[1]
    for r in range(1, half):
        other_way = straight[-r] = rotate(other_way, -1)
    for r in range(1, chain):
        across[r] = flip(straight[r], 2)
    pieces = straight + across
    early = pieces[:late] + pieces[late + 1 :]

    smoothed = pl.pallas_call(
        smooth_kernel,
        out_shape=jax.ShapeDtypeStruct((latent_dim, bins), BF16),
        in_specs=[VMEM] * 7,
        out_specs=VMEM,
        compiler_params=pltpu.CompilerParams(vmem_limit_bytes=16 * MIB),
        cost_estimate=pl.CostEstimate(flops=mxu, bytes_accessed=4 * MIB, transcendentals=0),
        name="smooth",
    )(held_bins, core_side, far_side, *spectrum)

    slots = jax.ShapeDtypeStruct((entries * BLK, latent_dim), BF16)

    def pack(first, total):
        return pl.pallas_call(
            functools.partial(pack_kernel, first, total, late),
            out_shape=jax.ShapeDtypeStruct((total * BLK, latent_dim), BF16),
            in_specs=[smem] + [VMEM] * len(early),
            out_specs=VMEM,
            compiler_params=pltpu.CompilerParams(vmem_limit_bytes=4 * MIB + 3 * piece_bytes),
            cost_estimate=pl.CostEstimate(flops=0, bytes_accessed=2**20, transcendentals=0),
            name="pack",
        )(asked, *early)

    asked, smoothed, mask = lax.optimization_barrier((asked, smoothed, mask))
    packed = [flip(pack(first, entries // 2), 1) for first in (0, entries // 2)]
    pieces[late], smoothed = lax.optimization_barrier((pieces[late], smoothed))
    late_theirs = flip(pieces[late], 1)

    group = 4
    extended = jax.ShapeDtypeStruct((entries * BLK + latent_dim, latent_dim), BF16)
    grad, far_side, terms = pl.pallas_call(
        functools.partial(session_kernel, entries, group, late),
        out_shape=(
            jax.ShapeDtypeStruct((latent_dim, bins), F32),
            jax.ShapeDtypeStruct((latent_dim, 2 * halfwidth), BF16),
            extended,
        ),
        in_specs=[smem] * 2 + [VMEM] * (5 + len(pieces)),
        out_specs=(VMEM,) * 3,
        scratch_shapes=[
            pltpu.VMEM((group * BLK, latent_dim), BF16),
            pltpu.VMEM((group * BLK, bins), BF16),
        ],
        compiler_params=pltpu.CompilerParams(vmem_limit_bytes=12 * MIB + 6 * piece_bytes),
        cost_estimate=pl.CostEstimate(
            flops=6 * entries * BLK * latent_dim * bins, bytes_accessed=8 * 2**20, transcendentals=0
        ),
        name="session",
    )(
        ids,
        mask,
        smoothed,
        recorded.reshape(entries, BLK, bins),
        *packed,
        late_theirs,
        *pieces,
    )

    got = flip(terms, 1)
    narrow = jax.ShapeDtypeStruct((chunk, latent_dim), BF16)
    sent = pl.pallas_call(
        functools.partial(merge_late_kernel, entries, late_sum),
        out_shape=narrow,
        in_specs=[smem] * 2 + [VMEM] * 2,
        out_specs=VMEM,
        scratch_shapes=[pltpu.VMEM((chunk, latent_dim), F32)],
        compiler_params=pltpu.CompilerParams(vmem_limit_bytes=4 * MIB + 3 * piece_bytes),
        cost_estimate=pl.CostEstimate(flops=0, bytes_accessed=2**20, transcendentals=0),
        name="merge_late",
    )(ids, asked, terms, got)
    wide = jax.ShapeDtypeStruct((chunk, latent_dim), F32)
    sent, ids = lax.optimization_barrier((sent, ids))
    back = flip(sent, 2)
    merged = pl.pallas_call(
        functools.partial(merge_kernel, entries, late_sum),
        out_shape=(wide,) * chain + (narrow,) * (chain - 1),
        in_specs=[smem] * 2 + [VMEM] * 2,
        out_specs=(VMEM,) * (2 * chain - 1),
        scratch_shapes=[pltpu.VMEM(((chain - 1) * chunk, latent_dim), F32)],
        compiler_params=pltpu.CompilerParams(vmem_limit_bytes=4 * MIB + 6 * piece_bytes),
        cost_estimate=pl.CostEstimate(flops=0, bytes_accessed=5 * 2**20, transcendentals=0),
        name="merge",
    )(ids, asked, terms, got)
    crossed = {r: merged[chain + r - (r > half)] for r in range(chain) if r != half}
    other = {r: flip(part, 2) for r, part in crossed.items() if r}

    def hop(total, *came):
        return pl.pallas_call(
            hop_kernel,
            out_shape=narrow,
            in_specs=[VMEM] * (1 + len(came)),
            out_specs=VMEM,
            compiler_params=pltpu.CompilerParams(vmem_limit_bytes=8 * MIB),
            cost_estimate=pl.CostEstimate(flops=0, bytes_accessed=MIB, transcendentals=0),
            name="hop",
        )(total, *came)

    rise = hop(merged[half], back)
    rise, far_side = lax.optimization_barrier((rise, far_side))
    far_side = permute(far_side, odd_even)
    far_side, own = lax.optimization_barrier((far_side, crossed[0]))
    other[0] = flip(own, 2)
    rise = rotate(rise, 1)
    for r in range(half - 1, 0, -1):
        rise = rotate(hop(merged[r], other[r], rise), 1)
    fall = rotate(hop(merged[half + 1], other[half + 1]), -1)
    for r in range(half + 2, chain):
        fall = rotate(hop(merged[r], other[r], fall), -1)
    loading_grad = merged[0] + other[0].astype(F32) + rise.astype(F32) + fall.astype(F32)

    latent_grad = pl.pallas_call(
        unsmooth_kernel,
        out_shape=jax.ShapeDtypeStruct((latent_dim, bins), F32),
        in_specs=[VMEM] * 7,
        out_specs=VMEM,
        compiler_params=pltpu.CompilerParams(vmem_limit_bytes=16 * MIB),
        cost_estimate=pl.CostEstimate(flops=mxu, bytes_accessed=4 * MIB, transcendentals=0),
        name="unsmooth",
    )(grad, got, far_side, *spectrum)
    return latent_grad, loading_grad


def solution(mesh):
    return jax.shard_map(
        local,
        mesh=mesh,
        in_specs=(
            P(None, ("groups", "tm")),
            P(),
            P(("groups", "tm"), None),
            P(None, None, None, ("groups", "tm")),
            P(("groups", "tm"), None, None),
            P(("groups", "tm"), None, None),
            P(None, None, ("groups", "tm")),
        ),
        out_specs=(P(None, ("groups", "tm")), P(("groups", "tm"), None)),
        check_vma=False,
    )
```

```python
import functools

import jax
import jax.numpy as jnp
import numpy as np
from jax import lax
from jax.experimental import pallas as pl
from jax.experimental.pallas import tpu as pltpu
from jax.sharding import PartitionSpec as P

BLK = 128
ROW = 4
MIB = 2**20
F32 = jnp.float32
BF16 = jnp.bfloat16
VMEM = pl.BlockSpec(memory_space=pltpu.VMEM)
HBM = pl.BlockSpec(memory_space=pltpu.HBM)


def split_const(a):
    high = a.astype(jnp.bfloat16)
    low = (a - high.astype(np.float64)).astype(jnp.bfloat16)
    return high, low


@functools.lru_cache(maxsize=None)
def dft_tables(size):
    t = np.arange(size)[:, None]
    g = np.arange(size)[None, :]
    half = size // 2
    angle = 2 * np.pi * ((t * g[:, :half]) % size) / size
    cos, sin = np.cos(angle), np.sin(angle)
    sin[:, 0] = 1 - 2 * (np.arange(size) % 2)
    real = np.concatenate([cos, sin], axis=1)
    angle = 2 * np.pi * ((t * (3 * g + 1)) % (3 * size)) / (3 * size)
    cos, sin = np.cos(angle), np.sin(angle)
    weight = np.full((size,), 2.0)
    weight[0] = weight[half] = 1.0
    scale = 1.0 / (3 * size)
    tables = [real, cos, sin, (real * weight).T * scale, cos.T * 2 * scale, sin.T * 2 * scale]
    return np.concatenate([part for table in tables for part in split_const(table)])


def parts(a):
    high = a.astype(BF16)
    return high, (a - high.astype(F32)).astype(BF16)


def times(a, tables, index):
    rows, size = a.shape
    high, low = parts(a)
    first = 2 * index * size
    t_high, t_low = tables[first : first + size], tables[first + size : first + 2 * size]
    out = jnp.dot(jnp.concatenate([high, low]), t_high, preferred_element_type=F32)
    return out[:rows] + out[rows:] + jnp.dot(high, t_low, preferred_element_type=F32)


ROOT = 0.75**0.5


def spectrum_of(thirds, tables):
    first, second, third = thirds
    rows = first.shape[0]
    base = times(first + second + third, tables, 0)
    y = jnp.concatenate([first - 0.5 * (second + third), ROOT * (third - second)])
    cos, sin = times(y, tables, 1), times(y, tables, 2)
    return base, cos[:rows] + sin[rows:], cos[rows:] - sin[:rows]


def filtered(signal, taps, sign, tables, wanted):
    (xb, xr, xi), (kb, kr, ki) = signal, taps
    rows, size = xb.shape
    half = size // 2
    first = lax.broadcasted_iota(jnp.int32, (rows, half), 1) == 0
    kc, ks = kb[:, :half], kb[:, half:]
    kc_s = jnp.where(first, ks, kc)
    ks_x = jnp.where(first, 0.0, ks) * sign
    xc, xs = xb[:, :half], xb[:, half:]
    base = times(jnp.concatenate([xc * kc + xs * ks_x, xs * kc_s - xc * ks_x], axis=1), tables, 3)
    ki = ki * sign
    z = jnp.concatenate([xr * kr + xi * ki, xi * kr - xr * ki])
    cos, sin = times(z, tables, 4), times(z, tables, 5)
    vr, vi = cos[:rows] - sin[rows:], sin[:rows] + cos[rows:]
    each = (base + vr, base - 0.5 * vr - ROOT * vi, base - 0.5 * vr + ROOT * vi)
    return jnp.concatenate([each[m] for m in wanted], axis=1)


def thirds_of(mid, core_side, far_side):
    width = core_side.shape[1]
    size = 2 * width
    even = lax.rem(lax.axis_index("tm"), 2) == 0
    low, high = jnp.where(even, far_side, core_side), jnp.where(even, core_side, far_side)
    last = mid.shape[1] - width
    return (
        jnp.concatenate([low, mid[:, :width]], axis=1),
        mid[:, width : width + size],
        jnp.concatenate([mid[:, last:], high], axis=1),
    )


def prepare_kernel(table, taps, mid, tables, bins, base, kr, ki, held, sem):
    rows = table.shape[0] // 6
    cuts = [pl.ds(i * rows, rows) for i in range(6)]
    copies = [pltpu.make_async_copy(taps, held, sem.at[0])]
    copies += [
        pltpu.make_async_copy(table.at[cut], tables.at[cut], sem.at[1 + i])
        for i, cut in enumerate(cuts)
    ]
    copies += [pltpu.make_async_copy(mid, bins, sem.at[7])]
    for copy in copies:
        copy.start()
    copies[0].wait()
    for i, (ref, sign) in enumerate(((base, 1.0), (kr, 1.0), (ki, -1.0))):
        copies[1 + i].wait()
        ref[...] = times(held[...], tables, i) * sign
    for copy in copies[4:]:
        copy.wait()


def smooth_kernel(mid, core_side, far_side, tables, base, kr, ki, out):
    thirds = thirds_of(mid[...], core_side[...], far_side[...])
    signal = spectrum_of(thirds, tables)
    taps = (base[...], kr[...], ki[...])
    out[...] = filtered(signal, taps, 1.0, tables, (0, 1)).astype(out.dtype)


def unsmooth_kernel(mid, got, far_side, tables, base, kr, ki, out):
    width = far_side.shape[1] // 2
    core = got[got.shape[0] - far_side.shape[0] :].astype(F32)
    far = far_side[...].astype(F32)
    thirds = thirds_of(
        mid[...], core[:, :width] + core[:, width:], far[:, :width] + far[:, width:]
    )
    signal = spectrum_of(thirds, tables)
    taps = (base[...], kr[...], ki[...])
    out[...] = filtered(signal, taps, -1.0, tables, (1, 2))


def divide(a, n):
    return a >> (n.bit_length() - 1) if n & (n - 1) == 0 else a // n


def remainder(a, n):
    return a & (n - 1) if n & (n - 1) == 0 else a % n


def place_of(ids, e, me, blocks, forward):
    chain = lax.axis_size("tm") // ROW
    top = ids.shape[1]
    code = ids[divide(e, top), remainder(e, top)]
    owner, slot = divide(code, blocks), remainder(code, blocks)
    step = divide(owner, ROW) - divide(me, ROW)
    step = step if forward else -step
    turn = jnp.where(step < 0, step + chain, step)
    differ = owner ^ me
    piece = jnp.where(differ & 2 == 0, 0, chain) + turn
    return differ & 1 == 0, piece, pl.multiple_of(slot * BLK, BLK)


def pick(refs, index, act):
    if len(refs) == 1:
        act(refs[0])
        return
    half = len(refs) // 2
    lax.cond(
        index < half,
        lambda: pick(refs[:half], index, act),
        lambda: pick(refs[half:], index - half, act),
    )


def pack_kernel(first, entries, late, asked, *refs):
    pieces, out = refs[:-1], refs[-1]
    blocks = pieces[0].shape[0] // BLK
    me = lax.axis_index("tm")

    def body(e, _):
        core, piece, row = place_of(asked, first + e, me, blocks, False)
        target = pl.ds(pl.multiple_of(e * BLK, BLK), BLK)

        @pl.when(jnp.logical_and(core, piece != late))
        def _():
            def act(ref):
                out[target] = ref[pl.ds(row, BLK)]

            pick(pieces, jnp.where(piece < late, piece, piece - 1), act)

        return 0

    lax.fori_loop(0, entries, body, 0)


def session_kernel(
    entries, group, late, ids, mask, smoothed, recorded, packed, packed_rest, late_theirs, *refs
):
    pieces = refs[:-5]
    grad, far_side, terms, rows, resid = refs[-5:]
    blocks = pieces[0].shape[0] // BLK
    bins = smoothed.shape[1]
    top = ids.shape[1]
    me = lax.axis_index("tm")
    grad[...] = jnp.zeros_like(grad)
    depth = group * BLK

    def step(g, _):
        for i in range(group):
            e = g * group + i
            core, piece, row = place_of(ids, e, me, blocks, False)

            def own():
                def act(ref):
                    rows[i * BLK : (i + 1) * BLK] = ref[pl.ds(row, BLK)]

                pick(pieces, piece, act)

            def other():
                @pl.when(piece == late)
                def _():
                    rows[i * BLK : (i + 1) * BLK] = late_theirs[pl.ds(row, BLK)]

                @pl.when(piece != late)
                def _():
                    def act(ref):
                        source = pl.ds(pl.multiple_of(remainder(e, entries // 2) * BLK, BLK), BLK)
                        rows[i * BLK : (i + 1) * BLK] = ref[source]

                    pick((packed, packed_rest), divide(e, entries // 2), act)

            lax.cond(core, own, other)
        block = rows[...]
        predicted = jnp.dot(block, smoothed[...], preferred_element_type=F32)
        for i in range(group):
            e = g * group + i
            for t in range(bins // BLK):
                cut = slice(t * BLK, (t + 1) * BLK)
                weight = mask[divide(e, top), t, remainder(e, top)].astype(F32)
                part = predicted[i * BLK : (i + 1) * BLK, cut]
                seen = recorded[e, :, cut].astype(F32)
                resid[i * BLK : (i + 1) * BLK, cut] = (weight * (part - seen)).astype(BF16)
        term = lax.dot_general(
            resid[...], smoothed[...], (((1,), (1,)), ((), ())), preferred_element_type=F32
        )
        target = pl.ds(pl.multiple_of(g * depth, depth), depth)
        terms[target] = (term * (1.0 / BLK)).astype(BF16)
        grad[...] += lax.dot_general(
            block, resid[...], (((0,), (0,)), ((), ())), preferred_element_type=F32
        ) * (1.0 / BLK)
        return 0

    lax.fori_loop(0, entries // group, step, 0)
    latent_dim, width = grad.shape[0], rows.shape[1] // 2
    even = me & 1 == 0
    later, earlier = grad[:, bins - width :], grad[:, :width]
    core_edge, far_edge = jnp.where(even, later, earlier), jnp.where(even, earlier, later)
    terms[pl.ds(entries * BLK, latent_dim)] = jnp.concatenate(parts(core_edge), axis=1)
    far_side[...] = jnp.concatenate(parts(far_edge), axis=1)


def merge_late_kernel(entries, late, ids, asked, own, got, out, sums):
    blocks = out.shape[0] // BLK
    me = lax.axis_index("tm")
    sums[...] = jnp.zeros_like(sums)

    def add(e, _):
        source = pl.ds(pl.multiple_of(e * BLK, BLK), BLK)
        for names, terms in ((ids, own), (asked, got)):
            core, piece, row = place_of(names, e, me, blocks, True)

            @pl.when(jnp.logical_and(core, piece == late))
            def _():
                sums[pl.ds(row, BLK)] += terms[source].astype(F32)

        return 0

    lax.fori_loop(0, entries, add, 0)
    out[...] = sums[...].astype(out.dtype)


def merge_kernel(entries, late, ids, asked, own, got, *refs):
    chain = len(refs) // 2
    kept, outs, sums = refs[:chain], refs[chain:-1], refs[-1]
    chunk = kept[0].shape[0]
    me = lax.axis_index("tm")
    for ref in kept:
        ref[...] = jnp.zeros_like(ref)
    sums[...] = jnp.zeros_like(sums)

    def add(e, _):
        source = pl.ds(pl.multiple_of(e * BLK, BLK), BLK)
        for names, terms in ((ids, own), (asked, got)):
            core, piece, row = place_of(names, e, me, chunk // BLK, True)
            index = jnp.where(piece < late, piece - chain, piece - 1 - chain)

            @pl.when(jnp.logical_and(core, piece < chain))
            def _():
                def act(ref):
                    ref[pl.ds(row, BLK)] += terms[source].astype(F32)

                pick(kept, piece, act)

            @pl.when(jnp.logical_and(core, jnp.logical_and(piece >= chain, piece != late)))
            def _():
                sums[pl.ds(pl.multiple_of(index * chunk + row, BLK), BLK)] += terms[source].astype(F32)

        return 0

    lax.fori_loop(0, entries, add, 0)
    for q, out in enumerate(outs):
        out[...] = sums[q * chunk : (q + 1) * chunk].astype(out.dtype)


def hop_kernel(total, *refs):
    out = refs[-1]
    value = total[...]
    for came in refs[:-1]:
        value += came[...].astype(F32)
    out[...] = value.astype(out.dtype)


def local(latents, kernel, loadings, recorded, owner_ids, local_ids, recorded_mask):
    latent_dim, bins = latents.shape
    halfwidth = kernel.shape[1] // 2
    count = lax.axis_size("tm")
    chain = count // ROW
    chunk = loadings.shape[0]
    entries = owner_ids.size
    piece_bytes = count * chunk * latent_dim
    smem = pl.BlockSpec(memory_space=pltpu.SMEM)

    def permute(x, pairs):
        return lax.ppermute(x, "tm", pairs)

    def rotate(x, r):
        return permute(x, [(i, (i + r * ROW) % count) for i in range(count)])

    def flip(x, bit):
        return permute(x, [(i, i ^ bit) for i in range(count)])

    odd_even = [(i, i + 1) for i in range(1, count - 1, 2)]
    odd_even += [(target, source) for source, target in odd_even]

    ids = owner_ids[0] * (chunk // BLK) + local_ids[0]
    asked = flip(ids, 1)
    mask = jnp.transpose(recorded_mask, (0, 2, 1))

    even = lax.axis_index("tm") % 2 == 0
    later, earlier = latents[:, bins - halfwidth :], latents[:, :halfwidth]
    core_side = flip(jnp.where(even, later, earlier), 1)
    far_side = permute(jnp.where(even, earlier, later), odd_even)

    half = chain // 2
    late = chain + half
    straight = [loadings] * chain
    for r in range(1, half):
        straight[r] = rotate(straight[r - 1], 1)
        straight[-r] = rotate(straight[1 - r], -1)
    across = [flip(loadings, 2)] + [None] * (chain - 1)
    if half > 1:
        straight[1], across[0] = lax.optimization_barrier((straight[1], across[0]))
    straight[half] = rotate(straight[half - 1], 1)
    straight[1], kernel = lax.optimization_barrier((straight[1], kernel))
    table = dft_tables(2 * halfwidth)
    mxu = 30 * 2 * latent_dim * (2 * halfwidth) ** 2
    square = jax.ShapeDtypeStruct((latent_dim, 2 * halfwidth), F32)
    prepared = pl.pallas_call(
        prepare_kernel,
        out_shape=(
            jax.ShapeDtypeStruct(table.shape, BF16),
            jax.ShapeDtypeStruct(latents.shape, F32),
        )
        + (square,) * 3,
        in_specs=[HBM] * 3,
        out_specs=(VMEM,) * 5,
        scratch_shapes=[pltpu.VMEM(kernel.shape, F32), pltpu.SemaphoreType.DMA((8,))],
        compiler_params=pltpu.CompilerParams(vmem_limit_bytes=50 * MIB),
        cost_estimate=pl.CostEstimate(flops=mxu // 3, bytes_accessed=4 * MIB, transcendentals=0),
        name="prepare",
    )(table, kernel, latents)
    straight[-1], *prepared = lax.optimization_barrier((straight[-1], *prepared))
    spectrum, held_bins = [prepared[0], *prepared[2:]], prepared[1]
    for r in range(1, chain):
        if r != half:
            across[r] = flip(straight[r], 2)

    smoothed = pl.pallas_call(
        smooth_kernel,
        out_shape=jax.ShapeDtypeStruct((latent_dim, bins), BF16),
        in_specs=[VMEM] * 7,
        out_specs=VMEM,
        compiler_params=pltpu.CompilerParams(vmem_limit_bytes=16 * MIB),
        cost_estimate=pl.CostEstimate(flops=mxu, bytes_accessed=4 * MIB, transcendentals=0),
        name="smooth",
    )(held_bins, core_side, far_side, *spectrum)

    slots = jax.ShapeDtypeStruct((entries * BLK, latent_dim), BF16)
    across[half] = flip(straight[half], 2)
    early = straight + across[:half] + across[half + 1 :]

    def pack(first, total):
        return pl.pallas_call(
            functools.partial(pack_kernel, first, total, late),
            out_shape=jax.ShapeDtypeStruct((total * BLK, latent_dim), BF16),
            in_specs=[smem] + [VMEM] * len(early),
            out_specs=VMEM,
            compiler_params=pltpu.CompilerParams(vmem_limit_bytes=4 * MIB + 3 * piece_bytes),
            cost_estimate=pl.CostEstimate(flops=0, bytes_accessed=2**20, transcendentals=0),
            name="pack",
        )(asked, *early)

    asked, smoothed, mask = lax.optimization_barrier((asked, smoothed, mask))
    packed = [flip(pack(first, entries // 2), 1) for first in (0, entries // 2)]
    last, smoothed = lax.optimization_barrier((across[half], smoothed))
    late_theirs = flip(last, 1)
    pieces = straight + across

    group = 4
    extended = jax.ShapeDtypeStruct((entries * BLK + latent_dim, latent_dim), BF16)
    grad, far_side, terms = pl.pallas_call(
        functools.partial(session_kernel, entries, group, late),
        out_shape=(
            jax.ShapeDtypeStruct((latent_dim, bins), F32),
            jax.ShapeDtypeStruct((latent_dim, 2 * halfwidth), BF16),
            extended,
        ),
        in_specs=[smem] * 2 + [VMEM] * (5 + len(pieces)),
        out_specs=(VMEM,) * 3,
        scratch_shapes=[
            pltpu.VMEM((group * BLK, latent_dim), BF16),
            pltpu.VMEM((group * BLK, bins), BF16),
        ],
        compiler_params=pltpu.CompilerParams(vmem_limit_bytes=12 * MIB + 6 * piece_bytes),
        cost_estimate=pl.CostEstimate(
            flops=6 * entries * BLK * latent_dim * bins, bytes_accessed=8 * 2**20, transcendentals=0
        ),
        name="session",
    )(
        ids,
        mask,
        smoothed,
        recorded.reshape(entries, BLK, bins),
        *packed,
        late_theirs,
        *pieces,
    )

    got = flip(terms, 1)
    narrow = jax.ShapeDtypeStruct((chunk, latent_dim), BF16)
    sent = pl.pallas_call(
        functools.partial(merge_late_kernel, entries, late),
        out_shape=narrow,
        in_specs=[smem] * 2 + [VMEM] * 2,
        out_specs=VMEM,
        scratch_shapes=[pltpu.VMEM((chunk, latent_dim), F32)],
        compiler_params=pltpu.CompilerParams(vmem_limit_bytes=4 * MIB + 3 * piece_bytes),
        cost_estimate=pl.CostEstimate(flops=0, bytes_accessed=2**20, transcendentals=0),
        name="merge_late",
    )(ids, asked, terms, got)
    wide = jax.ShapeDtypeStruct((chunk, latent_dim), F32)
    sent, ids = lax.optimization_barrier((sent, ids))
    back = flip(sent, 2)
    merged = pl.pallas_call(
        functools.partial(merge_kernel, entries, late),
        out_shape=(wide,) * chain + (narrow,) * (chain - 1),
        in_specs=[smem] * 2 + [VMEM] * 2,
        out_specs=(VMEM,) * (2 * chain - 1),
        scratch_shapes=[pltpu.VMEM(((chain - 1) * chunk, latent_dim), F32)],
        compiler_params=pltpu.CompilerParams(vmem_limit_bytes=4 * MIB + 6 * piece_bytes),
        cost_estimate=pl.CostEstimate(flops=0, bytes_accessed=5 * 2**20, transcendentals=0),
        name="merge",
    )(ids, asked, terms, got)
    crossed = {r: merged[chain + r - (r > half)] for r in range(chain) if r != half}
    back, *held = lax.optimization_barrier((back, *(crossed[r] for r in range(1, half))))
    other = {r: flip(part, 2) for r, part in enumerate(held, 1)}
    for r in range(half + 1, chain):
        other[r] = flip(crossed[r], 2)

    def hop(total, *came):
        return pl.pallas_call(
            hop_kernel,
            out_shape=narrow,
            in_specs=[VMEM] * (1 + len(came)),
            out_specs=VMEM,
            compiler_params=pltpu.CompilerParams(vmem_limit_bytes=8 * MIB),
            cost_estimate=pl.CostEstimate(flops=0, bytes_accessed=MIB, transcendentals=0),
            name="hop",
        )(total, *came)

    rise = hop(merged[half], back)
    rise, far_side = lax.optimization_barrier((rise, far_side))
    far_side = permute(far_side, odd_even)
    far_side, own = lax.optimization_barrier((far_side, crossed[0]))
    other[0] = flip(own, 2)
    rise = rotate(rise, 1)
    for r in range(half - 1, 0, -1):
        rise = rotate(hop(merged[r], other[r], rise), 1)
    fall = rotate(hop(merged[half + 1], other[half + 1]), -1)
    for r in range(half + 2, chain):
        fall = rotate(hop(merged[r], other[r], fall), -1)
    loading_grad = merged[0] + other[0].astype(F32) + rise.astype(F32) + fall.astype(F32)

    latent_grad = pl.pallas_call(
        unsmooth_kernel,
        out_shape=jax.ShapeDtypeStruct((latent_dim, bins), F32),
        in_specs=[VMEM] * 7,
        out_specs=VMEM,
        compiler_params=pltpu.CompilerParams(vmem_limit_bytes=16 * MIB),
        cost_estimate=pl.CostEstimate(flops=mxu, bytes_accessed=4 * MIB, transcendentals=0),
        name="unsmooth",
    )(grad, got, far_side, *spectrum)
    return latent_grad, loading_grad


def solution(mesh):
    return jax.shard_map(
        local,
        mesh=mesh,
        in_specs=(
            P(None, ("groups", "tm")),
            P(),
            P(("groups", "tm"), None),
            P(None, None, None, ("groups", "tm")),
            P(("groups", "tm"), None, None),
            P(("groups", "tm"), None, None),
            P(None, None, ("groups", "tm")),
        ),
        out_specs=(P(None, ("groups", "tm")), P(("groups", "tm"), None)),
        check_vma=False,
    )
```

```python
import functools

import jax
import jax.numpy as jnp
import numpy as np
from jax import lax
from jax.experimental import pallas as pl
from jax.experimental.pallas import tpu as pltpu
from jax.sharding import PartitionSpec as P

BLK = 128
ROW = 4
MIB = 2**20
F32 = jnp.float32
BF16 = jnp.bfloat16
VMEM = pl.BlockSpec(memory_space=pltpu.VMEM)
HBM = pl.BlockSpec(memory_space=pltpu.HBM)


def split_const(a):
    high = a.astype(jnp.bfloat16)
    low = (a - high.astype(np.float64)).astype(jnp.bfloat16)
    return high, low


@functools.lru_cache(maxsize=None)
def dft_tables(size):
    t = np.arange(size)[:, None]
    g = np.arange(size)[None, :]
    half = size // 2
    angle = 2 * np.pi * ((t * g[:, :half]) % size) / size
    cos, sin = np.cos(angle), np.sin(angle)
    sin[:, 0] = 1 - 2 * (np.arange(size) % 2)
    real = np.concatenate([cos, sin], axis=1)
    angle = 2 * np.pi * ((t * (3 * g + 1)) % (3 * size)) / (3 * size)
    cos, sin = np.cos(angle), np.sin(angle)
    weight = np.full((size,), 2.0)
    weight[0] = weight[half] = 1.0
    scale = 1.0 / (3 * size)
    tables = [real, cos, sin, (real * weight).T * scale, cos.T * 2 * scale, sin.T * 2 * scale]
    return np.concatenate([part for table in tables for part in split_const(table)])


def parts(a):
    high = a.astype(BF16)
    return high, (a - high.astype(F32)).astype(BF16)


def times(a, tables, index):
    rows, size = a.shape
    high, low = parts(a)
    first = 2 * index * size
    t_high, t_low = tables[first : first + size], tables[first + size : first + 2 * size]
    out = jnp.dot(jnp.concatenate([high, low]), t_high, preferred_element_type=F32)
    return out[:rows] + out[rows:] + jnp.dot(high, t_low, preferred_element_type=F32)


ROOT = 0.75**0.5


def spectrum_of(thirds, tables):
    first, second, third = thirds
    rows = first.shape[0]
    base = times(first + second + third, tables, 0)
    y = jnp.concatenate([first - 0.5 * (second + third), ROOT * (third - second)])
    cos, sin = times(y, tables, 1), times(y, tables, 2)
    return base, cos[:rows] + sin[rows:], cos[rows:] - sin[:rows]


def filtered(signal, taps, sign, tables, wanted):
    (xb, xr, xi), (kb, kr, ki) = signal, taps
    rows, size = xb.shape
    half = size // 2
    first = lax.broadcasted_iota(jnp.int32, (rows, half), 1) == 0
    kc, ks = kb[:, :half], kb[:, half:]
    kc_s = jnp.where(first, ks, kc)
    ks_x = jnp.where(first, 0.0, ks) * sign
    xc, xs = xb[:, :half], xb[:, half:]
    base = times(jnp.concatenate([xc * kc + xs * ks_x, xs * kc_s - xc * ks_x], axis=1), tables, 3)
    ki = ki * sign
    z = jnp.concatenate([xr * kr + xi * ki, xi * kr - xr * ki])
    cos, sin = times(z, tables, 4), times(z, tables, 5)
    vr, vi = cos[:rows] - sin[rows:], sin[:rows] + cos[rows:]
    each = (base + vr, base - 0.5 * vr - ROOT * vi, base - 0.5 * vr + ROOT * vi)
    return jnp.concatenate([each[m] for m in wanted], axis=1)


def thirds_of(mid, core_side, far_side):
    width = core_side.shape[1]
    size = 2 * width
    even = lax.rem(lax.axis_index("tm"), 2) == 0
    low, high = jnp.where(even, far_side, core_side), jnp.where(even, core_side, far_side)
    last = mid.shape[1] - width
    return (
        jnp.concatenate([low, mid[:, :width]], axis=1),
        mid[:, width : width + size],
        jnp.concatenate([mid[:, last:], high], axis=1),
    )


def prepare_kernel(table, taps, mid, tables, bins, base, kr, ki, held, sem):
    rows = table.shape[0] // 6
    cuts = [pl.ds(i * rows, rows) for i in range(6)]
    copies = [pltpu.make_async_copy(taps, held, sem.at[0])]
    copies += [
        pltpu.make_async_copy(table.at[cut], tables.at[cut], sem.at[1 + i])
        for i, cut in enumerate(cuts)
    ]
    copies += [pltpu.make_async_copy(mid, bins, sem.at[7])]
    for copy in copies:
        copy.start()
    copies[0].wait()
    for i, (ref, sign) in enumerate(((base, 1.0), (kr, 1.0), (ki, -1.0))):
        copies[1 + i].wait()
        ref[...] = times(held[...], tables, i) * sign
    for copy in copies[4:]:
        copy.wait()


def smooth_kernel(mid, core_side, far_side, tables, base, kr, ki, out):
    thirds = thirds_of(mid[...], core_side[...], far_side[...])
    signal = spectrum_of(thirds, tables)
    taps = (base[...], kr[...], ki[...])
    out[...] = filtered(signal, taps, 1.0, tables, (0, 1)).astype(out.dtype)


def unsmooth_kernel(mid, got, far_side, tables, base, kr, ki, out):
    width = far_side.shape[1] // 2
    core = got[got.shape[0] - far_side.shape[0] :].astype(F32)
    far = far_side[...].astype(F32)
    thirds = thirds_of(
        mid[...], core[:, :width] + core[:, width:], far[:, :width] + far[:, width:]
    )
    signal = spectrum_of(thirds, tables)
    taps = (base[...], kr[...], ki[...])
    out[...] = filtered(signal, taps, -1.0, tables, (1, 2))


def divide(a, n):
    return a >> (n.bit_length() - 1) if n & (n - 1) == 0 else a // n


def remainder(a, n):
    return a & (n - 1) if n & (n - 1) == 0 else a % n


def place_of(ids, e, me, blocks, forward):
    chain = lax.axis_size("tm") // ROW
    top = ids.shape[1]
    code = ids[divide(e, top), remainder(e, top)]
    owner, slot = divide(code, blocks), remainder(code, blocks)
    step = divide(owner, ROW) - divide(me, ROW)
    step = step if forward else -step
    turn = jnp.where(step < 0, step + chain, step)
    differ = owner ^ me
    piece = jnp.where(differ & 2 == 0, 0, chain) + turn
    return differ & 1 == 0, piece, pl.multiple_of(slot * BLK, BLK)


def pick(refs, index, act):
    if len(refs) == 1:
        act(refs[0])
        return
    half = len(refs) // 2
    lax.cond(
        index < half,
        lambda: pick(refs[:half], index, act),
        lambda: pick(refs[half:], index - half, act),
    )


def pack_kernel(first, entries, late, asked, *refs):
    pieces, out = refs[:-1], refs[-1]
    blocks = pieces[0].shape[0] // BLK
    me = lax.axis_index("tm")

    def body(e, _):
        core, piece, row = place_of(asked, first + e, me, blocks, False)
        target = pl.ds(pl.multiple_of(e * BLK, BLK), BLK)

        @pl.when(jnp.logical_and(core, piece != late))
        def _():
            def act(ref):
                out[target] = ref[pl.ds(row, BLK)]

            pick(pieces, jnp.where(piece < late, piece, piece - 1), act)

        return 0

    lax.fori_loop(0, entries, body, 0)


def session_kernel(
    entries, group, late, ids, mask, smoothed, recorded, packed, packed_rest, late_theirs, *refs
):
    pieces = refs[:-5]
    grad, far_side, terms, rows, resid = refs[-5:]
    blocks = pieces[0].shape[0] // BLK
    bins = smoothed.shape[1]
    top = ids.shape[1]
    me = lax.axis_index("tm")
    grad[...] = jnp.zeros_like(grad)
    depth = group * BLK

    def step(g, _):
        for i in range(group):
            e = g * group + i
            core, piece, row = place_of(ids, e, me, blocks, False)

            def own():
                def act(ref):
                    rows[i * BLK : (i + 1) * BLK] = ref[pl.ds(row, BLK)]

                pick(pieces, piece, act)

            def other():
                @pl.when(piece == late)
                def _():
                    rows[i * BLK : (i + 1) * BLK] = late_theirs[pl.ds(row, BLK)]

                @pl.when(piece != late)
                def _():
                    def act(ref):
                        source = pl.ds(pl.multiple_of(remainder(e, entries // 2) * BLK, BLK), BLK)
                        rows[i * BLK : (i + 1) * BLK] = ref[source]

                    pick((packed, packed_rest), divide(e, entries // 2), act)

            lax.cond(core, own, other)
        block = rows[...]
        predicted = jnp.dot(block, smoothed[...], preferred_element_type=F32)
        for i in range(group):
            e = g * group + i
            for t in range(bins // BLK):
                cut = slice(t * BLK, (t + 1) * BLK)
                weight = mask[divide(e, top), t, remainder(e, top)].astype(F32)
                part = predicted[i * BLK : (i + 1) * BLK, cut]
                seen = recorded[e, :, cut].astype(F32)
                resid[i * BLK : (i + 1) * BLK, cut] = (weight * (part - seen)).astype(BF16)
        term = lax.dot_general(
            resid[...], smoothed[...], (((1,), (1,)), ((), ())), preferred_element_type=F32
        )
        target = pl.ds(pl.multiple_of(g * depth, depth), depth)
        terms[target] = (term * (1.0 / BLK)).astype(BF16)
        grad[...] += lax.dot_general(
            block, resid[...], (((0,), (0,)), ((), ())), preferred_element_type=F32
        ) * (1.0 / BLK)
        return 0

    lax.fori_loop(0, entries // group, step, 0)
    latent_dim, width = grad.shape[0], rows.shape[1] // 2
    even = me & 1 == 0
    later, earlier = grad[:, bins - width :], grad[:, :width]
    core_edge, far_edge = jnp.where(even, later, earlier), jnp.where(even, earlier, later)
    terms[pl.ds(entries * BLK, latent_dim)] = jnp.concatenate(parts(core_edge), axis=1)
    far_side[...] = jnp.concatenate(parts(far_edge), axis=1)


def merge_late_kernel(entries, late, ids, asked, own, got, out, sums):
    blocks = out.shape[0] // BLK
    me = lax.axis_index("tm")
    sums[...] = jnp.zeros_like(sums)

    def add(e, _):
        source = pl.ds(pl.multiple_of(e * BLK, BLK), BLK)
        for names, terms in ((ids, own), (asked, got)):
            core, piece, row = place_of(names, e, me, blocks, True)

            @pl.when(jnp.logical_and(core, piece == late))
            def _():
                sums[pl.ds(row, BLK)] += terms[source].astype(F32)

        return 0

    lax.fori_loop(0, entries, add, 0)
    out[...] = sums[...].astype(out.dtype)


def merge_kernel(entries, late, ids, asked, own, got, *refs):
    chain = len(refs) // 2
    kept, outs, sums = refs[:chain], refs[chain:-1], refs[-1]
    chunk = kept[0].shape[0]
    me = lax.axis_index("tm")
    for ref in kept:
        ref[...] = jnp.zeros_like(ref)
    sums[...] = jnp.zeros_like(sums)

    def add(e, _):
        source = pl.ds(pl.multiple_of(e * BLK, BLK), BLK)
        for names, terms in ((ids, own), (asked, got)):
            core, piece, row = place_of(names, e, me, chunk // BLK, True)
            index = jnp.where(piece < late, piece - chain, piece - 1 - chain)

            @pl.when(jnp.logical_and(core, piece < chain))
            def _():
                def act(ref):
                    ref[pl.ds(row, BLK)] += terms[source].astype(F32)

                pick(kept, piece, act)

            @pl.when(jnp.logical_and(core, jnp.logical_and(piece >= chain, piece != late)))
            def _():
                sums[pl.ds(pl.multiple_of(index * chunk + row, BLK), BLK)] += terms[source].astype(F32)

        return 0

    lax.fori_loop(0, entries, add, 0)
    for q, out in enumerate(outs):
        out[...] = sums[q * chunk : (q + 1) * chunk].astype(out.dtype)


def hop_kernel(total, *refs):
    out = refs[-1]
    value = total[...]
    for came in refs[:-1]:
        value += came[...].astype(F32)
    out[...] = value.astype(out.dtype)


def local(latents, kernel, loadings, recorded, owner_ids, local_ids, recorded_mask):
    latent_dim, bins = latents.shape
    halfwidth = kernel.shape[1] // 2
    count = lax.axis_size("tm")
    chain = count // ROW
    chunk = loadings.shape[0]
    entries = owner_ids.size
    piece_bytes = count * chunk * latent_dim
    smem = pl.BlockSpec(memory_space=pltpu.SMEM)

    def permute(x, pairs):
        return lax.ppermute(x, "tm", pairs)

    def rotate(x, r):
        return permute(x, [(i, (i + r * ROW) % count) for i in range(count)])

    def flip(x, bit):
        return permute(x, [(i, i ^ bit) for i in range(count)])

    odd_even = [(i, i + 1) for i in range(1, count - 1, 2)]
    odd_even += [(target, source) for source, target in odd_even]

    ids = owner_ids[0] * (chunk // BLK) + local_ids[0]
    asked = flip(ids, 1)
    mask = jnp.transpose(recorded_mask, (0, 2, 1))

    even = lax.axis_index("tm") % 2 == 0
    later, earlier = latents[:, bins - halfwidth :], latents[:, :halfwidth]
    core_side = flip(jnp.where(even, later, earlier), 1)
    far_side = permute(jnp.where(even, earlier, later), odd_even)

    half = chain // 2
    late = chain + half
    straight = [loadings] * chain
    for r in range(1, half):
        straight[r] = rotate(straight[r - 1], 1)
        straight[-r] = rotate(straight[1 - r], -1)
    across = [flip(loadings, 2)] + [None] * (chain - 1)
    if half > 1:
        straight[1], across[0] = lax.optimization_barrier((straight[1], across[0]))
    straight[half] = rotate(straight[half - 1], 1)
    straight[1], kernel = lax.optimization_barrier((straight[1], kernel))
    table = dft_tables(2 * halfwidth)
    mxu = 30 * 2 * latent_dim * (2 * halfwidth) ** 2
    square = jax.ShapeDtypeStruct((latent_dim, 2 * halfwidth), F32)
    prepared = pl.pallas_call(
        prepare_kernel,
        out_shape=(
            jax.ShapeDtypeStruct(table.shape, BF16),
            jax.ShapeDtypeStruct(latents.shape, F32),
        )
        + (square,) * 3,
        in_specs=[HBM] * 3,
        out_specs=(VMEM,) * 5,
        scratch_shapes=[pltpu.VMEM(kernel.shape, F32), pltpu.SemaphoreType.DMA((8,))],
        compiler_params=pltpu.CompilerParams(vmem_limit_bytes=50 * MIB),
        cost_estimate=pl.CostEstimate(flops=mxu // 3, bytes_accessed=4 * MIB, transcendentals=0),
        name="prepare",
    )(table, kernel, latents)
    straight[-1], *prepared = lax.optimization_barrier((straight[-1], *prepared))
    spectrum, held_bins = [prepared[0], *prepared[2:]], prepared[1]
    for r in range(1, chain):
        if r != half:
            across[r] = flip(straight[r], 2)

    smoothed = pl.pallas_call(
        smooth_kernel,
        out_shape=jax.ShapeDtypeStruct((latent_dim, bins), BF16),
        in_specs=[VMEM] * 7,
        out_specs=VMEM,
        compiler_params=pltpu.CompilerParams(vmem_limit_bytes=16 * MIB),
        cost_estimate=pl.CostEstimate(flops=mxu, bytes_accessed=4 * MIB, transcendentals=0),
        name="smooth",
    )(held_bins, core_side, far_side, *spectrum)

    slots = jax.ShapeDtypeStruct((entries * BLK, latent_dim), BF16)
    across[half] = flip(straight[half], 2)
    early = straight + across[:half] + across[half + 1 :]

    def pack(first, total):
        return pl.pallas_call(
            functools.partial(pack_kernel, first, total, late),
            out_shape=jax.ShapeDtypeStruct((total * BLK, latent_dim), BF16),
            in_specs=[smem] + [VMEM] * len(early),
            out_specs=VMEM,
            compiler_params=pltpu.CompilerParams(vmem_limit_bytes=4 * MIB + 3 * piece_bytes),
            cost_estimate=pl.CostEstimate(flops=0, bytes_accessed=2**20, transcendentals=0),
            name="pack",
        )(asked, *early)

    asked, smoothed, mask = lax.optimization_barrier((asked, smoothed, mask))
    packed = [flip(pack(first, entries // 2), 1) for first in (0, entries // 2)]
    last, smoothed = lax.optimization_barrier((across[half], smoothed))
    late_theirs = flip(last, 1)
    pieces = straight + across

    group = 4
    extended = jax.ShapeDtypeStruct((entries * BLK + latent_dim, latent_dim), BF16)
    grad, far_side, terms = pl.pallas_call(
        functools.partial(session_kernel, entries, group, late),
        out_shape=(
            jax.ShapeDtypeStruct((latent_dim, bins), F32),
            jax.ShapeDtypeStruct((latent_dim, 2 * halfwidth), BF16),
            extended,
        ),
        in_specs=[smem] * 2 + [VMEM] * (5 + len(pieces)),
        out_specs=(VMEM,) * 3,
        scratch_shapes=[
            pltpu.VMEM((group * BLK, latent_dim), BF16),
            pltpu.VMEM((group * BLK, bins), BF16),
        ],
        compiler_params=pltpu.CompilerParams(vmem_limit_bytes=12 * MIB + 6 * piece_bytes),
        cost_estimate=pl.CostEstimate(
            flops=6 * entries * BLK * latent_dim * bins, bytes_accessed=8 * 2**20, transcendentals=0
        ),
        name="session",
    )(
        ids,
        mask,
        smoothed,
        recorded.reshape(entries, BLK, bins),
        *packed,
        late_theirs,
        *pieces,
    )

    got = flip(terms, 1)
    far_side = permute(far_side, odd_even)
    got, far_side = lax.optimization_barrier((got, far_side))
    narrow = jax.ShapeDtypeStruct((chunk, latent_dim), BF16)
    sent = pl.pallas_call(
        functools.partial(merge_late_kernel, entries, late),
        out_shape=narrow,
        in_specs=[smem] * 2 + [VMEM] * 2,
        out_specs=VMEM,
        scratch_shapes=[pltpu.VMEM((chunk, latent_dim), F32)],
        compiler_params=pltpu.CompilerParams(vmem_limit_bytes=4 * MIB + 3 * piece_bytes),
        cost_estimate=pl.CostEstimate(flops=0, bytes_accessed=2**20, transcendentals=0),
        name="merge_late",
    )(ids, asked, terms, got)
    wide = jax.ShapeDtypeStruct((chunk, latent_dim), F32)
    sent, ids = lax.optimization_barrier((sent, ids))
    back = flip(sent, 2)
    merged = pl.pallas_call(
        functools.partial(merge_kernel, entries, late),
        out_shape=(wide,) * chain + (narrow,) * (chain - 1),
        in_specs=[smem] * 2 + [VMEM] * 2,
        out_specs=(VMEM,) * (2 * chain - 1),
        scratch_shapes=[pltpu.VMEM(((chain - 1) * chunk, latent_dim), F32)],
        compiler_params=pltpu.CompilerParams(vmem_limit_bytes=4 * MIB + 6 * piece_bytes),
        cost_estimate=pl.CostEstimate(flops=0, bytes_accessed=5 * 2**20, transcendentals=0),
        name="merge",
    )(ids, asked, terms, got)
    crossed = {r: merged[chain + r - (r > half)] for r in range(chain) if r != half}
    back, *held = lax.optimization_barrier((back, *(crossed[r] for r in range(half))))
    other = {r: flip(part, 2) for r, part in enumerate(held)}
    for r in range(half + 1, chain):
        other[r] = flip(crossed[r], 2)

    def hop(total, *came):
        return pl.pallas_call(
            hop_kernel,
            out_shape=narrow,
            in_specs=[VMEM] * (1 + len(came)),
            out_specs=VMEM,
            compiler_params=pltpu.CompilerParams(vmem_limit_bytes=8 * MIB),
            cost_estimate=pl.CostEstimate(flops=0, bytes_accessed=MIB, transcendentals=0),
            name="hop",
        )(total, *came)

    rise = hop(merged[half], back)
    rise = rotate(rise, 1)
    for r in range(half - 1, 0, -1):
        rise = rotate(hop(merged[r], other[r], rise), 1)
    fall = rotate(hop(merged[half + 1], other[half + 1]), -1)
    for r in range(half + 2, chain):
        fall = rotate(hop(merged[r], other[r], fall), -1)
    loading_grad = merged[0] + other[0].astype(F32) + rise.astype(F32) + fall.astype(F32)

    latent_grad = pl.pallas_call(
        unsmooth_kernel,
        out_shape=jax.ShapeDtypeStruct((latent_dim, bins), F32),
        in_specs=[VMEM] * 7,
        out_specs=VMEM,
        compiler_params=pltpu.CompilerParams(vmem_limit_bytes=16 * MIB),
        cost_estimate=pl.CostEstimate(flops=mxu, bytes_accessed=4 * MIB, transcendentals=0),
        name="unsmooth",
    )(grad, got, far_side, *spectrum)
    return latent_grad, loading_grad


def solution(mesh):
    return jax.shard_map(
        local,
        mesh=mesh,
        in_specs=(
            P(None, ("groups", "tm")),
            P(),
            P(("groups", "tm"), None),
            P(None, None, None, ("groups", "tm")),
            P(("groups", "tm"), None, None),
            P(("groups", "tm"), None, None),
            P(None, None, ("groups", "tm")),
        ),
        out_specs=(P(None, ("groups", "tm")), P(("groups", "tm"), None)),
        check_vma=False,
    )
```

```python
import functools

import jax
import jax.numpy as jnp
import numpy as np
from jax import lax
from jax.experimental import pallas as pl
from jax.experimental.pallas import tpu as pltpu
from jax.sharding import PartitionSpec as P

BLK = 128
ROW = 4
MIB = 2**20
F32 = jnp.float32
BF16 = jnp.bfloat16
VMEM = pl.BlockSpec(memory_space=pltpu.VMEM)
HBM = pl.BlockSpec(memory_space=pltpu.HBM)


def split_const(a):
    high = a.astype(jnp.bfloat16)
    low = (a - high.astype(np.float64)).astype(jnp.bfloat16)
    return high, low


@functools.lru_cache(maxsize=None)
def dft_tables(size):
    t = np.arange(size)[:, None]
    g = np.arange(size)[None, :]
    half = size // 2
    angle = 2 * np.pi * ((t * g[:, :half]) % size) / size
    cos, sin = np.cos(angle), np.sin(angle)
    sin[:, 0] = 1 - 2 * (np.arange(size) % 2)
    real = np.concatenate([cos, sin], axis=1)
    angle = 2 * np.pi * ((t * (3 * g + 1)) % (3 * size)) / (3 * size)
    cos, sin = np.cos(angle), np.sin(angle)
    weight = np.full((size,), 2.0)
    weight[0] = weight[half] = 1.0
    scale = 1.0 / (3 * size)
    tables = [real, cos, sin, (real * weight).T * scale, cos.T * 2 * scale, sin.T * 2 * scale]
    return np.concatenate([part for table in tables for part in split_const(table)])


def parts(a):
    high = a.astype(BF16)
    return high, (a - high.astype(F32)).astype(BF16)


def times(a, tables, index):
    rows, size = a.shape
    high, low = parts(a)
    first = 2 * index * size
    t_high, t_low = tables[first : first + size], tables[first + size : first + 2 * size]
    out = jnp.dot(jnp.concatenate([high, low]), t_high, preferred_element_type=F32)
    return out[:rows] + out[rows:] + jnp.dot(high, t_low, preferred_element_type=F32)


ROOT = 0.75**0.5


def spectrum_of(thirds, tables):
    first, second, third = thirds
    rows = first.shape[0]
    base = times(first + second + third, tables, 0)
    y = jnp.concatenate([first - 0.5 * (second + third), ROOT * (third - second)])
    cos, sin = times(y, tables, 1), times(y, tables, 2)
    return base, cos[:rows] + sin[rows:], cos[rows:] - sin[:rows]


def filtered(signal, taps, sign, tables, wanted):
    (xb, xr, xi), (kb, kr, ki) = signal, taps
    rows, size = xb.shape
    half = size // 2
    first = lax.broadcasted_iota(jnp.int32, (rows, half), 1) == 0
    kc, ks = kb[:, :half], kb[:, half:]
    kc_s = jnp.where(first, ks, kc)
    ks_x = jnp.where(first, 0.0, ks) * sign
    xc, xs = xb[:, :half], xb[:, half:]
    base = times(jnp.concatenate([xc * kc + xs * ks_x, xs * kc_s - xc * ks_x], axis=1), tables, 3)
    ki = ki * sign
    z = jnp.concatenate([xr * kr + xi * ki, xi * kr - xr * ki])
    cos, sin = times(z, tables, 4), times(z, tables, 5)
    vr, vi = cos[:rows] - sin[rows:], sin[:rows] + cos[rows:]
    each = (base + vr, base - 0.5 * vr - ROOT * vi, base - 0.5 * vr + ROOT * vi)
    return jnp.concatenate([each[m] for m in wanted], axis=1)


def thirds_of(mid, core_side, far_side):
    width = core_side.shape[1]
    size = 2 * width
    even = lax.rem(lax.axis_index("tm"), 2) == 0
    low, high = jnp.where(even, far_side, core_side), jnp.where(even, core_side, far_side)
    last = mid.shape[1] - width
    return (
        jnp.concatenate([low, mid[:, :width]], axis=1),
        mid[:, width : width + size],
        jnp.concatenate([mid[:, last:], high], axis=1),
    )


def prepare_kernel(table, taps, mid, tables, bins, base, kr, ki, held, sem):
    rows = table.shape[0] // 6
    cuts = [pl.ds(i * rows, rows) for i in range(6)]
    copies = [pltpu.make_async_copy(taps, held, sem.at[0])]
    copies += [
        pltpu.make_async_copy(table.at[cut], tables.at[cut], sem.at[1 + i])
        for i, cut in enumerate(cuts)
    ]
    copies += [pltpu.make_async_copy(mid, bins, sem.at[7])]
    for copy in copies:
        copy.start()
    copies[0].wait()
    for i, (ref, sign) in enumerate(((base, 1.0), (kr, 1.0), (ki, -1.0))):
        copies[1 + i].wait()
        ref[...] = times(held[...], tables, i) * sign
    for copy in copies[4:]:
        copy.wait()


def smooth_kernel(mid, core_side, far_side, tables, base, kr, ki, out):
    thirds = thirds_of(mid[...], core_side[...], far_side[...])
    signal = spectrum_of(thirds, tables)
    taps = (base[...], kr[...], ki[...])
    out[...] = filtered(signal, taps, 1.0, tables, (0, 1)).astype(out.dtype)


def unsmooth_kernel(mid, got, far_side, tables, base, kr, ki, out):
    width = far_side.shape[1] // 2
    core = got[got.shape[0] - far_side.shape[0] :].astype(F32)
    far = far_side[...].astype(F32)
    thirds = thirds_of(
        mid[...], core[:, :width] + core[:, width:], far[:, :width] + far[:, width:]
    )
    signal = spectrum_of(thirds, tables)
    taps = (base[...], kr[...], ki[...])
    out[...] = filtered(signal, taps, -1.0, tables, (1, 2))


def divide(a, n):
    return a >> (n.bit_length() - 1) if n & (n - 1) == 0 else a // n


def remainder(a, n):
    return a & (n - 1) if n & (n - 1) == 0 else a % n


def place_of(ids, e, me, blocks, forward):
    chain = lax.axis_size("tm") // ROW
    top = ids.shape[1]
    code = ids[divide(e, top), remainder(e, top)]
    owner, slot = divide(code, blocks), remainder(code, blocks)
    step = divide(owner, ROW) - divide(me, ROW)
    step = step if forward else -step
    turn = jnp.where(step < 0, step + chain, step)
    differ = owner ^ me
    piece = jnp.where(differ & 2 == 0, 0, chain) + turn
    return differ & 1 == 0, piece, pl.multiple_of(slot * BLK, BLK)


def pick(refs, index, act):
    if len(refs) == 1:
        act(refs[0])
        return
    half = len(refs) // 2
    lax.cond(
        index < half,
        lambda: pick(refs[:half], index, act),
        lambda: pick(refs[half:], index - half, act),
    )


def pack_kernel(first, entries, late, asked, *refs):
    pieces, out = refs[:-1], refs[-1]
    blocks = pieces[0].shape[0] // BLK
    me = lax.axis_index("tm")

    def body(e, _):
        core, piece, row = place_of(asked, first + e, me, blocks, False)
        target = pl.ds(pl.multiple_of(e * BLK, BLK), BLK)

        @pl.when(jnp.logical_and(core, piece != late))
        def _():
            def act(ref):
                out[target] = ref[pl.ds(row, BLK)]

            pick(pieces, jnp.where(piece < late, piece, piece - 1), act)

        return 0

    lax.fori_loop(0, entries, body, 0)


def session_kernel(
    entries, group, late, ids, mask, smoothed, recorded, packed, packed_rest, late_theirs, *refs
):
    pieces = refs[:-5]
    grad, far_side, terms, rows, resid = refs[-5:]
    blocks = pieces[0].shape[0] // BLK
    bins = smoothed.shape[1]
    top = ids.shape[1]
    me = lax.axis_index("tm")
    grad[...] = jnp.zeros_like(grad)
    depth = group * BLK

    def step(g, _):
        for i in range(group):
            e = g * group + i
            core, piece, row = place_of(ids, e, me, blocks, False)

            def own():
                def act(ref):
                    rows[i * BLK : (i + 1) * BLK] = ref[pl.ds(row, BLK)]

                pick(pieces, piece, act)

            def other():
                @pl.when(piece == late)
                def _():
                    rows[i * BLK : (i + 1) * BLK] = late_theirs[pl.ds(row, BLK)]

                @pl.when(piece != late)
                def _():
                    def act(ref):
                        source = pl.ds(pl.multiple_of(remainder(e, entries // 2) * BLK, BLK), BLK)
                        rows[i * BLK : (i + 1) * BLK] = ref[source]

                    pick((packed, packed_rest), divide(e, entries // 2), act)

            lax.cond(core, own, other)
        block = rows[...]
        predicted = jnp.dot(block, smoothed[...], preferred_element_type=F32)
        for i in range(group):
            e = g * group + i
            for t in range(bins // BLK):
                cut = slice(t * BLK, (t + 1) * BLK)
                weight = mask[divide(e, top), t, remainder(e, top)].astype(F32)
                part = predicted[i * BLK : (i + 1) * BLK, cut]
                seen = recorded[e, :, cut].astype(F32)
                resid[i * BLK : (i + 1) * BLK, cut] = (weight * (part - seen)).astype(BF16)
        term = lax.dot_general(
            resid[...], smoothed[...], (((1,), (1,)), ((), ())), preferred_element_type=F32
        )
        target = pl.ds(pl.multiple_of(g * depth, depth), depth)
        terms[target] = (term * (1.0 / BLK)).astype(BF16)
        grad[...] += lax.dot_general(
            block, resid[...], (((0,), (0,)), ((), ())), preferred_element_type=F32
        ) * (1.0 / BLK)
        return 0

    lax.fori_loop(0, entries // group, step, 0)
    latent_dim, width = grad.shape[0], rows.shape[1] // 2
    even = me & 1 == 0
    later, earlier = grad[:, bins - width :], grad[:, :width]
    core_edge, far_edge = jnp.where(even, later, earlier), jnp.where(even, earlier, later)
    terms[pl.ds(entries * BLK, latent_dim)] = jnp.concatenate(parts(core_edge), axis=1)
    far_side[...] = jnp.concatenate(parts(far_edge), axis=1)


def merge_late_kernel(entries, late, ids, asked, own, got, out, sums):
    blocks = out.shape[0] // BLK
    me = lax.axis_index("tm")
    sums[...] = jnp.zeros_like(sums)

    def add(e, _):
        source = pl.ds(pl.multiple_of(e * BLK, BLK), BLK)
        for names, terms in ((ids, own), (asked, got)):
            core, piece, row = place_of(names, e, me, blocks, True)

            @pl.when(jnp.logical_and(core, piece == late))
            def _():
                sums[pl.ds(row, BLK)] += terms[source].astype(F32)

        return 0

    lax.fori_loop(0, entries, add, 0)
    out[...] = sums[...].astype(out.dtype)


def merge_kernel(entries, late, ids, asked, own, got, *refs):
    chain = len(refs) // 2
    kept, outs, sums = refs[:chain], refs[chain:-1], refs[-1]
    chunk = kept[0].shape[0]
    me = lax.axis_index("tm")
    for ref in kept:
        ref[...] = jnp.zeros_like(ref)
    sums[...] = jnp.zeros_like(sums)

    def add(e, _):
        source = pl.ds(pl.multiple_of(e * BLK, BLK), BLK)
        for names, terms in ((ids, own), (asked, got)):
            core, piece, row = place_of(names, e, me, chunk // BLK, True)
            index = jnp.where(piece < late, piece - chain, piece - 1 - chain)

            @pl.when(jnp.logical_and(core, piece < chain))
            def _():
                def act(ref):
                    ref[pl.ds(row, BLK)] += terms[source].astype(F32)

                pick(kept, piece, act)

            @pl.when(jnp.logical_and(core, jnp.logical_and(piece >= chain, piece != late)))
            def _():
                sums[pl.ds(pl.multiple_of(index * chunk + row, BLK), BLK)] += terms[source].astype(F32)

        return 0

    lax.fori_loop(0, entries, add, 0)
    for q, out in enumerate(outs):
        out[...] = sums[q * chunk : (q + 1) * chunk].astype(out.dtype)


def hop_kernel(total, *refs):
    out = refs[-1]
    value = total[...]
    for came in refs[:-1]:
        value += came[...].astype(F32)
    out[...] = value.astype(out.dtype)


def local(latents, kernel, loadings, recorded, owner_ids, local_ids, recorded_mask):
    latent_dim, bins = latents.shape
    halfwidth = kernel.shape[1] // 2
    count = lax.axis_size("tm")
    chain = count // ROW
    chunk = loadings.shape[0]
    entries = owner_ids.size
    piece_bytes = count * chunk * latent_dim
    smem = pl.BlockSpec(memory_space=pltpu.SMEM)

    def permute(x, pairs):
        return lax.ppermute(x, "tm", pairs)

    def rotate(x, r):
        return permute(x, [(i, (i + r * ROW) % count) for i in range(count)])

    def flip(x, bit):
        return permute(x, [(i, i ^ bit) for i in range(count)])

    odd_even = [(i, i + 1) for i in range(1, count - 1, 2)]
    odd_even += [(target, source) for source, target in odd_even]

    ids = owner_ids[0] * (chunk // BLK) + local_ids[0]
    asked = flip(ids, 1)
    mask = jnp.transpose(recorded_mask, (0, 2, 1))

    even = lax.axis_index("tm") % 2 == 0
    later, earlier = latents[:, bins - halfwidth :], latents[:, :halfwidth]
    core_side = flip(jnp.where(even, later, earlier), 1)
    far_side = permute(jnp.where(even, earlier, later), odd_even)

    half = chain // 2
    late = chain + half
    straight = [loadings] * chain
    for r in range(1, half):
        straight[r] = rotate(straight[r - 1], 1)
        straight[-r] = rotate(straight[1 - r], -1)
    across = [flip(loadings, 2)] + [None] * (chain - 1)
    if half > 1:
        straight[1], across[0] = lax.optimization_barrier((straight[1], across[0]))
    straight[half] = rotate(straight[half - 1], 1)
    straight[1], kernel = lax.optimization_barrier((straight[1], kernel))
    table = dft_tables(2 * halfwidth)
    mxu = 30 * 2 * latent_dim * (2 * halfwidth) ** 2
    square = jax.ShapeDtypeStruct((latent_dim, 2 * halfwidth), F32)
    prepared = pl.pallas_call(
        prepare_kernel,
        out_shape=(
            jax.ShapeDtypeStruct(table.shape, BF16),
            jax.ShapeDtypeStruct(latents.shape, F32),
        )
        + (square,) * 3,
        in_specs=[HBM] * 3,
        out_specs=(VMEM,) * 5,
        scratch_shapes=[pltpu.VMEM(kernel.shape, F32), pltpu.SemaphoreType.DMA((8,))],
        compiler_params=pltpu.CompilerParams(vmem_limit_bytes=50 * MIB),
        cost_estimate=pl.CostEstimate(flops=mxu // 3, bytes_accessed=4 * MIB, transcendentals=0),
        name="prepare",
    )(table, kernel, latents)
    straight[-1], *prepared = lax.optimization_barrier((straight[-1], *prepared))
    spectrum, held_bins = [prepared[0], *prepared[2:]], prepared[1]
    for r in range(1, chain):
        if r != half:
            across[r] = flip(straight[r], 2)

    smoothed = pl.pallas_call(
        smooth_kernel,
        out_shape=jax.ShapeDtypeStruct((latent_dim, bins), BF16),
        in_specs=[VMEM] * 7,
        out_specs=VMEM,
        compiler_params=pltpu.CompilerParams(vmem_limit_bytes=16 * MIB),
        cost_estimate=pl.CostEstimate(flops=mxu, bytes_accessed=4 * MIB, transcendentals=0),
        name="smooth",
    )(held_bins, core_side, far_side, *spectrum)

    slots = jax.ShapeDtypeStruct((entries * BLK, latent_dim), BF16)
    across[half] = flip(straight[half], 2)
    early = straight + across[:half] + across[half + 1 :]

    def pack(first, total):
        return pl.pallas_call(
            functools.partial(pack_kernel, first, total, late),
            out_shape=jax.ShapeDtypeStruct((total * BLK, latent_dim), BF16),
            in_specs=[smem] + [VMEM] * len(early),
            out_specs=VMEM,
            compiler_params=pltpu.CompilerParams(vmem_limit_bytes=4 * MIB + 3 * piece_bytes),
            cost_estimate=pl.CostEstimate(flops=0, bytes_accessed=2**20, transcendentals=0),
            name="pack",
        )(asked, *early)

    asked, smoothed, mask = lax.optimization_barrier((asked, smoothed, mask))
    packed = [flip(pack(first, entries // 2), 1) for first in (0, entries // 2)]
    last, smoothed = lax.optimization_barrier((across[half], smoothed))
    late_theirs = flip(last, 1)
    pieces = straight + across

    group = 4
    extended = jax.ShapeDtypeStruct((entries * BLK + latent_dim, latent_dim), BF16)
    grad, far_side, terms = pl.pallas_call(
        functools.partial(session_kernel, entries, group, late),
        out_shape=(
            jax.ShapeDtypeStruct((latent_dim, bins), F32),
            jax.ShapeDtypeStruct((latent_dim, 2 * halfwidth), BF16),
            extended,
        ),
        in_specs=[smem] * 2 + [VMEM] * (5 + len(pieces)),
        out_specs=(VMEM,) * 3,
        scratch_shapes=[
            pltpu.VMEM((group * BLK, latent_dim), BF16),
            pltpu.VMEM((group * BLK, bins), BF16),
        ],
        compiler_params=pltpu.CompilerParams(vmem_limit_bytes=12 * MIB + 6 * piece_bytes),
        cost_estimate=pl.CostEstimate(
            flops=6 * entries * BLK * latent_dim * bins, bytes_accessed=8 * 2**20, transcendentals=0
        ),
        name="session",
    )(
        ids,
        mask,
        smoothed,
        recorded.reshape(entries, BLK, bins),
        *packed,
        late_theirs,
        *pieces,
    )

    got = flip(terms, 1)
    far_side = permute(far_side, odd_even)
    narrow = jax.ShapeDtypeStruct((chunk, latent_dim), BF16)
    sent = pl.pallas_call(
        functools.partial(merge_late_kernel, entries, late),
        out_shape=narrow,
        in_specs=[smem] * 2 + [VMEM] * 2,
        out_specs=VMEM,
        scratch_shapes=[pltpu.VMEM((chunk, latent_dim), F32)],
        compiler_params=pltpu.CompilerParams(vmem_limit_bytes=4 * MIB + 3 * piece_bytes),
        cost_estimate=pl.CostEstimate(flops=0, bytes_accessed=2**20, transcendentals=0),
        name="merge_late",
    )(ids, asked, terms, got)
    wide = jax.ShapeDtypeStruct((chunk, latent_dim), F32)
    sent, ids = lax.optimization_barrier((sent, ids))
    back = flip(sent, 2)
    merged = pl.pallas_call(
        functools.partial(merge_kernel, entries, late),
        out_shape=(wide,) * chain + (narrow,) * (chain - 1),
        in_specs=[smem] * 2 + [VMEM] * 2,
        out_specs=(VMEM,) * (2 * chain - 1),
        scratch_shapes=[pltpu.VMEM(((chain - 1) * chunk, latent_dim), F32)],
        compiler_params=pltpu.CompilerParams(vmem_limit_bytes=4 * MIB + 6 * piece_bytes),
        cost_estimate=pl.CostEstimate(flops=0, bytes_accessed=5 * 2**20, transcendentals=0),
        name="merge",
    )(ids, asked, terms, got)
    far_side, *merged = lax.optimization_barrier((far_side, *merged))
    crossed = {r: merged[chain + r - (r > half)] for r in range(chain) if r != half}
    back, *held = lax.optimization_barrier((back, *(crossed[r] for r in range(half))))
    other = {r: flip(part, 2) for r, part in enumerate(held)}
    for r in range(half + 1, chain):
        other[r] = flip(crossed[r], 2)

    def hop(total, *came):
        return pl.pallas_call(
            hop_kernel,
            out_shape=narrow,
            in_specs=[VMEM] * (1 + len(came)),
            out_specs=VMEM,
            compiler_params=pltpu.CompilerParams(vmem_limit_bytes=8 * MIB),
            cost_estimate=pl.CostEstimate(flops=0, bytes_accessed=MIB, transcendentals=0),
            name="hop",
        )(total, *came)

    rise = hop(merged[half], back)
    rise = rotate(rise, 1)
    for r in range(half - 1, 0, -1):
        rise = rotate(hop(merged[r], other[r], rise), 1)
    fall = rotate(hop(merged[half + 1], other[half + 1]), -1)
    for r in range(half + 2, chain):
        fall = rotate(hop(merged[r], other[r], fall), -1)
    loading_grad = merged[0] + other[0].astype(F32) + rise.astype(F32) + fall.astype(F32)

    latent_grad = pl.pallas_call(
        unsmooth_kernel,
        out_shape=jax.ShapeDtypeStruct((latent_dim, bins), F32),
        in_specs=[VMEM] * 7,
        out_specs=VMEM,
        compiler_params=pltpu.CompilerParams(vmem_limit_bytes=16 * MIB),
        cost_estimate=pl.CostEstimate(flops=mxu, bytes_accessed=4 * MIB, transcendentals=0),
        name="unsmooth",
    )(grad, got, far_side, *spectrum)
    return latent_grad, loading_grad


def solution(mesh):
    return jax.shard_map(
        local,
        mesh=mesh,
        in_specs=(
            P(None, ("groups", "tm")),
            P(),
            P(("groups", "tm"), None),
            P(None, None, None, ("groups", "tm")),
            P(("groups", "tm"), None, None),
            P(("groups", "tm"), None, None),
            P(None, None, ("groups", "tm")),
        ),
        out_specs=(P(None, ("groups", "tm")), P(("groups", "tm"), None)),
        check_vma=False,
    )
```

```python
import functools

import jax
import jax.numpy as jnp
import numpy as np
from jax import lax
from jax.experimental import pallas as pl
from jax.experimental.pallas import tpu as pltpu
from jax.sharding import PartitionSpec as P

BLK = 128
ROW = 4
MIB = 2**20
F32 = jnp.float32
BF16 = jnp.bfloat16
VMEM = pl.BlockSpec(memory_space=pltpu.VMEM)
HBM = pl.BlockSpec(memory_space=pltpu.HBM)


def split_const(a):
    high = a.astype(jnp.bfloat16)
    low = (a - high.astype(np.float64)).astype(jnp.bfloat16)
    return high, low


@functools.lru_cache(maxsize=None)
def dft_tables(size):
    t = np.arange(size)[:, None]
    g = np.arange(size)[None, :]
    half = size // 2
    angle = 2 * np.pi * ((t * g[:, :half]) % size) / size
    cos, sin = np.cos(angle), np.sin(angle)
    sin[:, 0] = 1 - 2 * (np.arange(size) % 2)
    real = np.concatenate([cos, sin], axis=1)
    angle = 2 * np.pi * ((t * (3 * g + 1)) % (3 * size)) / (3 * size)
    cos, sin = np.cos(angle), np.sin(angle)
    weight = np.full((size,), 2.0)
    weight[0] = weight[half] = 1.0
    scale = 1.0 / (3 * size)
    tables = [real, cos, sin, (real * weight).T * scale, cos.T * 2 * scale, sin.T * 2 * scale]
    return np.concatenate([part for table in tables for part in split_const(table)])


def parts(a):
    high = a.astype(BF16)
    return high, (a - high.astype(F32)).astype(BF16)


def times(a, tables, index):
    rows, size = a.shape
    high, low = parts(a)
    first = 2 * index * size
    t_high, t_low = tables[first : first + size], tables[first + size : first + 2 * size]
    out = jnp.dot(jnp.concatenate([high, low]), t_high, preferred_element_type=F32)
    return out[:rows] + out[rows:] + jnp.dot(high, t_low, preferred_element_type=F32)


ROOT = 0.75**0.5


def spectrum_of(thirds, tables):
    first, second, third = thirds
    rows = first.shape[0]
    base = times(first + second + third, tables, 0)
    y = jnp.concatenate([first - 0.5 * (second + third), ROOT * (third - second)])
    cos, sin = times(y, tables, 1), times(y, tables, 2)
    return base, cos[:rows] + sin[rows:], cos[rows:] - sin[:rows]


def filtered(signal, taps, sign, tables, wanted):
    (xb, xr, xi), (kb, kr, ki) = signal, taps
    rows, size = xb.shape
    half = size // 2
    first = lax.broadcasted_iota(jnp.int32, (rows, half), 1) == 0
    kc, ks = kb[:, :half], kb[:, half:]
    kc_s = jnp.where(first, ks, kc)
    ks_x = jnp.where(first, 0.0, ks) * sign
    xc, xs = xb[:, :half], xb[:, half:]
    base = times(jnp.concatenate([xc * kc + xs * ks_x, xs * kc_s - xc * ks_x], axis=1), tables, 3)
    ki = ki * sign
    z = jnp.concatenate([xr * kr + xi * ki, xi * kr - xr * ki])
    cos, sin = times(z, tables, 4), times(z, tables, 5)
    vr, vi = cos[:rows] - sin[rows:], sin[:rows] + cos[rows:]
    each = (base + vr, base - 0.5 * vr - ROOT * vi, base - 0.5 * vr + ROOT * vi)
    return jnp.concatenate([each[m] for m in wanted], axis=1)


def thirds_of(mid, core_side, far_side):
    width = core_side.shape[1]
    size = 2 * width
    even = lax.rem(lax.axis_index("tm"), 2) == 0
    low, high = jnp.where(even, far_side, core_side), jnp.where(even, core_side, far_side)
    last = mid.shape[1] - width
    return (
        jnp.concatenate([low, mid[:, :width]], axis=1),
        mid[:, width : width + size],
        jnp.concatenate([mid[:, last:], high], axis=1),
    )


def prepare_kernel(table, taps, mid, tables, bins, base, kr, ki, held, sem):
    rows = table.shape[0] // 6
    cuts = [pl.ds(i * rows, rows) for i in range(6)]
    copies = [pltpu.make_async_copy(taps, held, sem.at[0])]
    copies += [
        pltpu.make_async_copy(table.at[cut], tables.at[cut], sem.at[1 + i])
        for i, cut in enumerate(cuts)
    ]
    copies += [pltpu.make_async_copy(mid, bins, sem.at[7])]
    for copy in copies:
        copy.start()
    copies[0].wait()
    for i, (ref, sign) in enumerate(((base, 1.0), (kr, 1.0), (ki, -1.0))):
        copies[1 + i].wait()
        ref[...] = times(held[...], tables, i) * sign
    for copy in copies[4:]:
        copy.wait()


def smooth_kernel(mid, core_side, far_side, tables, base, kr, ki, out):
    thirds = thirds_of(mid[...], core_side[...], far_side[...])
    signal = spectrum_of(thirds, tables)
    taps = (base[...], kr[...], ki[...])
    out[...] = filtered(signal, taps, 1.0, tables, (0, 1)).astype(out.dtype)


def unsmooth_kernel(mid, got, far_side, tables, base, kr, ki, out):
    width = far_side.shape[1] // 2
    core = got[got.shape[0] - far_side.shape[0] :].astype(F32)
    far = far_side[...].astype(F32)
    thirds = thirds_of(
        mid[...], core[:, :width] + core[:, width:], far[:, :width] + far[:, width:]
    )
    signal = spectrum_of(thirds, tables)
    taps = (base[...], kr[...], ki[...])
    out[...] = filtered(signal, taps, -1.0, tables, (1, 2))


def divide(a, n):
    return a >> (n.bit_length() - 1) if n & (n - 1) == 0 else a // n


def remainder(a, n):
    return a & (n - 1) if n & (n - 1) == 0 else a % n


def place_of(ids, e, me, blocks, forward):
    chain = lax.axis_size("tm") // ROW
    top = ids.shape[1]
    code = ids[divide(e, top), remainder(e, top)]
    owner, slot = divide(code, blocks), remainder(code, blocks)
    step = divide(owner, ROW) - divide(me, ROW)
    step = step if forward else -step
    turn = jnp.where(step < 0, step + chain, step)
    differ = owner ^ me
    piece = jnp.where(differ & 2 == 0, 0, chain) + turn
    return differ & 1 == 0, piece, pl.multiple_of(slot * BLK, BLK)


def pick(refs, index, act):
    if len(refs) == 1:
        act(refs[0])
        return
    half = len(refs) // 2
    lax.cond(
        index < half,
        lambda: pick(refs[:half], index, act),
        lambda: pick(refs[half:], index - half, act),
    )


def pack_kernel(first, entries, late, asked, *refs):
    pieces, out = refs[:-1], refs[-1]
    blocks = pieces[0].shape[0] // BLK
    me = lax.axis_index("tm")

    def body(e, _):
        core, piece, row = place_of(asked, first + e, me, blocks, False)
        target = pl.ds(pl.multiple_of(e * BLK, BLK), BLK)

        @pl.when(jnp.logical_and(core, piece != late))
        def _():
            def act(ref):
                out[target] = ref[pl.ds(row, BLK)]

            pick(pieces, jnp.where(piece < late, piece, piece - 1), act)

        return 0

    lax.fori_loop(0, entries, body, 0)


def session_kernel(
    entries, group, late, ids, mask, smoothed, recorded, packed, packed_rest, late_theirs, *refs
):
    pieces = refs[:-5]
    grad, far_side, terms, rows, resid = refs[-5:]
    blocks = pieces[0].shape[0] // BLK
    bins = smoothed.shape[1]
    top = ids.shape[1]
    me = lax.axis_index("tm")
    grad[...] = jnp.zeros_like(grad)
    depth = group * BLK

    def step(g, _):
        for i in range(group):
            e = g * group + i
            core, piece, row = place_of(ids, e, me, blocks, False)

            def own():
                def act(ref):
                    rows[i * BLK : (i + 1) * BLK] = ref[pl.ds(row, BLK)]

                pick(pieces, piece, act)

            def other():
                @pl.when(piece == late)
                def _():
                    rows[i * BLK : (i + 1) * BLK] = late_theirs[pl.ds(row, BLK)]

                @pl.when(piece != late)
                def _():
                    def act(ref):
                        source = pl.ds(pl.multiple_of(remainder(e, entries // 2) * BLK, BLK), BLK)
                        rows[i * BLK : (i + 1) * BLK] = ref[source]

                    pick((packed, packed_rest), divide(e, entries // 2), act)

            lax.cond(core, own, other)
        block = rows[...]
        predicted = jnp.dot(block, smoothed[...], preferred_element_type=F32)
        for i in range(group):
            e = g * group + i
            for t in range(bins // BLK):
                cut = slice(t * BLK, (t + 1) * BLK)
                weight = mask[divide(e, top), t, remainder(e, top)].astype(F32)
                part = predicted[i * BLK : (i + 1) * BLK, cut]
                seen = recorded[e, :, cut].astype(F32)
                resid[i * BLK : (i + 1) * BLK, cut] = (weight * (part - seen)).astype(BF16)
        term = lax.dot_general(
            resid[...], smoothed[...], (((1,), (1,)), ((), ())), preferred_element_type=F32
        )
        target = pl.ds(pl.multiple_of(g * depth, depth), depth)
        terms[target] = (term * (1.0 / BLK)).astype(BF16)
        grad[...] += lax.dot_general(
            block, resid[...], (((0,), (0,)), ((), ())), preferred_element_type=F32
        ) * (1.0 / BLK)
        return 0

    lax.fori_loop(0, entries // group, step, 0)
    latent_dim, width = grad.shape[0], rows.shape[1] // 2
    even = me & 1 == 0
    later, earlier = grad[:, bins - width :], grad[:, :width]
    core_edge, far_edge = jnp.where(even, later, earlier), jnp.where(even, earlier, later)
    terms[pl.ds(entries * BLK, latent_dim)] = jnp.concatenate(parts(core_edge), axis=1)
    far_side[...] = jnp.concatenate(parts(far_edge), axis=1)


def merge_late_kernel(entries, late, ids, asked, own, got, out, sums):
    blocks = out.shape[0] // BLK
    me = lax.axis_index("tm")
    sums[...] = jnp.zeros_like(sums)

    def add(e, _):
        source = pl.ds(pl.multiple_of(e * BLK, BLK), BLK)
        for names, terms in ((ids, own), (asked, got)):
            core, piece, row = place_of(names, e, me, blocks, True)

            @pl.when(jnp.logical_and(core, piece == late))
            def _():
                sums[pl.ds(row, BLK)] += terms[source].astype(F32)

        return 0

    lax.fori_loop(0, entries, add, 0)
    out[...] = sums[...].astype(out.dtype)


def merge_kernel(entries, late, ids, asked, own, got, *refs):
    chain = len(refs) // 2
    kept, outs, sums = refs[:chain], refs[chain:-1], refs[-1]
    chunk = kept[0].shape[0]
    me = lax.axis_index("tm")
    for ref in kept:
        ref[...] = jnp.zeros_like(ref)
    sums[...] = jnp.zeros_like(sums)

    def add(e, _):
        source = pl.ds(pl.multiple_of(e * BLK, BLK), BLK)
        for names, terms in ((ids, own), (asked, got)):
            core, piece, row = place_of(names, e, me, chunk // BLK, True)
            index = jnp.where(piece < late, piece - chain, piece - 1 - chain)

            @pl.when(jnp.logical_and(core, piece < chain))
            def _():
                def act(ref):
                    ref[pl.ds(row, BLK)] += terms[source].astype(F32)

                pick(kept, piece, act)

            @pl.when(jnp.logical_and(core, jnp.logical_and(piece >= chain, piece != late)))
            def _():
                sums[pl.ds(pl.multiple_of(index * chunk + row, BLK), BLK)] += terms[source].astype(F32)

        return 0

    lax.fori_loop(0, entries, add, 0)
    for q, out in enumerate(outs):
        out[...] = sums[q * chunk : (q + 1) * chunk].astype(out.dtype)


def hop_kernel(total, *refs):
    out = refs[-1]
    value = total[...]
    for came in refs[:-1]:
        value += came[...].astype(F32)
    out[...] = value.astype(out.dtype)


def local(latents, kernel, loadings, recorded, owner_ids, local_ids, recorded_mask):
    latent_dim, bins = latents.shape
    halfwidth = kernel.shape[1] // 2
    count = lax.axis_size("tm")
    chain = count // ROW
    chunk = loadings.shape[0]
    entries = owner_ids.size
    piece_bytes = count * chunk * latent_dim
    smem = pl.BlockSpec(memory_space=pltpu.SMEM)

    def permute(x, pairs):
        return lax.ppermute(x, "tm", pairs)

    def rotate(x, r):
        return permute(x, [(i, (i + r * ROW) % count) for i in range(count)])

    def flip(x, bit):
        return permute(x, [(i, i ^ bit) for i in range(count)])

    odd_even = [(i, i + 1) for i in range(1, count - 1, 2)]
    odd_even += [(target, source) for source, target in odd_even]

    ids = owner_ids[0] * (chunk // BLK) + local_ids[0]
    asked = flip(ids, 1)
    mask = jnp.transpose(recorded_mask, (0, 2, 1))

    even = lax.axis_index("tm") % 2 == 0
    later, earlier = latents[:, bins - halfwidth :], latents[:, :halfwidth]
    core_side = flip(jnp.where(even, later, earlier), 1)
    far_side = permute(jnp.where(even, earlier, later), odd_even)

    half = chain // 2
    late = chain + half
    straight = [loadings] * chain
    for r in range(1, half):
        straight[r] = rotate(straight[r - 1], 1)
        straight[-r] = rotate(straight[1 - r], -1)
    across = [flip(loadings, 2)] + [None] * (chain - 1)
    if half > 1:
        straight[1], across[0] = lax.optimization_barrier((straight[1], across[0]))
    straight[half] = rotate(straight[half - 1], 1)
    straight[1], kernel = lax.optimization_barrier((straight[1], kernel))
    table = dft_tables(2 * halfwidth)
    mxu = 30 * 2 * latent_dim * (2 * halfwidth) ** 2
    square = jax.ShapeDtypeStruct((latent_dim, 2 * halfwidth), F32)
    prepared = pl.pallas_call(
        prepare_kernel,
        out_shape=(
            jax.ShapeDtypeStruct(table.shape, BF16),
            jax.ShapeDtypeStruct(latents.shape, F32),
        )
        + (square,) * 3,
        in_specs=[HBM] * 3,
        out_specs=(VMEM,) * 5,
        scratch_shapes=[pltpu.VMEM(kernel.shape, F32), pltpu.SemaphoreType.DMA((8,))],
        compiler_params=pltpu.CompilerParams(vmem_limit_bytes=50 * MIB),
        cost_estimate=pl.CostEstimate(flops=mxu // 3, bytes_accessed=4 * MIB, transcendentals=0),
        name="prepare",
    )(table, kernel, latents)
    straight[-1], *prepared = lax.optimization_barrier((straight[-1], *prepared))
    spectrum, held_bins = [prepared[0], *prepared[2:]], prepared[1]
    for r in range(1, chain):
        if r != half:
            across[r] = flip(straight[r], 2)

    smoothed = pl.pallas_call(
        smooth_kernel,
        out_shape=jax.ShapeDtypeStruct((latent_dim, bins), BF16),
        in_specs=[VMEM] * 7,
        out_specs=VMEM,
        compiler_params=pltpu.CompilerParams(vmem_limit_bytes=16 * MIB),
        cost_estimate=pl.CostEstimate(flops=mxu, bytes_accessed=4 * MIB, transcendentals=0),
        name="smooth",
    )(held_bins, core_side, far_side, *spectrum)

    slots = jax.ShapeDtypeStruct((entries * BLK, latent_dim), BF16)
    across[half] = flip(straight[half], 2)
    early = straight + across[:half] + across[half + 1 :]

    def pack(first, total):
        return pl.pallas_call(
            functools.partial(pack_kernel, first, total, late),
            out_shape=jax.ShapeDtypeStruct((total * BLK, latent_dim), BF16),
            in_specs=[smem] + [VMEM] * len(early),
            out_specs=VMEM,
            compiler_params=pltpu.CompilerParams(vmem_limit_bytes=4 * MIB + 3 * piece_bytes),
            cost_estimate=pl.CostEstimate(flops=0, bytes_accessed=2**20, transcendentals=0),
            name="pack",
        )(asked, *early)

    asked, smoothed, mask = lax.optimization_barrier((asked, smoothed, mask))
    packed = [flip(pack(first, entries // 2), 1) for first in (0, entries // 2)]
    last, smoothed = lax.optimization_barrier((across[half], smoothed))
    late_theirs = flip(last, 1)
    pieces = straight + across

    group = 4
    extended = jax.ShapeDtypeStruct((entries * BLK + latent_dim, latent_dim), BF16)
    grad, far_side, terms = pl.pallas_call(
        functools.partial(session_kernel, entries, group, late),
        out_shape=(
            jax.ShapeDtypeStruct((latent_dim, bins), F32),
            jax.ShapeDtypeStruct((latent_dim, 2 * halfwidth), BF16),
            extended,
        ),
        in_specs=[smem] * 2 + [VMEM] * (5 + len(pieces)),
        out_specs=(VMEM,) * 3,
        scratch_shapes=[
            pltpu.VMEM((group * BLK, latent_dim), BF16),
            pltpu.VMEM((group * BLK, bins), BF16),
        ],
        compiler_params=pltpu.CompilerParams(vmem_limit_bytes=12 * MIB + 6 * piece_bytes),
        cost_estimate=pl.CostEstimate(
            flops=6 * entries * BLK * latent_dim * bins, bytes_accessed=8 * 2**20, transcendentals=0
        ),
        name="session",
    )(
        ids,
        mask,
        smoothed,
        recorded.reshape(entries, BLK, bins),
        *packed,
        late_theirs,
        *pieces,
    )

    got = flip(terms, 1)
    narrow = jax.ShapeDtypeStruct((chunk, latent_dim), BF16)
    sent = pl.pallas_call(
        functools.partial(merge_late_kernel, entries, late),
        out_shape=narrow,
        in_specs=[smem] * 2 + [VMEM] * 2,
        out_specs=VMEM,
        scratch_shapes=[pltpu.VMEM((chunk, latent_dim), F32)],
        compiler_params=pltpu.CompilerParams(vmem_limit_bytes=4 * MIB + 3 * piece_bytes),
        cost_estimate=pl.CostEstimate(flops=0, bytes_accessed=2**20, transcendentals=0),
        name="merge_late",
    )(ids, asked, terms, got)
    wide = jax.ShapeDtypeStruct((chunk, latent_dim), F32)
    sent, ids = lax.optimization_barrier((sent, ids))
    back = flip(sent, 2)
    merged = pl.pallas_call(
        functools.partial(merge_kernel, entries, late),
        out_shape=(wide,) * chain + (narrow,) * (chain - 1),
        in_specs=[smem] * 2 + [VMEM] * 2,
        out_specs=(VMEM,) * (2 * chain - 1),
        scratch_shapes=[pltpu.VMEM(((chain - 1) * chunk, latent_dim), F32)],
        compiler_params=pltpu.CompilerParams(vmem_limit_bytes=4 * MIB + 6 * piece_bytes),
        cost_estimate=pl.CostEstimate(flops=0, bytes_accessed=5 * 2**20, transcendentals=0),
        name="merge",
    )(ids, asked, terms, got)
    crossed = {r: merged[chain + r - (r > half)] for r in range(chain) if r != half}
    other = {r: flip(part, 2) for r, part in crossed.items() if r}

    def hop(total, *came):
        return pl.pallas_call(
            hop_kernel,
            out_shape=narrow,
            in_specs=[VMEM] * (1 + len(came)),
            out_specs=VMEM,
            compiler_params=pltpu.CompilerParams(vmem_limit_bytes=8 * MIB),
            cost_estimate=pl.CostEstimate(flops=0, bytes_accessed=MIB, transcendentals=0),
            name="hop",
        )(total, *came)

    rise = hop(merged[half], back)
    rise, far_side = lax.optimization_barrier((rise, far_side))
    far_side = permute(far_side, odd_even)
    other[1], far_side = lax.optimization_barrier((other[1], far_side))
    _, own = lax.optimization_barrier((other[half + 1], crossed[0]))
    other[0] = flip(own, 2)
    rise = rotate(rise, 1)
    for r in range(half - 1, 0, -1):
        rise = rotate(hop(merged[r], other[r], rise), 1)
    fall = rotate(hop(merged[half + 1], other[half + 1]), -1)
    for r in range(half + 2, chain):
        fall = rotate(hop(merged[r], other[r], fall), -1)
    loading_grad = merged[0] + other[0].astype(F32) + rise.astype(F32) + fall.astype(F32)

    latent_grad = pl.pallas_call(
        unsmooth_kernel,
        out_shape=jax.ShapeDtypeStruct((latent_dim, bins), F32),
        in_specs=[VMEM] * 7,
        out_specs=VMEM,
        compiler_params=pltpu.CompilerParams(vmem_limit_bytes=16 * MIB),
        cost_estimate=pl.CostEstimate(flops=mxu, bytes_accessed=4 * MIB, transcendentals=0),
        name="unsmooth",
    )(grad, got, far_side, *spectrum)
    return latent_grad, loading_grad


def solution(mesh):
    return jax.shard_map(
        local,
        mesh=mesh,
        in_specs=(
            P(None, ("groups", "tm")),
            P(),
            P(("groups", "tm"), None),
            P(None, None, None, ("groups", "tm")),
            P(("groups", "tm"), None, None),
            P(("groups", "tm"), None, None),
            P(None, None, ("groups", "tm")),
        ),
        out_specs=(P(None, ("groups", "tm")), P(("groups", "tm"), None)),
        check_vma=False,
    )
```

```python
import functools

import jax
import jax.numpy as jnp
import numpy as np
from jax import lax
from jax.experimental import pallas as pl
from jax.experimental.pallas import tpu as pltpu
from jax.sharding import PartitionSpec as P

BLK = 128
ROW = 4
MIB = 2**20
F32 = jnp.float32
BF16 = jnp.bfloat16
VMEM = pl.BlockSpec(memory_space=pltpu.VMEM)
HBM = pl.BlockSpec(memory_space=pltpu.HBM)


def split_const(a):
    high = a.astype(jnp.bfloat16)
    low = (a - high.astype(np.float64)).astype(jnp.bfloat16)
    return high, low


@functools.lru_cache(maxsize=None)
def dft_tables(size):
    t = np.arange(size)[:, None]
    g = np.arange(size)[None, :]
    half = size // 2
    angle = 2 * np.pi * ((t * g[:, :half]) % size) / size
    cos, sin = np.cos(angle), np.sin(angle)
    sin[:, 0] = 1 - 2 * (np.arange(size) % 2)
    real = np.concatenate([cos, sin], axis=1)
    angle = 2 * np.pi * ((t * (3 * g + 1)) % (3 * size)) / (3 * size)
    cos, sin = np.cos(angle), np.sin(angle)
    weight = np.full((size,), 2.0)
    weight[0] = weight[half] = 1.0
    scale = 1.0 / (3 * size)
    tables = [real, cos, sin, (real * weight).T * scale, cos.T * 2 * scale, sin.T * 2 * scale]
    return np.concatenate([part for table in tables for part in split_const(table)])


def parts(a):
    high = a.astype(BF16)
    return high, (a - high.astype(F32)).astype(BF16)


def times(a, tables, index):
    rows, size = a.shape
    high, low = parts(a)
    first = 2 * index * size
    t_high, t_low = tables[first : first + size], tables[first + size : first + 2 * size]
    out = jnp.dot(jnp.concatenate([high, low]), t_high, preferred_element_type=F32)
    return out[:rows] + out[rows:] + jnp.dot(high, t_low, preferred_element_type=F32)


ROOT = 0.75**0.5


def spectrum_of(thirds, tables):
    first, second, third = thirds
    rows = first.shape[0]
    base = times(first + second + third, tables, 0)
    y = jnp.concatenate([first - 0.5 * (second + third), ROOT * (third - second)])
    cos, sin = times(y, tables, 1), times(y, tables, 2)
    return base, cos[:rows] + sin[rows:], cos[rows:] - sin[:rows]


def filtered(signal, taps, sign, tables, wanted):
    (xb, xr, xi), (kb, kr, ki) = signal, taps
    rows, size = xb.shape
    half = size // 2
    first = lax.broadcasted_iota(jnp.int32, (rows, half), 1) == 0
    kc, ks = kb[:, :half], kb[:, half:]
    kc_s = jnp.where(first, ks, kc)
    ks_x = jnp.where(first, 0.0, ks) * sign
    xc, xs = xb[:, :half], xb[:, half:]
    base = times(jnp.concatenate([xc * kc + xs * ks_x, xs * kc_s - xc * ks_x], axis=1), tables, 3)
    ki = ki * sign
    z = jnp.concatenate([xr * kr + xi * ki, xi * kr - xr * ki])
    cos, sin = times(z, tables, 4), times(z, tables, 5)
    vr, vi = cos[:rows] - sin[rows:], sin[:rows] + cos[rows:]
    each = (base + vr, base - 0.5 * vr - ROOT * vi, base - 0.5 * vr + ROOT * vi)
    return jnp.concatenate([each[m] for m in wanted], axis=1)


def thirds_of(mid, core_side, far_side):
    width = core_side.shape[1]
    size = 2 * width
    even = lax.rem(lax.axis_index("tm"), 2) == 0
    low, high = jnp.where(even, far_side, core_side), jnp.where(even, core_side, far_side)
    last = mid.shape[1] - width
    return (
        jnp.concatenate([low, mid[:, :width]], axis=1),
        mid[:, width : width + size],
        jnp.concatenate([mid[:, last:], high], axis=1),
    )


def prepare_kernel(table, taps, mid, tables, bins, base, kr, ki, held, sem):
    rows = table.shape[0] // 6
    cuts = [pl.ds(i * rows, rows) for i in range(6)]
    copies = [pltpu.make_async_copy(taps, held, sem.at[0])]
    copies += [
        pltpu.make_async_copy(table.at[cut], tables.at[cut], sem.at[1 + i])
        for i, cut in enumerate(cuts)
    ]
    copies += [pltpu.make_async_copy(mid, bins, sem.at[7])]
    for copy in copies:
        copy.start()
    copies[0].wait()
    for i, (ref, sign) in enumerate(((base, 1.0), (kr, 1.0), (ki, -1.0))):
        copies[1 + i].wait()
        ref[...] = times(held[...], tables, i) * sign
    for copy in copies[4:]:
        copy.wait()


def smooth_kernel(mid, core_side, far_side, tables, base, kr, ki, out):
    thirds = thirds_of(mid[...], core_side[...], far_side[...])
    signal = spectrum_of(thirds, tables)
    taps = (base[...], kr[...], ki[...])
    out[...] = filtered(signal, taps, 1.0, tables, (0, 1)).astype(out.dtype)


def unsmooth_kernel(mid, got, far_side, tables, base, kr, ki, out):
    width = far_side.shape[1] // 2
    core = got[got.shape[0] - far_side.shape[0] :].astype(F32)
    far = far_side[...].astype(F32)
    thirds = thirds_of(
        mid[...], core[:, :width] + core[:, width:], far[:, :width] + far[:, width:]
    )
    signal = spectrum_of(thirds, tables)
    taps = (base[...], kr[...], ki[...])
    out[...] = filtered(signal, taps, -1.0, tables, (1, 2))


def divide(a, n):
    return a >> (n.bit_length() - 1) if n & (n - 1) == 0 else a // n


def remainder(a, n):
    return a & (n - 1) if n & (n - 1) == 0 else a % n


def place_of(ids, e, me, blocks, forward):
    chain = lax.axis_size("tm") // ROW
    top = ids.shape[1]
    code = ids[divide(e, top), remainder(e, top)]
    owner, slot = divide(code, blocks), remainder(code, blocks)
    step = divide(owner, ROW) - divide(me, ROW)
    step = step if forward else -step
    turn = jnp.where(step < 0, step + chain, step)
    differ = owner ^ me
    piece = jnp.where(differ & 2 == 0, 0, chain) + turn
    return differ & 1 == 0, piece, pl.multiple_of(slot * BLK, BLK)


def pick(refs, index, act):
    if len(refs) == 1:
        act(refs[0])
        return
    half = len(refs) // 2
    lax.cond(
        index < half,
        lambda: pick(refs[:half], index, act),
        lambda: pick(refs[half:], index - half, act),
    )


def pack_kernel(first, entries, late, asked, *refs):
    pieces, out = refs[:-1], refs[-1]
    blocks = pieces[0].shape[0] // BLK
    me = lax.axis_index("tm")

    def body(e, _):
        core, piece, row = place_of(asked, first + e, me, blocks, False)
        target = pl.ds(pl.multiple_of(e * BLK, BLK), BLK)

        @pl.when(jnp.logical_and(core, piece != late))
        def _():
            def act(ref):
                out[target] = ref[pl.ds(row, BLK)]

            pick(pieces, jnp.where(piece < late, piece, piece - 1), act)

        return 0

    lax.fori_loop(0, entries, body, 0)


def session_kernel(
    entries, group, late, ids, mask, smoothed, recorded, packed, packed_rest, late_theirs, *refs
):
    pieces = refs[:-5]
    grad, far_side, terms, rows, resid = refs[-5:]
    blocks = pieces[0].shape[0] // BLK
    bins = smoothed.shape[1]
    top = ids.shape[1]
    me = lax.axis_index("tm")
    grad[...] = jnp.zeros_like(grad)
    depth = group * BLK

    def step(g, _):
        for i in range(group):
            e = g * group + i
            core, piece, row = place_of(ids, e, me, blocks, False)

            def own():
                def act(ref):
                    rows[i * BLK : (i + 1) * BLK] = ref[pl.ds(row, BLK)]

                pick(pieces, piece, act)

            def other():
                @pl.when(piece == late)
                def _():
                    rows[i * BLK : (i + 1) * BLK] = late_theirs[pl.ds(row, BLK)]

                @pl.when(piece != late)
                def _():
                    def act(ref):
                        source = pl.ds(pl.multiple_of(remainder(e, entries // 2) * BLK, BLK), BLK)
                        rows[i * BLK : (i + 1) * BLK] = ref[source]

                    pick((packed, packed_rest), divide(e, entries // 2), act)

            lax.cond(core, own, other)
        block = rows[...]
        predicted = jnp.dot(block, smoothed[...], preferred_element_type=F32)
        for i in range(group):
            e = g * group + i
            for t in range(bins // BLK):
                cut = slice(t * BLK, (t + 1) * BLK)
                weight = mask[divide(e, top), t, remainder(e, top)].astype(F32)
                part = predicted[i * BLK : (i + 1) * BLK, cut]
                seen = recorded[e, :, cut].astype(F32)
                resid[i * BLK : (i + 1) * BLK, cut] = (weight * (part - seen)).astype(BF16)
        term = lax.dot_general(
            resid[...], smoothed[...], (((1,), (1,)), ((), ())), preferred_element_type=F32
        )
        target = pl.ds(pl.multiple_of(g * depth, depth), depth)
        terms[target] = (term * (1.0 / BLK)).astype(BF16)
        grad[...] += lax.dot_general(
            block, resid[...], (((0,), (0,)), ((), ())), preferred_element_type=F32
        ) * (1.0 / BLK)
        return 0

    lax.fori_loop(0, entries // group, step, 0)
    latent_dim, width = grad.shape[0], rows.shape[1] // 2
    even = me & 1 == 0
    later, earlier = grad[:, bins - width :], grad[:, :width]
    core_edge, far_edge = jnp.where(even, later, earlier), jnp.where(even, earlier, later)
    terms[pl.ds(entries * BLK, latent_dim)] = jnp.concatenate(parts(core_edge), axis=1)
    far_side[...] = jnp.concatenate(parts(far_edge), axis=1)


def merge_late_kernel(entries, late, ids, asked, own, got, out, sums):
    blocks = out.shape[0] // BLK
    me = lax.axis_index("tm")
    sums[...] = jnp.zeros_like(sums)

    def add(e, _):
        source = pl.ds(pl.multiple_of(e * BLK, BLK), BLK)
        for names, terms in ((ids, own), (asked, got)):
            core, piece, row = place_of(names, e, me, blocks, True)

            @pl.when(jnp.logical_and(core, piece == late))
            def _():
                sums[pl.ds(row, BLK)] += terms[source].astype(F32)

        return 0

    lax.fori_loop(0, entries, add, 0)
    out[...] = sums[...].astype(out.dtype)


def merge_kernel(entries, late, ids, asked, own, got, *refs):
    chain = len(refs) // 2
    kept, outs, sums = refs[:chain], refs[chain:-1], refs[-1]
    chunk = kept[0].shape[0]
    me = lax.axis_index("tm")
    for ref in kept:
        ref[...] = jnp.zeros_like(ref)
    sums[...] = jnp.zeros_like(sums)

    def add(e, _):
        source = pl.ds(pl.multiple_of(e * BLK, BLK), BLK)
        for names, terms in ((ids, own), (asked, got)):
            core, piece, row = place_of(names, e, me, chunk // BLK, True)
            index = jnp.where(piece < late, piece - chain, piece - 1 - chain)

            @pl.when(jnp.logical_and(core, piece < chain))
            def _():
                def act(ref):
                    ref[pl.ds(row, BLK)] += terms[source].astype(F32)

                pick(kept, piece, act)

            @pl.when(jnp.logical_and(core, jnp.logical_and(piece >= chain, piece != late)))
            def _():
                sums[pl.ds(pl.multiple_of(index * chunk + row, BLK), BLK)] += terms[source].astype(F32)

        return 0

    lax.fori_loop(0, entries, add, 0)
    for q, out in enumerate(outs):
        out[...] = sums[q * chunk : (q + 1) * chunk].astype(out.dtype)


def hop_kernel(total, *refs):
    out = refs[-1]
    value = total[...]
    for came in refs[:-1]:
        value += came[...].astype(F32)
    out[...] = value.astype(out.dtype)


def local(latents, kernel, loadings, recorded, owner_ids, local_ids, recorded_mask):
    latent_dim, bins = latents.shape
    halfwidth = kernel.shape[1] // 2
    count = lax.axis_size("tm")
    chain = count // ROW
    chunk = loadings.shape[0]
    entries = owner_ids.size
    piece_bytes = count * chunk * latent_dim
    smem = pl.BlockSpec(memory_space=pltpu.SMEM)

    def permute(x, pairs):
        return lax.ppermute(x, "tm", pairs)

    def rotate(x, r):
        return permute(x, [(i, (i + r * ROW) % count) for i in range(count)])

    def flip(x, bit):
        return permute(x, [(i, i ^ bit) for i in range(count)])

    odd_even = [(i, i + 1) for i in range(1, count - 1, 2)]
    odd_even += [(target, source) for source, target in odd_even]

    ids = owner_ids[0] * (chunk // BLK) + local_ids[0]
    asked = flip(ids, 1)
    mask = jnp.transpose(recorded_mask, (0, 2, 1))

    even = lax.axis_index("tm") % 2 == 0
    later, earlier = latents[:, bins - halfwidth :], latents[:, :halfwidth]
    core_side = flip(jnp.where(even, later, earlier), 1)
    far_side = permute(jnp.where(even, earlier, later), odd_even)

    half = chain // 2
    late = chain + half
    straight = [loadings] * chain
    for r in range(1, half):
        straight[r] = rotate(straight[r - 1], 1)
        straight[-r] = rotate(straight[1 - r], -1)
    across = [flip(loadings, 2)] + [None] * (chain - 1)
    if half > 1:
        straight[1], across[0] = lax.optimization_barrier((straight[1], across[0]))
    straight[half] = rotate(straight[half - 1], 1)
    straight[1], kernel = lax.optimization_barrier((straight[1], kernel))
    table = dft_tables(2 * halfwidth)
    mxu = 30 * 2 * latent_dim * (2 * halfwidth) ** 2
    square = jax.ShapeDtypeStruct((latent_dim, 2 * halfwidth), F32)
    prepared = pl.pallas_call(
        prepare_kernel,
        out_shape=(
            jax.ShapeDtypeStruct(table.shape, BF16),
            jax.ShapeDtypeStruct(latents.shape, F32),
        )
        + (square,) * 3,
        in_specs=[HBM] * 3,
        out_specs=(VMEM,) * 5,
        scratch_shapes=[pltpu.VMEM(kernel.shape, F32), pltpu.SemaphoreType.DMA((8,))],
        compiler_params=pltpu.CompilerParams(vmem_limit_bytes=50 * MIB),
        cost_estimate=pl.CostEstimate(flops=mxu // 3, bytes_accessed=4 * MIB, transcendentals=0),
        name="prepare",
    )(table, kernel, latents)
    straight[-1], *prepared = lax.optimization_barrier((straight[-1], *prepared))
    spectrum, held_bins = [prepared[0], *prepared[2:]], prepared[1]
    for r in range(1, chain):
        if r != half:
            across[r] = flip(straight[r], 2)

    smoothed = pl.pallas_call(
        smooth_kernel,
        out_shape=jax.ShapeDtypeStruct((latent_dim, bins), BF16),
        in_specs=[VMEM] * 7,
        out_specs=VMEM,
        compiler_params=pltpu.CompilerParams(vmem_limit_bytes=16 * MIB),
        cost_estimate=pl.CostEstimate(flops=mxu, bytes_accessed=4 * MIB, transcendentals=0),
        name="smooth",
    )(held_bins, core_side, far_side, *spectrum)

    slots = jax.ShapeDtypeStruct((entries * BLK, latent_dim), BF16)
    across[half] = flip(straight[half], 2)
    early = straight + across[:half] + across[half + 1 :]

    def pack(first, total):
        return pl.pallas_call(
            functools.partial(pack_kernel, first, total, late),
            out_shape=jax.ShapeDtypeStruct((total * BLK, latent_dim), BF16),
            in_specs=[smem] + [VMEM] * len(early),
            out_specs=VMEM,
            compiler_params=pltpu.CompilerParams(vmem_limit_bytes=4 * MIB + 3 * piece_bytes),
            cost_estimate=pl.CostEstimate(flops=0, bytes_accessed=2**20, transcendentals=0),
            name="pack",
        )(asked, *early)

    asked, smoothed, mask = lax.optimization_barrier((asked, smoothed, mask))
    packed = [flip(pack(first, entries // 2), 1) for first in (0, entries // 2)]
    last, smoothed = lax.optimization_barrier((across[half], smoothed))
    late_theirs = flip(last, 1)
    pieces = straight + across

    group = 4
    extended = jax.ShapeDtypeStruct((entries * BLK + latent_dim, latent_dim), BF16)
    grad, far_side, terms = pl.pallas_call(
        functools.partial(session_kernel, entries, group, late),
        out_shape=(
            jax.ShapeDtypeStruct((latent_dim, bins), F32),
            jax.ShapeDtypeStruct((latent_dim, 2 * halfwidth), BF16),
            extended,
        ),
        in_specs=[smem] * 2 + [VMEM] * (5 + len(pieces)),
        out_specs=(VMEM,) * 3,
        scratch_shapes=[
            pltpu.VMEM((group * BLK, latent_dim), BF16),
            pltpu.VMEM((group * BLK, bins), BF16),
        ],
        compiler_params=pltpu.CompilerParams(vmem_limit_bytes=12 * MIB + 6 * piece_bytes),
        cost_estimate=pl.CostEstimate(
            flops=6 * entries * BLK * latent_dim * bins, bytes_accessed=8 * 2**20, transcendentals=0
        ),
        name="session",
    )(
        ids,
        mask,
        smoothed,
        recorded.reshape(entries, BLK, bins),
        *packed,
        late_theirs,
        *pieces,
    )

    got = flip(terms, 1)
    narrow = jax.ShapeDtypeStruct((chunk, latent_dim), BF16)
    sent = pl.pallas_call(
        functools.partial(merge_late_kernel, entries, late),
        out_shape=narrow,
        in_specs=[smem] * 2 + [VMEM] * 2,
        out_specs=VMEM,
        scratch_shapes=[pltpu.VMEM((chunk, latent_dim), F32)],
        compiler_params=pltpu.CompilerParams(vmem_limit_bytes=4 * MIB + 3 * piece_bytes),
        cost_estimate=pl.CostEstimate(flops=0, bytes_accessed=2**20, transcendentals=0),
        name="merge_late",
    )(ids, asked, terms, got)
    wide = jax.ShapeDtypeStruct((chunk, latent_dim), F32)
    sent, ids = lax.optimization_barrier((sent, ids))
    back = flip(sent, 2)
    merged = pl.pallas_call(
        functools.partial(merge_kernel, entries, late),
        out_shape=(wide,) * chain + (narrow,) * (chain - 1),
        in_specs=[smem] * 2 + [VMEM] * 2,
        out_specs=(VMEM,) * (2 * chain - 1),
        scratch_shapes=[pltpu.VMEM(((chain - 1) * chunk, latent_dim), F32)],
        compiler_params=pltpu.CompilerParams(vmem_limit_bytes=4 * MIB + 6 * piece_bytes),
        cost_estimate=pl.CostEstimate(flops=0, bytes_accessed=5 * 2**20, transcendentals=0),
        name="merge",
    )(ids, asked, terms, got)
    crossed = {r: merged[chain + r - (r > half)] for r in range(chain) if r != half}
    back, *held = lax.optimization_barrier((back, *(crossed[r] for r in range(1, half))))
    other = {r: flip(part, 2) for r, part in enumerate(held, 1)}
    for r in range(half + 1, chain):
        other[r] = flip(crossed[r], 2)

    def hop(total, *came):
        return pl.pallas_call(
            hop_kernel,
            out_shape=narrow,
            in_specs=[VMEM] * (1 + len(came)),
            out_specs=VMEM,
            compiler_params=pltpu.CompilerParams(vmem_limit_bytes=8 * MIB),
            cost_estimate=pl.CostEstimate(flops=0, bytes_accessed=MIB, transcendentals=0),
            name="hop",
        )(total, *came)

    rise = hop(merged[half], back)
    rise, far_side = lax.optimization_barrier((rise, far_side))
    far_side = permute(far_side, odd_even)
    other[1], far_side = lax.optimization_barrier((other[1], far_side))
    _, own = lax.optimization_barrier((other[half + 1], crossed[0]))
    other[0] = flip(own, 2)
    rise = rotate(rise, 1)
    for r in range(half - 1, 0, -1):
        rise = rotate(hop(merged[r], other[r], rise), 1)
    fall = rotate(hop(merged[half + 1], other[half + 1]), -1)
    for r in range(half + 2, chain):
        fall = rotate(hop(merged[r], other[r], fall), -1)
    loading_grad = merged[0] + other[0].astype(F32) + rise.astype(F32) + fall.astype(F32)

    latent_grad = pl.pallas_call(
        unsmooth_kernel,
        out_shape=jax.ShapeDtypeStruct((latent_dim, bins), F32),
        in_specs=[VMEM] * 7,
        out_specs=VMEM,
        compiler_params=pltpu.CompilerParams(vmem_limit_bytes=16 * MIB),
        cost_estimate=pl.CostEstimate(flops=mxu, bytes_accessed=4 * MIB, transcendentals=0),
        name="unsmooth",
    )(grad, got, far_side, *spectrum)
    return latent_grad, loading_grad


def solution(mesh):
    return jax.shard_map(
        local,
        mesh=mesh,
        in_specs=(
            P(None, ("groups", "tm")),
            P(),
            P(("groups", "tm"), None),
            P(None, None, None, ("groups", "tm")),
            P(("groups", "tm"), None, None),
            P(("groups", "tm"), None, None),
            P(None, None, ("groups", "tm")),
        ),
        out_specs=(P(None, ("groups", "tm")), P(("groups", "tm"), None)),
        check_vma=False,
    )
```
